32 devices in a mesh: band: 8 (over y, x, core), batch: 4 (over z).
Axes of the slice: x: 2, y: 2, z: 4, core: 2. Of those that a mesh axis runs over, the one named last changes fastest.
Arguments:
- residual_in: bfloat16 [4, 4096, 768], P('batch', 'band'), may hold values from -6 to 6
- exit_layer: int32 [4, 4096], P('batch', 'band'), may hold values from 0 to 11, as said below
- band_edges: int32 [4, 2, 8], P('batch'), may hold values from 0 to 1792, as said below
- norm1_gain: bfloat16 [768], replicated, may hold values from 0.5 to 1.5
- norm1_bias: bfloat16 [768], replicated, may hold values from -1.25 to 1.25
- query_weight: bfloat16 [768, 768], replicated, may hold values from -0.21875 to 0.21875
- query_bias: bfloat16 [768], replicated, may hold values from -1.75 to 1.75
- key_weight: bfloat16 [768, 768], replicated, may hold values from -0.21875 to 0.21875
- value_weight: bfloat16 [768, 768], replicated, may hold values from -0.21875 to 0.21875
- value_bias: bfloat16 [768], replicated, may hold values from -0.3125 to 0.3125
- out_weight: bfloat16 [768, 768], replicated, may hold values from -1.75 to 1.75
- out_bias: bfloat16 [768], replicated, may hold values from -1.25 to 1.25
- norm2_gain: bfloat16 [768], replicated, may hold values from 0.5 to 1.5
- norm2_bias: bfloat16 [768], replicated, may hold values from -1.25 to 1.25
- up_weight: bfloat16 [768, 3072], replicated, may hold values from -0.21875 to 0.21875
- up_bias: bfloat16 [3072], replicated, may hold values from -1.75 to 1.75
- down_weight: bfloat16 [3072, 768], replicated, may hold values from -0.109375 to 0.109375
- down_bias: bfloat16 [768], replicated, may hold values from -1.25 to 1.25
- cotangent: bfloat16 [4, 4096, 768], P('batch', 'band'), may hold values from -6 to 6
Outputs:
- layer_out: bfloat16 [4, 4096, 768], P('batch', 'band')
- input_grad: float32 [4, 4096, 768], P('batch', 'band')
- norm1_gain_grad: float32 [768], replicated
- norm1_bias_grad: float32 [768], replicated
- query_weight_grad: float32 [768, 768], replicated
- query_bias_grad: float32 [768], replicated
- key_weight_grad: float32 [768, 768], replicated
- value_weight_grad: float32 [768, 768], replicated
- value_bias_grad: float32 [768], replicated
- out_weight_grad: float32 [768, 768], replicated
- out_bias_grad: float32 [768], replicated
- norm2_gain_grad: float32 [768], replicated
- norm2_bias_grad: float32 [768], replicated
- up_weight_grad: float32 [768, 3072], replicated
- up_bias_grad: float32 [3072], replicated
- down_weight_grad: float32 [3072, 768], replicated
- down_bias_grad: float32 [768], replicated
The draws below stay inside these ranges and needn't reach their ends.
Inputs may be any that keep to these rules, and one draw needn't show every extreme that they name: `exit_layer`: within a sequence the values never rise with position; in each group one sequence keeps 6 or more at every position. Values of slots that are not valid are arbitrary. band_edges[g, s, 0] is 0; each band holds 128 to 256 positions of each sequence, counts never falling from band to band, so that the last band holds 256; in each group one sequence holds 256 in every band.
All inputs are finite; a program needn't handle non-finite values.
Results may differ from the reference program's by a relative error of at most 0.015.
Values may be sent and summed in bfloat16 or wider, within the bound.
A program may use at most 384 MiB of HBM per device.

```python
import math
import jax
import jax.numpy as jnp
from jax import lax

D = 768
HEADS = 12
HEAD = 64
FF = 3072
LAYERS = 12
LAYER = 6
BAND_CAP = 256
SEQS = 2
SLOT_DEV = 512
SLOTS = 4096
MAXLEN = 2048
GROUPS = 4
N_BAND = 8
N_BATCH = 4


def band_counts(key):
    count_key, full_key, whole_key = jax.random.split(key, 3)
    half_cap = BAND_CAP // 2
    counts = jax.random.randint(count_key, (N_BATCH, SEQS, N_BAND), half_cap, BAND_CAP + 1, dtype=jnp.int32)
    full_band = jax.random.randint(full_key, (N_BATCH, SEQS, 1), 0, N_BAND, dtype=jnp.int32)
    counts = jnp.where(jnp.arange(N_BAND, dtype=jnp.int32)[None, None, :] == full_band, BAND_CAP, counts)
    whole_seq = jax.random.randint(whole_key, (N_BATCH, 1, 1), 0, SEQS, dtype=jnp.int32)
    counts = jnp.where(jnp.arange(SEQS, dtype=jnp.int32)[None, :, None] == whole_seq, BAND_CAP, counts)
    return jnp.sort(counts, axis=-1).astype(jnp.int32)


def draw_band_edges(key, part):
    band_sizes = band_counts(key)
    return (jnp.cumsum(band_sizes, axis=-1) - band_sizes).astype(jnp.int32)


def draw_exit_layer(key, part):
    band_sizes = band_counts(key)
    key = jax.random.fold_in(key, 3)
    edges_all = (jnp.cumsum(band_sizes, axis=-1) - band_sizes).astype(jnp.int32)
    totals = jnp.sum(band_sizes, axis=-1).astype(jnp.int32)
    top_key, drop_key, pick_key = jax.random.split(key, 3)
    highest = jax.random.randint(top_key, (N_BATCH, SEQS), LAYER, LAYERS, dtype=jnp.int32)
    falloff = jax.random.randint(drop_key, (N_BATCH, SEQS), 2, 2 * LAYERS, dtype=jnp.int32)
    chosen = jax.random.randint(pick_key, (N_BATCH, 1), 0, SEQS, dtype=jnp.int32)
    is_chosen = jnp.arange(SEQS, dtype=jnp.int32)[None, :] == chosen
    highest = jnp.where(is_chosen, LAYERS - 1, highest)
    falloff = jnp.where(is_chosen, LAYERS - 1 - LAYER, falloff)
    position = jnp.transpose(edges_all, (0, 2, 1))[..., None] + jnp.arange(BAND_CAP, dtype=jnp.int32)[None, None, None, :]
    depth = highest[:, None, :, None] - position * falloff[:, None, :, None] // totals[:, None, :, None]
    return jnp.clip(depth, 0, LAYERS - 1).reshape(N_BATCH, N_BAND * SEQS * BAND_CAP).astype(jnp.int32)


def block_levels(rng, extent, cuts, low, largest):
    def one(dim, shards_of):
        heights = jax.random.uniform(jax.random.fold_in(jax.random.fold_in(rng, 6), dim), (shards_of,), jnp.float32, low / len(cuts), largest / len(cuts))
        return jnp.repeat(jnp.exp(heights), extent[dim] // shards_of).reshape((-1,) + (1,) * (len(extent) - dim - 1))

    gain = one(*cuts[0])
    for cut in cuts[1:]:
        gain = gain * one(*cut)
    return gain


def noise(own_key, shape, scale, most, cuts=(), kind=jnp.bfloat16):
    drawn = scale * jax.random.normal(own_key, shape, jnp.float32)
    if cuts:
        drawn = drawn * block_levels(own_key, shape, cuts, -0.22, 0.18)
    return jnp.clip(drawn, -most, most).astype(kind)


def setup_inputs(seed: int = 0) -> dict:
    seeds = jax.random.split(jax.random.key(seed), 20)
    residual_in = noise(seeds[0], (GROUPS, SLOTS, D), 1.0, 6.0, ((0, 4), (1, 8)))
    exit_layer = draw_exit_layer(jax.random.fold_in(seeds[19], 71), 0)
    band_edges = draw_band_edges(jax.random.fold_in(seeds[19], 71), 0)
    norm1_gain = jnp.clip(1.0 + 0.1 * jax.random.normal(seeds[3], (D,), jnp.float32), 0.5, 1.5).astype(jnp.bfloat16)
    norm1_bias = noise(seeds[4], (D,), 0.2, 1.25)
    query_weight = noise(seeds[5], (D, D), D ** -0.5, 0.21875)
    query_bias = noise(seeds[6], (D,), 0.3, 1.75)
    key_weight = noise(seeds[7], (D, D), D ** -0.5, 0.21875)
    value_weight = noise(seeds[8], (D, D), D ** -0.5, 0.21875)
    value_bias = noise(seeds[9], (D,), 0.05, 0.3125)
    out_weight = noise(seeds[10], (D, D), (max(D // 64, 1)) ** -0.5, 1.75)
    out_bias = noise(seeds[11], (D,), 0.2, 1.25)
    norm2_gain = jnp.clip(1.0 + 0.1 * jax.random.normal(seeds[12], (D,), jnp.float32), 0.5, 1.5).astype(jnp.bfloat16)
    norm2_bias = noise(seeds[13], (D,), 0.2, 1.25)
    up_weight = noise(seeds[14], (D, FF), D ** -0.5, 0.21875)
    up_bias = noise(seeds[15], (FF,), 0.3, 1.75)
    down_weight = noise(seeds[16], (FF, D), FF ** -0.5, 0.109375)
    down_bias = noise(seeds[17], (D,), 0.2, 1.25)
    cotangent = noise(seeds[18], (GROUPS, SLOTS, D), 1.0, 6.0, ((0, 4), (1, 8)))
    return {"residual_in": residual_in, "exit_layer": exit_layer, "band_edges": band_edges, "norm1_gain": norm1_gain, "norm1_bias": norm1_bias, "query_weight": query_weight, "query_bias": query_bias, "key_weight": key_weight, "value_weight": value_weight, "value_bias": value_bias, "out_weight": out_weight, "out_bias": out_bias, "norm2_gain": norm2_gain, "norm2_bias": norm2_bias, "up_weight": up_weight, "up_bias": up_bias, "down_weight": down_weight, "down_bias": down_bias, "cotangent": cotangent}


@jax.custom_vjp
def low(v):
    return lax.optimization_barrier(v.astype(jnp.bfloat16)).astype(jnp.float32)

@jax.custom_vjp
def low_back(v):
    return v

def low_keep(v):
    return (low(v), None)

def low_pass(kept, grad):
    return (grad,)

def back_keep(v):
    return (v, None)

def back_low(kept, grad):
    return (low(grad),)
low.defvjp(low_keep, low_pass)
low_back.defvjp(back_keep, back_low)

def norm_rows(values):
    center = values - lax.optimization_barrier(jnp.mean(values, axis=-1, keepdims=True))
    spread = lax.optimization_barrier(jnp.mean(center * center, axis=-1, keepdims=True))
    return center * lax.rsqrt(spread + 1e-05)

def project(inputs, weight):
    return jnp.dot(inputs, weight, precision=lax.Precision.HIGHEST)

def pick_rows(source, index):
    return jnp.take_along_axis(source, index[..., None], axis=1)

def attend_sequence(packed):
    queries, keys_seq, values_seq, length = packed
    total_len = queries.shape[0]
    block_rows = math.gcd(512, total_len)
    score_scale = queries.shape[-1] ** (-0.5)
    key_pos = jnp.arange(total_len, dtype=jnp.int32)

    @jax.checkpoint
    def one_block(first_row):
        query_blk = lax.dynamic_slice_in_dim(queries, first_row, block_rows, 0)
        scores = jnp.einsum('qhd,khd->hqk', query_blk, keys_seq, precision=lax.Precision.HIGHEST) * score_scale
        scores = low_back(scores)
        query_pos = first_row + jnp.arange(block_rows, dtype=jnp.int32)
        causal = (key_pos[None, :] <= query_pos[:, None]) & (key_pos[None, :] < length)
        allowed = causal | (key_pos[None, :] == query_pos[:, None])
        scores = jnp.where(allowed[None], scores, -1e+30)
        probability = low(jax.nn.softmax(scores, axis=-1))
        return jnp.einsum('hqk,khd->qhd', probability, values_seq, precision=lax.Precision.HIGHEST)
    first_rows = jnp.arange(0, total_len, block_rows, dtype=jnp.int32)
    outputs = lax.map(one_block, first_rows)
    return outputs.reshape(queries.shape)

def reference(residual_in, exit_layer, band_edges, norm1_gain, norm1_bias, query_weight, query_bias, key_weight, value_weight, value_bias, out_weight, out_bias, norm2_gain, norm2_bias, up_weight, up_bias, down_weight, down_bias, cotangent):
    slot_index = jnp.arange(SLOTS, dtype=jnp.int32)
    owner = slot_index // SLOT_DEV
    within = slot_index - owner * SLOT_DEV
    member = within // BAND_CAP
    offset = within - member * BAND_CAP
    seq_lengths = (band_edges[:, :, -1] + BAND_CAP).astype(jnp.int32)
    finishes = jnp.concatenate([band_edges[:, :, 1:], seq_lengths[:, :, None]], axis=2)
    position = band_edges[:, member, owner] + offset[None, :]
    valid = position < finishes[:, member, owner]
    active = (valid & (exit_layer >= LAYER)).astype(jnp.float32)
    back_index = (member[None, :] * MAXLEN + jnp.minimum(position, MAXLEN - 1)).astype(jnp.int32)
    seq_pos = jnp.arange(MAXLEN, dtype=jnp.int32)
    band_of = (lax.optimization_barrier(jnp.sum((band_edges[:, :, None, :] <= seq_pos[None, None, :, None]).astype(jnp.int32), axis=-1)) - 1).astype(jnp.int32)
    edge_at = jnp.take_along_axis(band_edges, band_of, axis=2)
    inner = jnp.minimum(seq_pos[None, None, :] - edge_at, BAND_CAP - 1)
    seq_slot = band_of * SLOT_DEV + jnp.arange(SEQS, dtype=jnp.int32)[None, :, None] * BAND_CAP + inner
    seq_index = seq_slot.reshape(GROUPS, SEQS * MAXLEN).astype(jnp.int32)
    flat_lengths = seq_lengths.reshape(-1)

    def to_sequences(array):
        return pick_rows(array, seq_index).reshape(GROUPS * SEQS, MAXLEN, HEADS, HEAD)

    def forward(hidden_in, gain_one, shift_one, w_query, b_query, w_key, w_value, b_value, w_out, b_out, gain_two, shift_two, w_up, b_up, w_down, b_down):
        normed_one = low(norm_rows(hidden_in) * gain_one + shift_one)
        queries = low(low_back(project(normed_one, w_query) + b_query))
        keys_all = low(low_back(project(normed_one, w_key)))
        values_all = low(low_back(project(normed_one, w_value) + b_value))
        attended = lax.map(attend_sequence, (to_sequences(queries), to_sequences(keys_all), to_sequences(values_all), flat_lengths))
        attended = attended.reshape(GROUPS, SEQS * MAXLEN, D)
        mixed = low(low_back(pick_rows(attended, back_index)))
        branch = low_back(project(mixed, w_out) + b_out)
        middle = hidden_in + active[..., None] * branch
        normed_two = low(norm_rows(middle) * gain_two + shift_two)
        pre_act = low_back(project(normed_two, w_up) + b_up)
        activated = low(jax.nn.gelu(pre_act))
        down_out = low_back(project(activated, w_down) + b_down)
        return middle + active[..., None] * down_out
    layer_out, pullback = jax.vjp(forward, residual_in.astype(jnp.float32), norm1_gain.astype(jnp.float32), norm1_bias.astype(jnp.float32), query_weight.astype(jnp.float32), query_bias.astype(jnp.float32), key_weight.astype(jnp.float32), value_weight.astype(jnp.float32), value_bias.astype(jnp.float32), out_weight.astype(jnp.float32), out_bias.astype(jnp.float32), norm2_gain.astype(jnp.float32), norm2_bias.astype(jnp.float32), up_weight.astype(jnp.float32), up_bias.astype(jnp.float32), down_weight.astype(jnp.float32), down_bias.astype(jnp.float32))
    grads = pullback(cotangent.astype(jnp.float32))
    total = jnp.sum(active)
    return (layer_out.astype(jnp.bfloat16), grads[0], grads[1] / total, grads[2] / total, grads[3] / total, grads[4] / total, grads[5] / total, grads[6] / total, grads[7] / total, grads[8] / total, grads[9] / total, grads[10] / total, grads[11] / total, grads[12] / total, grads[13] / total, grads[14] / total, grads[15] / total)
```

```python
import functools

import jax
import jax.numpy as jnp
from jax import lax
from jax.experimental import pallas as pl
from jax.experimental.pallas import tpu as pltpu
from jax.sharding import PartitionSpec as P

MESH = pl.DeviceIdType.MESH
VM = pltpu.VMEM
BF = jnp.bfloat16
F32 = jnp.float32
HEADS = 12
LAYER = 6
HEAD = 64
BANDS = 8
CAP = 256
HALF = 128
MINE = 3
SHARE = MINE * HEAD
NEG = -1e30


def place():
    band = lax.axis_index("band")
    return band, band // 4, (band // 2) % 2, band % 2


def device(y, x, core):
    return (y * 4 + x * 2 + core, lax.axis_index("batch"))


def push(src, dst, send, recv, target):
    return pltpu.make_async_remote_copy(
        src_ref=src, dst_ref=dst, send_sem=send, recv_sem=recv, device_id=target, device_id_type=MESH
    )


def greet_band():
    band, _, _, _ = place()
    barrier = pltpu.get_barrier_semaphore()
    for step in range(1, BANDS):
        other = (band + step) % BANDS
        pl.semaphore_signal(
            barrier, inc=1, device_id=(other, lax.axis_index("batch")), device_id_type=MESH
        )
    pl.semaphore_wait(barrier, BANDS - 1)


def dot(a, b, dims):
    return lax.dot_general(a, b, ((dims[0], dims[1]), ((), ())), preferred_element_type=F32)


NN = ((1,), (0,))
NT = ((1,), (1,))
TN = ((0,), (0,))


def attend_kernel(
    cnt_ref, h_ref, gain_ref, shift_ref, wq_ref, bq_ref, wkv_ref, bkv_ref,
    n1_ref, q_ref, kv_ref, kvt_ref, o_ref, lse_ref, att_ref,
    rows_ref, out_ref, send, recv, out_send, out_recv,
):
    band, y, x, core = place()
    here_y = y * 2
    greet_band()
    own = pl.ds(pl.multiple_of(y * CAP, CAP), CAP)
    half = pl.ds(pl.multiple_of(core * HALF, HALF), HALF)
    other_y, other_x, other_core = 1 - y, 1 - x, 1 - core
    sibling = device(y, x, other_core)
    copies = {}

    def go(name, src, dst, index, recv_index, target):
        copy = push(src, dst, send.at[index], recv.at[recv_index], target)
        copy.start()
        copies[name] = copy

    for k in range(2):
        from_rows = pl.ds(pl.multiple_of(other_y * CAP + k * HALF, HALF), HALF)
        go(("y", k), h_ref.at[from_rows], rows_ref.at[band, pl.ds(k * HALF, HALF)], 1 + k, 1 + core,
           device(other_y, x, k))
    for k in range(2):
        from_rows = pl.ds(pl.multiple_of(y * CAP + k * HALF, HALF), HALF)
        go(("x", k), h_ref.at[from_rows], rows_ref.at[band, pl.ds(k * HALF, HALF)], 3 + k, 3 + core,
           device(y, other_x, k))
    go("sib", h_ref.at[own], rows_ref.at[band], 0, 0, sibling)

    gain, shift = gain_ref[...], shift_ref[...]

    def project(rows, which):
        wide = rows.astype(F32)
        center = wide - jnp.mean(wide, axis=-1, keepdims=True)
        spread = jnp.mean(center * center, axis=-1, keepdims=True)
        n1 = (center * lax.rsqrt(spread + 1e-05) * gain + shift).astype(BF)
        at = pl.ds(pl.multiple_of(which * CAP, CAP), CAP)
        n1_ref[at, :] = n1
        kv = (dot(n1, wkv_ref[...], NN) + bkv_ref[...]).astype(BF)
        turned = kv.T
        qt = ((dot(wq_ref[...], n1, NT) + bq_ref[...]) * 0.125).astype(BF)
        for h in range(MINE):
            kv_ref[h, at, :] = kv[:, h * 128 : (h + 1) * 128]
            kvt_ref[h, :, at] = turned[h * 128 : (h + 1) * 128]
            q_ref[h, :HEAD, at] = qt[h * HEAD : (h + 1) * HEAD]
            q_ref[h, HEAD:, at] = jnp.zeros((HEAD, CAP), BF)

    def project_two(first_y, first_x):
        def one(k, carry):
            which = first_y * 4 + first_x * 2 + k
            project(rows_ref[which], which)
            return carry

        lax.fori_loop(0, 2, one, 0)

    rows_ref[band] = h_ref[own, :]

    def wait_recv(index, which, size=HALF):
        ref = rows_ref.at[which] if size == CAP else rows_ref.at[which, half]
        push(ref, ref, send.at[0], recv.at[index], sibling).wait_recv()

    wait_recv(0, y * 4 + x * 2 + other_core, CAP)
    project_two(y, x)
    for k in range(2):
        from_band = other_y * 4 + x * 2 + k
        wait_recv(1 + k, from_band)
        piece = rows_ref.at[from_band, half]
        go(("fx", k), piece, piece, 5 + k, 5 + k, device(y, other_x, core))
        go(("fs", k), piece, piece, 7 + k, 7 + k, sibling)
    for k in range(2):
        from_band = y * 4 + other_x * 2 + k
        wait_recv(3 + k, from_band)
        piece = rows_ref.at[from_band, half]
        go(("fs", 2 + k), piece, piece, 9 + k, 9 + k, sibling)
    for k in range(2):
        copies[("fs", k)].wait_recv()
    project_two(other_y, x)
    for k in range(2):
        copies[("fs", 2 + k)].wait_recv()
    project_two(y, other_x)
    for k in range(2):
        from_band = other_y * 4 + other_x * 2 + k
        copies[("fx", k)].wait_recv()
        piece = rows_ref.at[from_band, half]
        go(("fs", 4 + k), piece, piece, 11 + k, 11 + k, sibling)
    for k in range(2):
        copies[("fs", 4 + k)].wait_recv()
    project_two(other_y, other_x)

    key_at = lax.broadcasted_iota(jnp.int32, (CAP, CAP), 0)
    query_at = lax.broadcasted_iota(jnp.int32, (CAP, CAP), 1)
    lane = lax.broadcasted_iota(jnp.int32, (1, CAP), 1)
    share = pl.ds(pl.multiple_of((2 * x + core) * SHARE, SHARE), SHARE)
    side = pl.ds(pl.multiple_of(y * CAP, CAP), CAP)
    for i in range(BANDS - 1, -1, -1):
        cols = pl.ds(i * CAP, CAP)

        def one_head(h, carry):
            qt = q_ref[h, :, cols]
            scores = []
            for j in range(i + 1):
                s = dot(kv_ref[h, j * CAP : (j + 1) * CAP, :], qt, NN)
                keep = key_at < cnt_ref[j]
                if i == j:
                    keep = keep & (key_at <= query_at)
                scores.append(jnp.where(keep, s, NEG))
            top = functools.reduce(jnp.maximum, [jnp.max(s, axis=0, keepdims=True) for s in scores])
            total = jnp.zeros((1, CAP), F32)
            mix = jnp.zeros((HEAD, CAP), F32)
            for j in range(i + 1):
                p = jnp.exp(scores[j] - top)
                total = total + jnp.sum(p, axis=0, keepdims=True)
                mix = mix + dot(kvt_ref[h, HEAD:, j * CAP : (j + 1) * CAP], p.astype(BF), NN)
            valid = lane < cnt_ref[i]
            mix = jnp.where(valid, mix / total, kvt_ref[h, HEAD:, cols].astype(F32))
            o_ref[h, :, cols] = mix
            lse_ref[h, i : i + 1, :] = jnp.where(valid, top + jnp.log(total), -NEG)
            return carry

        lax.fori_loop(0, MINE, one_head, 0)
        for h in range(MINE):
            out_ref[i, h * HEAD : (h + 1) * HEAD, :] = o_ref[h, :, cols].astype(BF)

        def send_away(i=i):
            push(out_ref.at[i], att_ref.at[share, side], out_send.at[i], out_recv.at[band],
                 (i, lax.axis_index("batch"))).start()

        def keep_here(i=i):
            pltpu.make_async_copy(out_ref.at[i], att_ref.at[share, side], out_recv.at[band]).start()

        pl.when(band != i)(send_away)
        pl.when(band == i)(keep_here)
    for i in range(BANDS):
        from_y, from_x, from_core = i // 4, (i // 2) % 2, i % 2
        ref = att_ref.at[pl.ds((2 * from_x + from_core) * SHARE, SHARE), pl.ds(from_y * CAP, CAP)]
        copy = push(out_ref.at[i], ref, out_send.at[i], out_recv.at[i], sibling)
        copy.wait_recv()
        pl.when(band != i)(copy.wait_send)
    for copy in copies.values():
        copy.wait_send()


def attend_call(cnt, h, gain, shift, wq, bq, wkv, bkv):
    width = h.shape[1]
    seq = BANDS * CAP
    vm = pl.BlockSpec(memory_space=VM)
    return pl.pallas_call(
        attend_kernel,
        name="attend",
        out_shape=[
            jax.ShapeDtypeStruct((seq, width), BF),
            jax.ShapeDtypeStruct((MINE, 128, seq), BF),
            jax.ShapeDtypeStruct((MINE, seq, 128), BF),
            jax.ShapeDtypeStruct((MINE, 128, seq), BF),
            jax.ShapeDtypeStruct((MINE, HEAD, seq), F32),
            jax.ShapeDtypeStruct((MINE, BANDS, CAP), F32),
            jax.ShapeDtypeStruct((4 * SHARE, 2 * CAP), BF),
        ],
        in_specs=[pl.BlockSpec(memory_space=pltpu.SMEM)] + [vm] * 7,
        out_specs=[vm] * 7,
        scratch_shapes=[
            VM((BANDS, CAP, width), BF),
            VM((BANDS, SHARE, CAP), BF),
            pltpu.SemaphoreType.DMA((13,)),
            pltpu.SemaphoreType.DMA((13,)),
            pltpu.SemaphoreType.DMA((BANDS,)),
            pltpu.SemaphoreType.DMA((BANDS,)),
        ],
        compiler_params=pltpu.CompilerParams(
            collective_id=0, has_side_effects=True, vmem_limit_bytes=56 * 2**20
        ),
    )(cnt, h, gain, shift, wq, bq, wkv, bkv)


def back_kernel(
    cnt_ref, da_ref, n1_ref, q_ref, kv_ref, kvt_ref, o_ref, lse_ref, w_ref,
    dn_ref, dw_ref, sums_ref,
    do_ref, dk_ref, d_ref, mine_ref, sib_out, sib_in, row_out,
    do_send, do_recv, sib_send, sib_recv, dn_send, dn_recv,
):
    band, y, x, core = place()
    batch = lax.axis_index("batch")
    greet_band()
    sibling = device(y, x, 1 - core)
    half = pl.ds(pl.multiple_of(core * HALF, HALF), HALF)
    other = pl.ds(pl.multiple_of((1 - core) * HALF, HALF), HALF)

    def part_for(i):
        to_y, to_x, to_core = i // 4, (i // 2) % 2, i % 2
        return da_ref.at[pl.ds((2 * to_x + to_core) * SHARE, SHARE), pl.ds(to_y * CAP, CAP)]

    for i in range(BANDS):
        copy = push(part_for(i), do_ref.at[band], do_send.at[i], do_recv.at[band], (i, batch))
        pl.when(band != i)(copy.start)
        local = pltpu.make_async_copy(part_for(i), do_ref.at[band], do_recv.at[band])
        pl.when(band == i)(local.start)

    key_at = lax.broadcasted_iota(jnp.int32, (CAP, CAP), 0)
    query_at = lax.broadcasted_iota(jnp.int32, (CAP, CAP), 1)
    dk_ref[...] = jnp.zeros_like(dk_ref)

    def sib_copy(i):
        return push(sib_out.at[i], sib_in.at[i], sib_send.at[i], sib_recv.at[i], sibling)

    def finish(i):
        sib_copy(i).wait_recv()
        row_out[i] = (mine_ref[i % 2] + sib_in[i].astype(F32)).astype(BF)
        copy = push(row_out.at[i], dn_ref.at[y, x, half], dn_send.at[i], dn_recv.at[band], (i, batch))
        pl.when(band != i)(copy.start)
        local = pltpu.make_async_copy(row_out.at[i], dn_ref.at[y, x, half], dn_recv.at[band])
        pl.when(band == i)(local.start)

    for i in range(BANDS - 1, -1, -1):
        cols = pl.ds(i * CAP, CAP)
        push(do_ref.at[i], do_ref.at[i], do_send.at[i], do_recv.at[i], sibling).wait_recv()

        def one_head(h, carry):
            qt = q_ref[h, :, cols]
            dot_t = do_ref[i, pl.ds(pl.multiple_of(h * HEAD, HEAD), HEAD), :]
            dop = jnp.concatenate([jnp.zeros_like(dot_t), dot_t], axis=0)
            lse = lse_ref[h, i : i + 1, :]
            delta = jnp.sum(dot_t.astype(F32) * o_ref[h, :, cols], axis=0, keepdims=True)
            dq = jnp.zeros((HEAD, CAP), F32)
            for j in range(i + 1):
                at = pl.ds(j * CAP, CAP)
                kv = kv_ref[h, at, :]
                s = dot(kv, qt, NN)
                dp = dot(kv, dop, NN)
                keep = key_at < cnt_ref[j]
                if i == j:
                    keep = keep & (key_at <= query_at)
                p = jnp.where(keep, jnp.exp(s - lse), 0.0)
                if i == j:
                    alone = (key_at == query_at) & (query_at >= cnt_ref[i])
                    p = jnp.where(alone, 1.0, p)
                ds = (p * (dp - delta)).astype(BF)
                dq = dq + dot(kvt_ref[h, :HEAD, at], ds, NN)
                dk_ref[h, at, :] += dot(ds, qt, NT) + dot(p.astype(BF), dop, NT)
            d_ref[pl.ds(pl.multiple_of(h * HEAD, HEAD), HEAD), cols] = (dq * 0.125).astype(BF)
            d_ref[pl.ds(pl.multiple_of(SHARE + h * 128, HEAD), 128), cols] = dk_ref[h, cols, :].T.astype(BF)
            return carry

        lax.fori_loop(0, MINE, one_head, 0)
        dn = dot(d_ref[:, cols], w_ref[...], TN)
        mine_ref[2, :, :] = dn[:HALF]
        mine_ref[3, :, :] = dn[HALF:]
        sib_out[i] = mine_ref[2 + (1 - core)].astype(BF)
        mine_ref[i % 2] = mine_ref[2 + core]
        sib_copy(i).start()
        if i < BANDS - 1:
            finish(i + 1)
    dw_ref[...] = dot(d_ref[...], n1_ref[...], NN)
    sums_ref[...] = dot(jnp.ones((8, d_ref.shape[1]), BF), d_ref[...], NT)
    finish(0)
    for i in range(BANDS):
        copy = push(part_for(i), do_ref.at[i], do_send.at[i], do_recv.at[i], sibling)
        pl.when(band != i)(copy.wait_send)
        sib_copy(i).wait_send()
        copy = push(row_out.at[i], dn_ref.at[i // 4, i // 2 % 2, pl.ds(i % 2 * HALF, HALF)],
                    dn_send.at[i], dn_recv.at[i], sibling)
        pl.when(band != i)(copy.wait_send)
        copy.wait_recv()


def back_call(cnt, da, n1, q, kv, kvt, o, lse, w):
    width = n1.shape[1]
    seq = BANDS * CAP
    vm = pl.BlockSpec(memory_space=VM)
    dma = pltpu.SemaphoreType.DMA((BANDS,))
    return pl.pallas_call(
        back_kernel,
        name="back",
        out_shape=[
            jax.ShapeDtypeStruct((2, 2, CAP, width), BF),
            jax.ShapeDtypeStruct((3 * SHARE, width), F32),
            jax.ShapeDtypeStruct((8, 3 * SHARE), F32),
        ],
        in_specs=[pl.BlockSpec(memory_space=pltpu.SMEM)] + [vm] * 8,
        out_specs=[vm] * 3,
        scratch_shapes=[
            VM((BANDS, SHARE, CAP), BF),
            VM((MINE, seq, 128), F32),
            VM((3 * SHARE, seq), BF),
            VM((4, HALF, width), F32),
            VM((BANDS, HALF, width), BF),
            VM((BANDS, HALF, width), BF),
            VM((BANDS, HALF, width), BF),
        ] + [dma] * 6,
        compiler_params=pltpu.CompilerParams(
            collective_id=1, has_side_effects=True, vmem_limit_bytes=56 * 2**20
        ),
    )(cnt, da, n1, q, kv, kvt, o, lse, w)


CHUNK = 1024
QROWS = 640
STAGES = 9


def sum_kernel(
    g_ref, gq_ref, f_ref, fq_ref,
    b0, a0, b1, a1, b2, a2, b3, qb1, qa1, qb3,
    s0, r0, s1, r1, s2, r2, s3, r3, t3, u3, t2, u2, t1, u1, t0, u0,
    qs, qr, qs3, qr3, qt3, qu3,
):
    band, y, x, core = place()
    batch = lax.axis_index("batch")
    chunks = g_ref.shape[0]
    sibling = device(y, x, 1 - core)
    x_side = device(y, 1 - x, core)
    y_side = device(1 - y, x, core)
    barrier = pltpu.get_barrier_semaphore()
    for target in (sibling, x_side, y_side):
        pl.semaphore_signal(barrier, inc=1, device_id=target, device_id_type=MESH)
    for step in range(1, 4):
        pl.semaphore_signal(
            barrier, inc=1, device_id=(band, (batch + step) % 4), device_id_type=MESH
        )
    pl.semaphore_wait(barrier, 6)

    first, second = (x, y), (y, x)
    first_to, second_to = (x_side, y_side), (y_side, x_side)

    def send0(k):
        return push(g_ref.at[k, 1 - core], b0.at[k], s0.at[k], r0.at[k], sibling)

    def send1(k, p):
        return push(a0.at[k, p, 1 - first[p]], b1.at[k, p], s1.at[k, p], r1.at[k, p], first_to[p])

    def send2(k, p):
        return push(a1.at[k, p, 1 - second[p]], b2.at[k, p], s2.at[k, p], r2.at[k, p], second_to[p])

    def send3(k, step):
        to = (batch + step) % 4
        return push(a2.at[k, to], b3.at[k, step - 1], s3.at[k, step - 1], r3.at[k, step - 1], (band, to))

    def back3(k, p, step, frm):
        piece = f_ref.at[k, core, p, first[p], second[p], frm]
        return push(piece, piece, t3.at[k, p, step - 1], u3.at[k, p, step - 1], (band, (batch + step) % 4))

    def back2(k, p, at):
        piece = f_ref.at[k, core, p, first[p], at]
        return push(piece, piece, t2.at[k, p], u2.at[k, p], second_to[p])

    def back1(k, p, at):
        piece = f_ref.at[k, core, p, at]
        return push(piece, piece, t1.at[k, p], u1.at[k, p], first_to[p])

    def back0(k, at):
        piece = f_ref.at[k, at]
        return push(piece, piece, t0.at[k], u0.at[k], sibling)

    def stage(index, k):
        if index == 0:
            send0(k).start()
        elif index == 1:
            send0(k).wait_recv()
            for p in range(2):
                for f in range(2):
                    a0[k, p, f] = (g_ref[k, core, p, f].astype(F32) + b0[k, p, f].astype(F32)).astype(BF)
                send1(k, p).start()
        elif index == 2:
            for p in range(2):
                send1(k, p).wait_recv()
                a1[k, p] = (a0[k, p, first[p]].astype(F32) + b1[k, p].astype(F32)).astype(BF)
                send2(k, p).start()
        elif index == 3:
            for p in range(2):
                send2(k, p).wait_recv()
                for z in range(4):
                    a2[k, z, p] = (a1[k, p, second[p], z].astype(F32) + b2[k, p, z].astype(F32)).astype(BF)
            for step in range(1, 4):
                send3(k, step).start()
        elif index == 4:
            for step in range(1, 4):
                send3(k, step).wait_recv()
            for p in range(2):
                total = a2[k, batch, p].astype(F32)
                for step in range(3):
                    total = total + b3[k, step, p].astype(F32)
                f_ref[k, core, p, first[p], second[p], batch] = total.astype(BF)
                for step in range(1, 4):
                    back3(k, p, step, batch).start()
        elif index == 5:
            for p in range(2):
                for step in range(1, 4):
                    back3(k, p, step, (batch + 4 - step) % 4).wait_recv()
                back2(k, p, second[p]).start()
        elif index == 6:
            for p in range(2):
                back2(k, p, 1 - second[p]).wait_recv()
                back1(k, p, first[p]).start()
        elif index == 7:
            for p in range(2):
                back1(k, p, 1 - first[p]).wait_recv()
            back0(k, core).start()
        elif index == 8:
            back0(k, 1 - core).wait_recv()

    def drain(k):
        send0(k).wait_send()
        for p in range(2):
            send1(k, p).wait_send()
            send2(k, p).wait_send()
            back2(k, p, second[p]).wait_send()
            back1(k, p, first[p]).wait_send()
            for step in range(1, 4):
                back3(k, p, step, batch).wait_send()
        for step in range(1, 4):
            send3(k, step).wait_send()
        back0(k, core).wait_send()

    def q1():
        return push(gq_ref.at[1 - y], qb1, qs.at[0], qr.at[0], y_side)

    def q3(step):
        to = (batch + step) % 4
        return push(qa1.at[to], qb3.at[step - 1], qs3.at[step - 1], qr3.at[step - 1], (band, to))

    def q_back3(step, frm):
        piece = fq_ref.at[x, core, y, frm]
        return push(piece, piece, qt3.at[step - 1], qu3.at[step - 1], (band, (batch + step) % 4))

    def q_back(index, at):
        if index == 1:
            piece, to = fq_ref.at[x, core, at], y_side
        elif index == 2:
            piece, to = fq_ref.at[at, core], x_side
        else:
            piece, to = fq_ref.at[:, at], sibling
        return push(piece, piece, qs.at[index], qr.at[index], to)

    def q_stage(index):
        if index == 0:
            q1().start()
        elif index == 1:
            q1().wait_recv()
            for z in range(4):
                qa1[z] = (gq_ref[y, z].astype(F32) + qb1[z].astype(F32)).astype(BF)
            for step in range(1, 4):
                q3(step).start()
        elif index == 2:
            for step in range(1, 4):
                q3(step).wait_recv()
            total = qa1[batch].astype(F32)
            for step in range(3):
                total = total + qb3[step].astype(F32)
            fq_ref[x, core, y, batch] = total.astype(BF)
            for step in range(1, 4):
                q_back3(step, batch).start()
        elif index == 3:
            for step in range(1, 4):
                q_back3(step, (batch + 4 - step) % 4).wait_recv()
            q_back(1, y).start()
        elif index == 4:
            q_back(1, 1 - y).wait_recv()
            q_back(2, x).start()
        elif index == 5:
            q_back(2, 1 - x).wait_recv()
            q_back(3, core).start()
        elif index == 6:
            q_back(3, 1 - core).wait_recv()

    def q_drain():
        q1().wait_send()
        for step in range(1, 4):
            q3(step).wait_send()
            q_back3(step, batch).wait_send()
        q_back(1, y).wait_send()
        q_back(2, x).wait_send()
        q_back(3, core).wait_send()

    def step(t, carry):
        for index in range(STAGES - 1, -1, -1):
            k = t - index

            @pl.when((k >= 0) & (k < chunks))
            def _(index=index, k=k):
                stage(index, k)

        for index in range(6, -1, -1):

            @pl.when(t == 2 + index * 2)
            def _(index=index):
                q_stage(index)

        return carry

    lax.fori_loop(0, chunks + STAGES, step, 0)

    def finish(k, carry):
        drain(k)
        return carry

    lax.fori_loop(0, chunks, finish, 0)
    q_drain()


def sum_call(g, gq):
    chunks, width = g.shape[0] // CHUNK, g.shape[1]
    vm = pl.BlockSpec(memory_space=VM)
    dma = pltpu.SemaphoreType.DMA
    g = g.reshape(chunks, 2, 2, 2, 2, 4, 16, width)
    gq = gq.reshape(2, 4, QROWS // 8, width)

    def room(*shape):
        return VM(shape + (width,), BF)

    f, fq = pl.pallas_call(
        sum_kernel,
        name="sum_all",
        out_shape=[
            jax.ShapeDtypeStruct(g.shape, BF),
            jax.ShapeDtypeStruct((2, 2, 2, 4, QROWS // 8, width), BF),
        ],
        in_specs=[vm] * 2,
        out_specs=[vm] * 2,
        scratch_shapes=[
            room(chunks, 2, 2, 2, 4, 16),
            room(chunks, 2, 2, 2, 4, 16),
            room(chunks, 2, 2, 4, 16),
            room(chunks, 2, 2, 4, 16),
            room(chunks, 2, 4, 16),
            room(chunks, 4, 2, 16),
            room(chunks, 3, 2, 16),
            room(4, QROWS // 8),
            room(4, QROWS // 8),
            room(3, QROWS // 8),
        ]
        + [dma((chunks,))] * 2 + [dma((chunks, 2))] * 4 + [dma((chunks, 3))] * 2
        + [dma((chunks, 2, 3))] * 2 + [dma((chunks, 2))] * 4 + [dma((chunks,))] * 2
        + [dma((4,))] * 2 + [dma((3,))] * 4,
        compiler_params=pltpu.CompilerParams(
            collective_id=2, has_side_effects=True, vmem_limit_bytes=60 * 2**20
        ),
    )(g, gq)
    return f.reshape(chunks * CHUNK, width), fq.reshape(4, QROWS, width)


def left_product(left_mat, right_mat):
    return lax.dot_general(
        left_mat, right_mat, (((0,), (0,)), ((), ())), preferred_element_type=jnp.float32
    )


def right_product(left_mat, weight):
    return lax.dot_general(
        left_mat, weight, (((1,), (1,)), ((), ())), preferred_element_type=jnp.float32
    )


def slot_tags(first_row, count_rows, layout):
    begins_flat, finishes_flat, slot_rows, band_cap, band_count = layout
    slot_index = first_row + jnp.arange(count_rows, dtype=jnp.int32)
    owner = slot_index // slot_rows
    within = slot_index - owner * slot_rows
    member = within // band_cap
    offset = within - member * band_cap
    flat_code = member * band_count + owner
    all_codes = jnp.arange(begins_flat.shape[0], dtype=jnp.int32)
    hit_table = flat_code[:, None] == all_codes[None, :]
    begins = jnp.sum(jnp.where(hit_table, begins_flat[None, :], 0), axis=1)
    finish = jnp.sum(jnp.where(hit_table, finishes_flat[None, :], 0), axis=1)
    position = begins + offset
    return (member, position, position < finish, slot_index)


def allowed_pairs(query_tags, key_tags):
    query_member, query_position, query_valid, query_slot = query_tags
    key_member, key_position, key_valid, key_slot = key_tags
    same_slot = query_slot[:, None] == key_slot[None, :]
    causal = (query_member[:, None] == key_member[None, :]) & (
        key_position[None, :] <= query_position[:, None]
    )
    return same_slot | query_valid[:, None] & key_valid[None, :] & causal


def on_device(
    residual_in,
    exit_layer,
    band_edges,
    norm1_gain,
    norm1_bias,
    query_weight,
    query_bias,
    key_weight,
    value_weight,
    value_bias,
    out_weight,
    out_bias,
    norm2_gain,
    norm2_bias,
    up_weight,
    up_bias,
    down_weight,
    down_bias,
    cotangent,
):
    slot_rows = residual_in.shape[1]
    model_width = residual_in.shape[2]
    head_size = model_width // HEADS
    score_scale = head_size ** (-0.5)
    band_here = lax.axis_index("band")
    band_count = lax.axis_size("band")
    band_cap = slot_rows // band_edges.shape[1]
    finishes = jnp.concatenate([band_edges[0][:, 1:], band_edges[0][:, -1:] + band_cap], axis=1)
    layout = (band_edges[0].reshape(-1), finishes.reshape(-1), slot_rows, band_cap, band_count)
    own_tags = slot_tags(band_here * slot_rows, slot_rows, layout)
    active = ((exit_layer[0] >= LAYER) & own_tags[2]).astype(jnp.float32)[:, None]
    total_active = lax.psum(jnp.sum(active), ("band", "batch"))
    hidden_in = residual_in[0].astype(jnp.float32)
    normed_one, norm_one_back = jax.vjp(
        norm_affine, hidden_in, norm1_gain.astype(jnp.float32), norm1_bias.astype(jnp.float32)
    )
    normed_low = normed_one.astype(jnp.bfloat16)
    queries = (
        jnp.dot(normed_low, query_weight, preferred_element_type=jnp.float32)
        + query_bias.astype(jnp.float32)
    ).astype(jnp.bfloat16)
    keys_own = jnp.dot(normed_low, key_weight, preferred_element_type=jnp.float32).astype(
        jnp.bfloat16
    )
    values_own = (
        jnp.dot(normed_low, value_weight, preferred_element_type=jnp.float32)
        + value_bias.astype(jnp.float32)
    ).astype(jnp.bfloat16)
    query_heads = queries.reshape(slot_rows, HEADS, head_size)
    start_state = (
        jnp.full((HEADS, slot_rows), -1e30, jnp.float32),
        jnp.zeros((HEADS, slot_rows), jnp.float32),
        jnp.zeros((slot_rows, HEADS, head_size), jnp.float32),
    )
    key_piece = lax.all_gather(keys_own, "band", axis=0, tiled=True)
    value_piece = lax.all_gather(values_own, "band", axis=0, tiled=True)
    piece_rows = key_piece.shape[0]
    step_rows = min(piece_rows, slot_rows)

    def one_step(step_index, inner_state):
        offset_row = step_index * step_rows
        key_block = lax.dynamic_slice_in_dim(key_piece, offset_row, step_rows, 0).reshape(
            step_rows, HEADS, head_size
        )
        value_block = lax.dynamic_slice_in_dim(value_piece, offset_row, step_rows, 0).reshape(
            step_rows, HEADS, head_size
        )
        mask = allowed_pairs(own_tags, slot_tags(offset_row, step_rows, layout))

        def accumulate(running):
            top_old, total_old, sum_old = running
            scores = (
                jnp.einsum(
                    "qhd,khd->hqk", query_heads, key_block, preferred_element_type=jnp.float32
                )
                * score_scale
            )
            scores = jnp.where(mask[None], scores, -1e30)
            top_new = jnp.maximum(top_old, jnp.max(scores, axis=-1))
            rescale = jnp.exp(top_old - top_new)
            weights_new = jnp.where(mask[None], jnp.exp(scores - top_new[..., None]), 0.0)
            total_new = total_old * rescale + jnp.sum(weights_new, axis=-1)
            sum_new = sum_old * rescale.T[..., None] + jnp.einsum(
                "hqk,khd->qhd",
                weights_new.astype(jnp.bfloat16),
                value_block,
                preferred_element_type=jnp.float32,
            )
            return (top_new, total_new, sum_new)

        return lax.cond(jnp.any(mask), accumulate, lambda running: running, inner_state)

    top_score, weight_total, weighted_sum = lax.fori_loop(
        0, piece_rows // step_rows, one_step, start_state
    )
    attended = weighted_sum / weight_total.T[..., None]
    log_total = top_score + jnp.log(weight_total)
    mixed_low = attended.reshape(slot_rows, model_width).astype(jnp.bfloat16)
    branch = jnp.dot(mixed_low, out_weight, preferred_element_type=jnp.float32) + out_bias.astype(
        jnp.float32
    )
    middle = hidden_in + active * branch
    normed_two, norm_two_back = jax.vjp(
        norm_affine, middle, norm2_gain.astype(jnp.float32), norm2_bias.astype(jnp.float32)
    )
    normed_two_low = normed_two.astype(jnp.bfloat16)
    pre_act = jnp.dot(
        normed_two_low, up_weight, preferred_element_type=jnp.float32
    ) + up_bias.astype(jnp.float32)
    activated, gelu_back = jax.vjp(jax.nn.gelu, pre_act)
    activated_low = activated.astype(jnp.bfloat16)
    down_out = jnp.dot(
        activated_low, down_weight, preferred_element_type=jnp.float32
    ) + down_bias.astype(jnp.float32)
    layer_out = (middle + active * down_out).astype(jnp.bfloat16)[None]
    out_grad = cotangent[0].astype(jnp.float32)
    down_grad = (active * out_grad).astype(jnp.bfloat16)
    down_weight_sum = left_product(activated_low, down_grad)
    down_bias_sum = jnp.sum(down_grad.astype(jnp.float32), axis=0)
    (pre_grad,) = gelu_back(right_product(down_grad, down_weight))
    pre_low = pre_grad.astype(jnp.bfloat16)
    up_weight_sum = left_product(normed_two_low, pre_low)
    up_bias_sum = jnp.sum(pre_low.astype(jnp.float32), axis=0)
    middle_norm, gain_two_sum, shift_two_sum = norm_two_back(right_product(pre_low, up_weight))
    middle_grad = out_grad + middle_norm
    branch_grad = (active * middle_grad).astype(jnp.bfloat16)
    out_weight_sum = left_product(mixed_low, branch_grad)
    out_bias_sum = jnp.sum(branch_grad.astype(jnp.float32), axis=0)
    mixed_grad = right_product(branch_grad, out_weight).astype(jnp.bfloat16)
    grad_heads = mixed_grad.reshape(slot_rows, HEADS, head_size)
    delta_row = jnp.sum(grad_heads.astype(jnp.float32) * attended, axis=-1).T

    def pair_terms(query_blk, grad_blk, logsum_blk, delta_blk, key_block, value_block, mask):
        scores = (
            jnp.einsum("qhd,khd->hqk", query_blk, key_block, preferred_element_type=jnp.float32)
            * score_scale
        )
        probability = jnp.where(mask[None], jnp.exp(scores - logsum_blk[..., None]), 0.0)
        prob_grad = jnp.einsum(
            "qhd,khd->hqk", grad_blk, value_block, preferred_element_type=jnp.float32
        )
        score_grad = (probability * (prob_grad - delta_blk[..., None])).astype(jnp.bfloat16)
        return (probability.astype(jnp.bfloat16), score_grad)

    all_rows = slot_rows * band_count
    start_back = (
        jnp.zeros((slot_rows, HEADS, head_size), jnp.float32),
        jnp.zeros((all_rows, model_width), jnp.float32),
        jnp.zeros((all_rows, model_width), jnp.float32),
    )
    fold_key_piece = lax.all_gather(keys_own, "band", axis=0, tiled=True)
    fold_value_piece = lax.all_gather(values_own, "band", axis=0, tiled=True)
    piece_rows = fold_key_piece.shape[0]
    fold_step_rows = min(piece_rows, slot_rows)

    def one_step(step_index, inner_state):
        offset_row = step_index * fold_step_rows
        key_block = lax.dynamic_slice_in_dim(fold_key_piece, offset_row, fold_step_rows, 0).reshape(
            fold_step_rows, HEADS, head_size
        )
        value_block = lax.dynamic_slice_in_dim(
            fold_value_piece, offset_row, fold_step_rows, 0
        ).reshape(fold_step_rows, HEADS, head_size)
        mask = allowed_pairs(own_tags, slot_tags(offset_row, fold_step_rows, layout))

        def accumulate(running):
            query_acc, key_sums, value_sums = running
            prob_low, score_grad = pair_terms(
                query_heads, grad_heads, log_total, delta_row, key_block, value_block, mask
            )
            query_acc = (
                query_acc
                + jnp.einsum(
                    "hqk,khd->qhd", score_grad, key_block, preferred_element_type=jnp.float32
                )
                * score_scale
            )
            key_term = (
                jnp.einsum(
                    "hqk,qhd->khd", score_grad, query_heads, preferred_element_type=jnp.float32
                ).reshape(fold_step_rows, model_width)
                * score_scale
            )
            value_term = jnp.einsum(
                "hqk,qhd->khd", prob_low, grad_heads, preferred_element_type=jnp.float32
            ).reshape(fold_step_rows, model_width)
            key_sums = lax.dynamic_update_slice_in_dim(
                key_sums,
                lax.dynamic_slice_in_dim(key_sums, offset_row, fold_step_rows, 0) + key_term,
                offset_row,
                0,
            )
            value_sums = lax.dynamic_update_slice_in_dim(
                value_sums,
                lax.dynamic_slice_in_dim(value_sums, offset_row, fold_step_rows, 0) + value_term,
                offset_row,
                0,
            )
            return (query_acc, key_sums, value_sums)

        return lax.cond(jnp.any(mask), accumulate, lambda running: running, inner_state)

    back_state = lax.fori_loop(0, piece_rows // fold_step_rows, one_step, start_back)
    query_sum, key_sums_all, value_sums_all = back_state
    key_sum, value_sum = (
        lax.psum_scatter(
            key_sums_all.astype(jnp.bfloat16), "band", scatter_dimension=0, tiled=True
        ).astype(jnp.float32),
        lax.psum_scatter(
            value_sums_all.astype(jnp.bfloat16), "band", scatter_dimension=0, tiled=True
        ).astype(jnp.float32),
    )
    query_low = query_sum.reshape(slot_rows, model_width).astype(jnp.bfloat16)
    key_low = key_sum.astype(jnp.bfloat16)
    value_low = value_sum.astype(jnp.bfloat16)
    query_weight_sum = left_product(normed_low, query_low)
    query_bias_sum = jnp.sum(query_low.astype(jnp.float32), axis=0)
    key_weight_sum = left_product(normed_low, key_low)
    value_weight_sum = left_product(normed_low, value_low)
    value_bias_sum = jnp.sum(value_low.astype(jnp.float32), axis=0)
    normed_grad = (
        right_product(query_low, query_weight)
        + right_product(key_low, key_weight)
        + right_product(value_low, value_weight)
    )
    input_norm, gain_one_sum, shift_one_sum = norm_one_back(normed_grad)
    input_grad = (middle_grad + input_norm)[None]
    (
        total_g1,
        total_b1,
        total_qw,
        total_qb,
        total_kw,
        total_vw,
        total_vb,
        total_ow,
        total_ob,
        total_g2,
        total_b2,
        total_uw,
        total_ub,
        total_dw,
        total_db,
    ) = lax.psum(
        (
            gain_one_sum,
            shift_one_sum,
            query_weight_sum,
            query_bias_sum,
            key_weight_sum,
            value_weight_sum,
            value_bias_sum,
            out_weight_sum,
            out_bias_sum,
            gain_two_sum,
            shift_two_sum,
            up_weight_sum,
            up_bias_sum,
            down_weight_sum,
            down_bias_sum,
        ),
        ("band", "batch"),
    )
    return (
        layer_out,
        input_grad,
        total_g1 / total_active,
        total_b1 / total_active,
        total_qw / total_active,
        total_qb / total_active,
        total_kw / total_active,
        total_vw / total_active,
        total_vb / total_active,
        total_ow / total_active,
        total_ob / total_active,
        total_g2 / total_active,
        total_b2 / total_active,
        total_uw / total_active,
        total_ub / total_active,
        total_dw / total_active,
        total_db / total_active,
    )


def norm_rows(values):
    center = values - jnp.mean(values, axis=-1, keepdims=True)
    spread = jnp.mean(center * center, axis=-1, keepdims=True)
    return center * lax.rsqrt(spread + 1e-05)


def norm_affine(values, gain_vec, shift_vec):
    return norm_rows(values) * gain_vec + shift_vec


def fast_device(
    residual_in, exit_layer, band_edges, norm1_gain, norm1_bias, query_weight, query_bias,
    key_weight, value_weight, value_bias, out_weight, out_bias, norm2_gain, norm2_bias,
    up_weight, up_bias, down_weight, down_bias, cotangent,
):
    band, y, x, core = place()
    width = residual_in.shape[2]
    hidden = up_weight.shape[1]
    edges = band_edges[0]
    counts = jnp.concatenate([edges[:, 1:], edges[:, -1:] + CAP], axis=1) - edges
    cnt_seq = lax.dynamic_index_in_dim(counts, y, 0, keepdims=False)
    cnt_own = lax.dynamic_index_in_dim(counts, band, 1, keepdims=False)
    valid = (jnp.arange(CAP)[None, :] < cnt_own[:, None]).reshape(-1)
    active = ((exit_layer[0] >= LAYER) & valid).astype(F32)[:, None]
    total_active = lax.psum(jnp.sum(active), ("band", "batch"))
    start = (2 * x + core) * SHARE
    wq_t = lax.dynamic_slice_in_dim(query_weight, start, SHARE, 1).T
    wk = lax.dynamic_slice_in_dim(key_weight, start, SHARE, 1).reshape(width, MINE, HEAD)
    wv = lax.dynamic_slice_in_dim(value_weight, start, SHARE, 1).reshape(width, MINE, HEAD)
    wkv = jnp.concatenate([wk, wv], axis=2).reshape(width, 2 * SHARE)
    bq = lax.dynamic_slice_in_dim(query_bias, start, SHARE, 0).astype(F32)[:, None]
    bv = lax.dynamic_slice_in_dim(value_bias, start, SHARE, 0).astype(F32).reshape(MINE, HEAD)
    bkv = jnp.concatenate([jnp.zeros_like(bv), bv], axis=1).reshape(1, 2 * SHARE)
    w_back = jnp.concatenate([wq_t, wkv.T], axis=0)
    n1, q, kv, kvt, o, lse, mixed_t = attend_call(
        cnt_seq, residual_in[0], norm1_gain.astype(F32)[None], norm1_bias.astype(F32)[None], wq_t, bq, wkv, bkv
    )
    hidden_in = residual_in[0].astype(F32)
    branch = dot(mixed_t, out_weight, TN) + out_bias.astype(F32)
    middle = hidden_in + active * branch
    normed_two, norm_two_back = jax.vjp(
        norm_affine, middle, norm2_gain.astype(F32), norm2_bias.astype(F32)
    )
    normed_two_low = normed_two.astype(BF)
    pre_act = dot(normed_two_low, up_weight, NN) + up_bias.astype(F32)
    activated, gelu_back = jax.vjp(jax.nn.gelu, pre_act)
    activated_low = activated.astype(BF)
    down_out = dot(activated_low, down_weight, NN) + down_bias.astype(F32)
    layer_out = (middle + active * down_out).astype(BF)[None]
    out_grad = cotangent[0].astype(F32)
    down_grad = (active * out_grad).astype(BF)
    down_weight_sum = dot(activated_low, down_grad, TN)
    down_bias_sum = jnp.sum(down_grad.astype(F32), axis=0)
    (pre_grad,) = gelu_back(dot(down_grad, down_weight, NT))
    pre_low = pre_grad.astype(BF)
    up_weight_sum = dot(normed_two_low, pre_low, TN)
    up_bias_sum = jnp.sum(pre_low.astype(F32), axis=0)
    middle_norm, gain_two_sum, shift_two_sum = norm_two_back(dot(pre_low, up_weight, NT))
    middle_grad = out_grad + middle_norm
    branch_grad = (active * middle_grad).astype(BF)
    out_weight_sum = dot(mixed_t, branch_grad, NN)
    out_bias_sum = jnp.sum(branch_grad.astype(F32), axis=0)
    da_t = dot(out_weight, branch_grad, NT).astype(BF)
    dn_parts, dw, sums = back_call(cnt_seq, da_t, n1, q, kv, kvt, o, lse, w_back)
    dn1 = jnp.sum(dn_parts.astype(F32), axis=1).reshape(2 * CAP, width)
    _, norm_one_back = jax.vjp(norm_rows, hidden_in)
    (input_norm,) = norm_one_back(dn1 * norm1_gain.astype(F32))
    input_grad = (middle_grad + input_norm)[None]

    small = jnp.concatenate(
        [up_bias_sum.reshape(-1, width), down_bias_sum[None], out_bias_sum[None],
         gain_two_sum[None], shift_two_sum[None]], axis=0)
    small = jnp.pad(small, ((0, 256 - small.shape[0]), (0, 0)))
    up_blocks = up_weight_sum.reshape(width, -1, width).transpose(1, 0, 2).reshape(-1, width)
    g = jnp.concatenate([down_weight_sum, up_blocks, out_weight_sum, small], axis=0).astype(BF)
    gq = jnp.concatenate(
        [dw, jnp.pad(sums, ((0, QROWS - 584), (0, width - 3 * SHARE)))], axis=0).astype(BF)
    f, fq = sum_call(g, gq)
    scale = 1.0 / total_active
    f = f.astype(F32) * scale
    fq = fq.astype(F32) * scale
    down_w = f[:hidden]
    up_w = f[hidden : 2 * hidden].reshape(-1, width, width).transpose(1, 0, 2).reshape(width, hidden)
    out_w = f[2 * hidden : 2 * hidden + width]
    rest = f[2 * hidden + width :]
    per = hidden // width
    up_b = rest[:per].reshape(hidden)
    down_b, out_b, gain2, shift2 = rest[per], rest[per + 1], rest[per + 2], rest[per + 3]
    query_t = fq[:, :SHARE].reshape(width, width)
    pair = fq[:, SHARE : 3 * SHARE].reshape(4, MINE, 2, HEAD, width)
    key_t = pair[:, :, 0].reshape(width, width)
    value_t = pair[:, :, 1].reshape(width, width)
    biases = fq[:, 3 * SHARE, : 3 * SHARE]
    query_b = biases[:, :SHARE].reshape(width)
    pair_b = biases[:, SHARE:].reshape(4, MINE, 2, HEAD)
    key_b, value_b = pair_b[:, :, 0].reshape(width), pair_b[:, :, 1].reshape(width)
    shift1 = (
        jnp.sum(query_weight.astype(F32) * query_b, axis=1)
        + jnp.sum(key_weight.astype(F32) * key_b, axis=1)
        + jnp.sum(value_weight.astype(F32) * value_b, axis=1)
    )
    query_w, key_w, value_w = query_t.T, key_t.T, value_t.T
    joint = (
        jnp.sum(query_weight.astype(F32) * query_w, axis=1)
        + jnp.sum(key_weight.astype(F32) * key_w, axis=1)
        + jnp.sum(value_weight.astype(F32) * value_w, axis=1)
    )
    gain1 = (joint - norm1_bias.astype(F32) * shift1) / norm1_gain.astype(F32)
    return (
        layer_out, input_grad, gain1, shift1, query_w, query_b, key_w, value_w, value_b,
        out_w, out_b, gain2, shift2, up_w, up_b, down_w, down_b,
    )


def solution(mesh):
    placed = (
        (P("batch", "band", None), P("batch", "band"), P("batch", None, None))
        + (P(),) * 15
        + (P("batch", "band", None),)
    )
    fast = mesh.shape["band"] == BANDS and mesh.shape["batch"] == 4
    return jax.shard_map(
        fast_device if fast else on_device,
        mesh=mesh,
        in_specs=placed,
        out_specs=(P("batch", "band", None),) * 2 + (P(),) * 15,
        check_vma=False,
    )
```

```python
import functools

import jax
import jax.numpy as jnp
from jax import lax
from jax.experimental import pallas as pl
from jax.experimental.pallas import tpu as pltpu
from jax.sharding import PartitionSpec as P

MESH = pl.DeviceIdType.MESH
VM = pltpu.VMEM
BF = jnp.bfloat16
F32 = jnp.float32
HEADS = 12
LAYER = 6
HEAD = 64
BANDS = 8
CAP = 256
HALF = 128
MINE = 3
SHARE = MINE * HEAD
NEG = -1e30


def place():
    band = lax.axis_index("band")
    return band, band // 4, (band // 2) % 2, band % 2


def device(y, x, core):
    return (y * 4 + x * 2 + core, lax.axis_index("batch"))


def push(src, dst, send, recv, target):
    return pltpu.make_async_remote_copy(
        src_ref=src, dst_ref=dst, send_sem=send, recv_sem=recv, device_id=target, device_id_type=MESH
    )


def greet_band():
    band, _, _, _ = place()
    barrier = pltpu.get_barrier_semaphore()
    for step in range(1, BANDS):
        other = (band + step) % BANDS
        pl.semaphore_signal(
            barrier, inc=1, device_id=(other, lax.axis_index("batch")), device_id_type=MESH
        )
    pl.semaphore_wait(barrier, BANDS - 1)


def dot(a, b, dims):
    return lax.dot_general(a, b, ((dims[0], dims[1]), ((), ())), preferred_element_type=F32)


NN = ((1,), (0,))
NT = ((1,), (1,))
TN = ((0,), (0,))


def counts_of(edges_ref, seq, band):
    after = edges_ref[0, seq, jnp.minimum(band + 1, BANDS - 1)]
    return jnp.where(band == BANDS - 1, CAP, after - edges_ref[0, seq, band])


def attend_kernel(
    edges_ref, vec_ref, h_ref, wq_hbm, wk_hbm, wv_hbm,
    o_ref, lse_ref, att_ref, wback_ref, n1_hbm, q_hbm, kv_hbm, kt_hbm,
    rows_ref, n1_ref, q_ref, kv_ref, kvt_ref, cols_ref, turned_ref,
    send, recv, out_send, out_recv, load, store,
):
    band, y, x, core = place()
    width = h_ref.shape[1]
    group = 2 * x + core
    wide = pl.ds(pl.multiple_of(x * 2 * SHARE + core * 128, 128), 256)
    loads = [
        pltpu.make_async_copy(ref.at[:, wide], cols_ref.at[k], load.at[k])
        for k, ref in enumerate((wq_hbm, wk_hbm, wv_hbm))
    ]
    for copy in loads:
        copy.start()
    greet_band()
    own = pl.ds(pl.multiple_of(y * CAP, CAP), CAP)
    half = pl.ds(pl.multiple_of(core * HALF, HALF), HALF)
    other_y, other_x, other_core = 1 - y, 1 - x, 1 - core
    sibling = device(y, x, other_core)
    copies = {}

    def go(name, src, dst, index, recv_index, target):
        copy = push(src, dst, send.at[index], recv.at[recv_index], target)
        copy.start()
        copies[name] = copy

    for k in range(2):
        from_rows = pl.ds(pl.multiple_of(other_y * CAP + k * HALF, HALF), HALF)
        go(("y", k), h_ref.at[from_rows], rows_ref.at[band, pl.ds(k * HALF, HALF)], 1 + k, 1 + core,
           device(other_y, x, k))
    for k in range(2):
        from_rows = pl.ds(pl.multiple_of(y * CAP + k * HALF, HALF), HALF)
        go(("x", k), h_ref.at[from_rows], rows_ref.at[band, pl.ds(k * HALF, HALF)], 3 + k, 3 + core,
           device(y, other_x, k))
    go("sib", h_ref.at[own], rows_ref.at[band], 0, 0, sibling)

    gain, shift = vec_ref[:, :width], vec_ref[:, width : 2 * width]
    for k, copy in enumerate(loads):
        copy.wait()
        turned_ref[k] = cols_ref[k].T
        for h in range(MINE):
            part = turned_ref[k, pl.ds(pl.multiple_of(core * HEAD + h * HEAD, HEAD), HEAD), :]
            at = h * HEAD if k == 0 else SHARE + h * 128 + (k - 1) * HEAD
            wback_ref[at : at + HEAD, :] = part
    row = lax.broadcasted_iota(jnp.int32, (3 * SHARE, width), 0)
    col = lax.broadcasted_iota(jnp.int32, (3 * SHARE, width), 1) - group * SHARE
    inner = row - SHARE
    from_value = jnp.where((inner >= 0) & (inner % 128 >= HEAD), inner // 128 * HEAD + inner % 128 - HEAD, -width)
    pick_q = jnp.where((row == col) & (row < SHARE), 1.0, 0.0).astype(BF)
    pick_v = jnp.where(from_value == col, 1.0, 0.0).astype(BF)

    def spread_row(k):
        return jnp.broadcast_to(vec_ref[:, k * width : (k + 1) * width], (8, width)).astype(BF)

    bias = (dot(pick_q, spread_row(2), NT) + dot(pick_v, spread_row(3), NT))[:, :1]

    def project(rows, which):
        wide_rows = rows.astype(F32)
        center = wide_rows - jnp.mean(wide_rows, axis=-1, keepdims=True)
        spread = jnp.mean(center * center, axis=-1, keepdims=True)
        n1 = (center * lax.rsqrt(spread + 1e-05) * gain + shift).astype(BF)
        at = pl.ds(pl.multiple_of(which * CAP, CAP), CAP)
        n1_ref[at, :] = n1
        all_t = dot(wback_ref[...], n1, NT) + bias
        qt = (all_t[:SHARE] * 0.125).astype(BF)
        kvt = all_t[SHARE:].astype(BF)
        for h in range(MINE):
            one = kvt[h * 128 : (h + 1) * 128]
            kvt_ref[h, :, at] = one
            kv_ref[h, at, :] = one.T
            q_ref[h, :HEAD, at] = qt[h * HEAD : (h + 1) * HEAD]
            q_ref[h, HEAD:, at] = jnp.zeros((HEAD, CAP), BF)

    def project_two(first_y, first_x):
        def one(k, carry):
            which = first_y * 4 + first_x * 2 + k
            project(rows_ref[which], which)
            return carry

        lax.fori_loop(0, 2, one, 0)

    rows_ref[band] = h_ref[own, :]

    def wait_recv(index, which, size=HALF):
        ref = rows_ref.at[which] if size == CAP else rows_ref.at[which, half]
        push(ref, ref, send.at[0], recv.at[index], sibling).wait_recv()

    wait_recv(0, y * 4 + x * 2 + other_core, CAP)
    project_two(y, x)
    for k in range(2):
        from_band = other_y * 4 + x * 2 + k
        wait_recv(1 + k, from_band)
        piece = rows_ref.at[from_band, half]
        go(("fx", k), piece, piece, 5 + k, 5 + k, device(y, other_x, core))
        go(("fs", k), piece, piece, 7 + k, 7 + k, sibling)
    for k in range(2):
        from_band = y * 4 + other_x * 2 + k
        wait_recv(3 + k, from_band)
        piece = rows_ref.at[from_band, half]
        go(("fs", 2 + k), piece, piece, 9 + k, 9 + k, sibling)
    for k in range(2):
        copies[("fs", k)].wait_recv()
    project_two(other_y, x)
    for k in range(2):
        copies[("fs", 2 + k)].wait_recv()
    project_two(y, other_x)
    for k in range(2):
        from_band = other_y * 4 + other_x * 2 + k
        copies[("fx", k)].wait_recv()
        piece = rows_ref.at[from_band, half]
        go(("fs", 4 + k), piece, piece, 11 + k, 11 + k, sibling)
    for k in range(2):
        copies[("fs", 4 + k)].wait_recv()
    project_two(other_y, other_x)
    stores = [
        pltpu.make_async_copy(src, dst, store.at[k])
        for k, (src, dst) in enumerate(
            ((n1_ref, n1_hbm), (q_ref, q_hbm), (kv_ref, kv_hbm), (kvt_ref.at[:, :HEAD], kt_hbm))
        )
    ]
    for copy in stores:
        copy.start()

    key_at = lax.broadcasted_iota(jnp.int32, (CAP, CAP), 0)
    query_at = lax.broadcasted_iota(jnp.int32, (CAP, CAP), 1)
    lane = lax.broadcasted_iota(jnp.int32, (1, CAP), 1)
    share = pl.ds(pl.multiple_of(group * SHARE, SHARE), SHARE)
    side = pl.ds(pl.multiple_of(y * CAP, CAP), CAP)
    for i in range(BANDS - 1, -1, -1):
        cols = pl.ds(i * CAP, CAP)

        def one_head(h, carry):
            qt = q_ref[h, :, cols]
            scores = []
            for j in range(i + 1):
                s = dot(kv_ref[h, j * CAP : (j + 1) * CAP, :], qt, NN)
                keep = key_at < counts_of(edges_ref, y, j)
                if i == j:
                    keep = keep & (key_at <= query_at)
                scores.append(jnp.where(keep, s, NEG))
            top = functools.reduce(jnp.maximum, [jnp.max(s, axis=0, keepdims=True) for s in scores])
            total = jnp.zeros((1, CAP), F32)
            mix = jnp.zeros((HEAD, CAP), F32)
            for j in range(i + 1):
                p = jnp.exp(scores[j] - top)
                total = total + jnp.sum(p, axis=0, keepdims=True)
                mix = mix + dot(kvt_ref[h, HEAD:, j * CAP : (j + 1) * CAP], p.astype(BF), NN)
            valid = lane < counts_of(edges_ref, y, i)
            mix = jnp.where(valid, mix / total, kvt_ref[h, HEAD:, cols].astype(F32))
            o_ref[i, pl.ds(pl.multiple_of(h * HEAD, HEAD), HEAD), :] = mix.astype(BF)
            lse_ref[h, i : i + 1, :] = jnp.where(valid, top + jnp.log(total), -NEG)
            return carry

        lax.fori_loop(0, MINE, one_head, 0)
        copy = push(o_ref.at[i], att_ref.at[share, side], out_send.at[i], out_recv.at[band],
                    (i, lax.axis_index("batch")))
        pl.when(band != i)(copy.start)
        local = pltpu.make_async_copy(o_ref.at[i], att_ref.at[share, side], out_recv.at[band])
        pl.when(band == i)(local.start)
    for i in range(BANDS):
        from_y, from_x, from_core = i // 4, (i // 2) % 2, i % 2
        ref = att_ref.at[pl.ds((2 * from_x + from_core) * SHARE, SHARE), pl.ds(from_y * CAP, CAP)]
        copy = push(o_ref.at[i], ref, out_send.at[i], out_recv.at[i], sibling)
        copy.wait_recv()
        pl.when(band != i)(copy.wait_send)
    for copy in copies.values():
        copy.wait_send()
    for copy in stores:
        copy.wait()


def attend_call(edges, vec, h, wq, wk, wv):
    width = h.shape[1]
    seq = BANDS * CAP
    vm = pl.BlockSpec(memory_space=VM)
    hbm = pl.BlockSpec(memory_space=pl.ANY)
    return pl.pallas_call(
        attend_kernel,
        name="attend",
        out_shape=[
            jax.ShapeDtypeStruct((BANDS, SHARE, CAP), BF),
            jax.ShapeDtypeStruct((MINE, BANDS, CAP), F32),
            jax.ShapeDtypeStruct((width, 2 * CAP), BF),
            jax.ShapeDtypeStruct((3 * SHARE, width), BF),
            jax.ShapeDtypeStruct((seq, width), BF),
            jax.ShapeDtypeStruct((MINE, 128, seq), BF),
            jax.ShapeDtypeStruct((MINE, seq, 128), BF),
            jax.ShapeDtypeStruct((MINE, HEAD, seq), BF),
        ],
        in_specs=[pl.BlockSpec(memory_space=pltpu.SMEM)] + [vm] * 2 + [hbm] * 3,
        out_specs=[vm] * 4 + [hbm] * 4,
        scratch_shapes=[
            VM((BANDS, CAP, width), BF),
            VM((seq, width), BF),
            VM((MINE, 128, seq), BF),
            VM((MINE, seq, 128), BF),
            VM((MINE, 128, seq), BF),
            VM((3, width, 256), BF),
            VM((3, 256, width), BF),
            pltpu.SemaphoreType.DMA((13,)),
            pltpu.SemaphoreType.DMA((13,)),
            pltpu.SemaphoreType.DMA((BANDS,)),
            pltpu.SemaphoreType.DMA((BANDS,)),
            pltpu.SemaphoreType.DMA((3,)),
            pltpu.SemaphoreType.DMA((4,)),
        ],
        compiler_params=pltpu.CompilerParams(
            collective_id=0, has_side_effects=True, vmem_limit_bytes=56 * 2**20
        ),
    )(edges, vec, h, wq, wk, wv)


BLOCK = 512
BLOCKS = 6
QROWS = 640
ORDERS = (
    (("x", "y", "a", "b"), ("y", "x", "a", "b")),
    (("x", "y", "a", "b"), ("a", "y", "x", "b")),
    (("a", "x", "y", "b"), ("y", "x", "a", "b")),
    (("x", "y", "a", "b"), ("y", "x", "a", "b")),
    (("x", "y", "a", "b"), ("a", "y", "x", "b")),
    (("a", "x", "y", "b"), ("y", "x", "a", "b")),
    (("x", "y", "a", "b"), ("y", "x", "a", "b")),
)
LAST = 11
MLP_TICKS = 1
BACK_TICKS = (1, 1, 1, 1, 1, 1, 1, 1)


def partners():
    band, y, x, core = place()
    z = lax.axis_index("batch")
    return {
        "core": (core, device(y, x, 1 - core)),
        "x": (x, device(y, 1 - x, core)),
        "y": (y, device(1 - y, x, core)),
        "a": (z % 2, (band, z + 1 - 2 * (z % 2))),
        "b": (z // 2, (band, (z + 2) % 4)),
    }


class Chain:
    def __init__(self, total, landing, send, recv, free, index, order, out, out_sem):
        self.total, self.landing, self.send, self.recv, self.free = total, landing, send, recv, free
        self.index, self.order, self.out, self.out_sem = index, order, out, out_sem
        self.links = partners()
        self.core = self.links["core"][0]
        rows = total.shape[2]
        self.keep, self.give = [], []
        start = 0
        for axis in order:
            rows //= 2
            bit = self.links[axis][0]
            self.keep.append((start + bit * rows, rows))
            self.give.append((start + (1 - bit) * rows, rows))
            start = start + bit * rows

    def piece(self, span):
        return self.total.at[self.index, self.core, pl.ds(pl.multiple_of(span[0], 16), span[1])]

    def copy(self, slot):
        target = self.links["core" if slot in (0, 9) else self.order[slot - 1 if slot < 5 else 8 - slot]][1]
        send, recv = self.send.at[self.index, slot], self.recv.at[self.index, slot]
        if slot == 0:
            return push(self.total.at[self.index, 1 - self.core], self.landing[0].at[self.index], send, recv, target)
        if slot < 5:
            return push(self.piece(self.give[slot - 1]), self.landing[slot].at[self.index], send, recv, target)
        if slot < 9:
            piece = self.piece(self.keep[8 - slot])
        else:
            piece = self.total.at[self.index, self.core]
        return push(piece, piece, send, recv, target)

    def arrival(self, slot):
        if slot < 5:
            return self.copy(slot)
        if slot < 9:
            piece = self.piece(self.give[8 - slot])
        else:
            piece = self.total.at[self.index, 1 - self.core]
        send, recv = self.send.at[self.index, slot], self.recv.at[self.index, slot]
        return push(piece, piece, send, recv, self.links["core"][1])

    def add(self, slot):
        if slot == 0:
            start, rows = 0, self.total.shape[2]
        else:
            start, rows = self.keep[slot - 1]
        landing, total, index, core = self.landing[slot], self.total, self.index, self.core

        def some(r, carry):
            here = pl.ds(pl.multiple_of(start + r * 16, 16), 16)
            there = pl.ds(pl.multiple_of(r * 16, 16), 16)
            total[index, core, here] = (
                total[index, core, here].astype(F32) + landing[index, there].astype(F32)
            ).astype(BF)
            return carry

        lax.fori_loop(0, rows // 16, some, 0, unroll=min(2, rows // 16))

    def store(self):
        return pltpu.make_async_copy(self.total.at[self.index], self.out.at[self.index], self.out_sem.at[self.index])

    def stage(self, stage):
        if stage > 0:
            self.arrival(stage - 1).wait_recv()
            if stage <= 5:
                self.copy(stage - 1).wait_send()
                axis = "core" if stage == 1 else self.order[stage - 2]
                pl.semaphore_signal(
                    self.free.at[self.index, stage - 1], inc=1, device_id=self.links[axis][1], device_id_type=MESH
                )
                self.add(stage - 1)
        if stage < 10:
            if stage >= 5:
                pl.semaphore_wait(self.free.at[self.index, 9 - stage], 1)
            self.copy(stage).start()
        else:
            self.store().start()

    def drain(self):
        for slot in range(5, 10):
            self.copy(slot).wait_send()
        self.store().wait()


def layer_kernel(
    edges_ref, exit_ref, vec_ref, h_ref, cot_ref, att_ref, o_ref, lse_ref, wback_ref, wout_ref,
    n1_hbm, q_hbm, kv_hbm, kt_hbm, wup_hbm, wdown_hbm,
    layer_ref, dmid_ref, dn_ref, fq_ref, fd_hbm, fu_hbm,
    gd_ref, gu_ref, d0, d1, d2, d3, d4, u0, u1, u2, u3, u4, q1, q2, q3,
    q_ref, kv_ref, kt_ref, dz_ref, da_ref, do_ref, sib_out, sib_in, row_out,
    d_send, d_recv, u_send, u_recv, d_out, u_out, q_send, q_recv, d_free, u_free, q_free,
    do_send, do_recv, sib_send, sib_recv, dn_send, dn_recv, load, wload,
):
    band, y, x, core = place()
    batch = lax.axis_index("batch")
    links = partners()
    sibling = links["core"][1]
    width = h_ref.shape[1]
    loads = [
        pltpu.make_async_copy(q_hbm, q_ref, load.at[0]),
        pltpu.make_async_copy(kv_hbm, kv_ref, load.at[1]),
        pltpu.make_async_copy(kt_hbm, kt_ref, load.at[2]),
    ]
    barrier = pltpu.get_barrier_semaphore()
    for step in range(1, BANDS):
        pl.semaphore_signal(barrier, inc=1, device_id=((band + step) % BANDS, batch), device_id_type=MESH)
    for axis in ("a", "b"):
        pl.semaphore_signal(barrier, inc=1, device_id=links[axis][1], device_id_type=MESH)

    chunks = []
    for index in range(BLOCKS + 1):
        order = ORDERS[index]
        first = Chain(gd_ref, (d0, d1, d2, d3, d4), d_send, d_recv, d_free, index, order[0], fd_hbm, d_out)
        if index < BLOCKS:
            other = Chain(gu_ref, (u0, u1, u2, u3, u4), u_send, u_recv, u_free, index, order[1], fu_hbm, u_out)
        else:
            other = Chain(gd_ref, (d0, d1, d2, d3, d4), d_send, d_recv, d_free, index + 1, order[1], fd_hbm, d_out)
        chunks.append((first, other))
    progress = {}

    def tick(ready):
        for index in range(ready):
            at = progress.get(index, 0)
            if at < LAST:
                for chain in chunks[index]:
                    chain.stage(at)
                progress[index] = at + 1

    def vec(k, size=1):
        return vec_ref[:, k * width : (k + size) * width]

    lane = lax.broadcasted_iota(jnp.int32, (1, 2 * CAP), 1)
    limit = jnp.where(lane < CAP, counts_of(edges_ref, 0, band), counts_of(edges_ref, 1, band) + CAP)
    active_row = jnp.where((exit_ref[...] >= LAYER) & (lane < limit), 1.0, 0.0)
    active = jnp.broadcast_to(active_row, (8, 2 * CAP)).T[:, :1]

    def feed_forward(mid_ref, sum_ref, dn2_ref, n2_ref, n2t_ref, wu, wd, pre_ref, dact_ref, act_ref, dpre_ref, ub_ref, row_ref):
        def weights(f):
            at = pl.ds(f * BLOCK, BLOCK)
            return (
                pltpu.make_async_copy(wup_hbm.at[:, at], wu.at[f % 2], wload.at[0, f % 2]),
                pltpu.make_async_copy(wdown_hbm.at[at], wd.at[f % 2], wload.at[1, f % 2]),
            )

        for copy in weights(0):
            copy.start()
        for copy in loads:
            copy.start()
        branch = dot(att_ref[...], wout_ref[...], TN) + vec(4)
        middle = h_ref[...].astype(F32) + active * branch
        mid_ref[...] = middle
        center = middle - jnp.mean(middle, axis=-1, keepdims=True)
        spread = jnp.mean(center * center, axis=-1, keepdims=True)
        scale2 = lax.rsqrt(spread + 1e-05)
        n2 = (center * scale2 * vec(5) + vec(6)).astype(BF)
        n2_ref[...] = n2
        n2t_ref[...] = n2.T
        dz_ref[...] = (active * cot_ref[...].astype(F32)).astype(BF)
        row_ref[...] = jnp.zeros_like(row_ref)
        sum_ref[...] = jnp.zeros_like(sum_ref)
        dn2_ref[...] = jnp.zeros_like(dn2_ref)
        for f in range(BLOCKS):
            if f + 1 < BLOCKS:
                for copy in weights(f + 1):
                    copy.start()
            for copy in weights(f):
                copy.wait()
            slot = f % 2
            pre_ref[...] = dot(n2_ref[...], wu[slot], NN)
            dact_ref[...] = dot(dz_ref[...], wd[slot], NT)
            up_bias = vec_ref[:, 8 * width + f * BLOCK : 8 * width + (f + 1) * BLOCK]
            ub_ref[...] = jnp.zeros_like(ub_ref)

            def rows(r, carry):
                at = pl.ds(pl.multiple_of(r * 64, 64), 64)
                pre = pre_ref[at, :] + up_bias
                square = pre * pre
                t = jnp.tanh(0.7978845608028654 * pre * (1.0 + 0.044715 * square))
                half = 0.5 * (1.0 + t)
                slope = half + (0.5 * 0.7978845608028654) * pre * (1.0 - t * t) * (1.0 + 0.134145 * square)
                act_ref[at, :] = (pre * half).astype(BF)
                dpre = (dact_ref[at, :] * slope).astype(BF)
                dpre_ref[at, :] = dpre
                ub_ref[...] += jnp.sum(dpre.astype(F32).reshape(8, 8, BLOCK), axis=0)
                return carry

            lax.fori_loop(0, 2 * CAP // 64, rows, 0)
            down = dot(act_ref[...], dz_ref[...], TN).astype(BF)
            gd_ref[f, 0] = down[: BLOCK // 2]
            gd_ref[f, 1] = down[BLOCK // 2 :]
            up = dot(n2t_ref[...], dpre_ref[...], NN).astype(BF)
            gu_ref[f, 0] = up[:, : BLOCK // 2]
            gu_ref[f, 1] = up[:, BLOCK // 2 :]
            row_ref[f : f + 1, :BLOCK] = jnp.sum(ub_ref[...], axis=0, keepdims=True)
            if f == 0:
                pl.semaphore_wait(barrier, BANDS + 1)
            tick(f + 1)
            sum_ref[...] += dot(act_ref[...], wd[slot], NN)
            dn2_ref[...] += dot(dpre_ref[...], wu[slot], NT)
        middle = mid_ref[...]
        layer_ref[...] = (middle + active * (sum_ref[...] + vec(7))).astype(BF)
        center = middle - jnp.mean(middle, axis=-1, keepdims=True)
        spread = jnp.mean(center * center, axis=-1, keepdims=True)
        scale2 = lax.rsqrt(spread + 1e-05)
        xhat = center * scale2
        dn2 = dn2_ref[...]
        e2 = dn2 * vec(5)
        cot = cot_ref[...].astype(F32)
        dmid = cot + scale2 * (
            e2 - jnp.mean(e2, axis=-1, keepdims=True) - xhat * jnp.mean(e2 * xhat, axis=-1, keepdims=True)
        )
        dmid_ref[...] = dmid
        da = (active * dmid).astype(BF)
        n2_ref[...] = da
        da_ref[...] = dot(wout_ref[...], da, NT).astype(BF)
        for i in range(BANDS):
            copy = push(part_for(i), do_ref.at[band], do_send.at[i], do_recv.at[band], (i, batch))
            pl.when(band != i)(copy.start)
            local = pltpu.make_async_copy(part_for(i), do_ref.at[band], do_recv.at[band])
            pl.when(band == i)(local.start)
        out = dot(att_ref[...], n2_ref[...], NN).astype(BF)
        gd_ref[BLOCKS, 0] = out[:256]
        gd_ref[BLOCKS, 1] = out[256:512]
        gd_ref[BLOCKS + 1, 0] = out[512:]
        count = jnp.sum(active_row)
        big = jnp.floor(count * (1.0 / 64.0))
        mid = jnp.floor((count - 64.0 * big) * 0.125)
        small = count - 64.0 * big - 8.0 * mid
        at = lax.broadcasted_iota(jnp.int32, (1, width), 1)
        digits = jnp.where(at == 0, big, jnp.where(at == 1, mid, jnp.where(at == 2, small, 0.0)))

        def total(v):
            return jnp.sum(v, axis=0, keepdims=True)

        sums = [
            total(dz_ref[...].astype(F32)), total(da.astype(F32)), total(dn2 * xhat), total(dn2), digits,
        ]
        for k, row in enumerate(sums):
            row_ref[8 + k : 9 + k, :] = row
        gd_ref[BLOCKS + 1, 1, :16, :] = row_ref[...].astype(BF)

    def part_for(i):
        to_y, to_x, to_core = i // 4, (i // 2) % 2, i % 2
        return da_ref.at[pl.ds((2 * to_x + to_core) * SHARE, SHARE), pl.ds(to_y * CAP, CAP)]

    gd_ref[BLOCKS + 1, 1] = jnp.zeros(gd_ref.shape[2:], BF)
    rows2 = 2 * CAP
    pl.run_scoped(
        feed_forward,
        VM((rows2, width), F32), VM((rows2, width), F32), VM((rows2, width), F32),
        VM((rows2, width), BF), VM((width, rows2), BF),
        VM((2, width, BLOCK), BF), VM((2, BLOCK, width), BF),
        VM((rows2, BLOCK), F32), VM((rows2, BLOCK), F32), VM((rows2, BLOCK), BF), VM((rows2, BLOCK), BF),
        VM((8, BLOCK), F32), VM((16, width), F32),
    )
    tick(BLOCKS + 1)

    half = pl.ds(pl.multiple_of(core * HALF, HALF), HALF)
    key_at = lax.broadcasted_iota(jnp.int32, (CAP, CAP), 0)
    query_at = lax.broadcasted_iota(jnp.int32, (CAP, CAP), 1)

    def sib_copy(i):
        return push(sib_out.at[i % 2], sib_in.at[i], sib_send.at[i], sib_recv.at[i], sibling)

    def dn_copy(i):
        return push(row_out.at[i % 2], dn_ref.at[y, x, half], dn_send.at[i], dn_recv.at[band], (i, batch))

    def dn_local(i):
        return pltpu.make_async_copy(row_out.at[i % 2], dn_ref.at[y, x, half], dn_recv.at[band])

    def backward(dk_ref, d_ref, mine_ref, n1_ref, small_ref):
        rows_load = pltpu.make_async_copy(n1_hbm, n1_ref, load.at[3])
        rows_load.start()

        def finish(i):
            sib_copy(i).wait_recv()
            if i + 2 < BANDS:
                pl.when(band != i + 2)(dn_copy(i + 2).wait_send)

                @pl.when(band == i + 2)
                def _():
                    push(row_out.at[0], dn_ref.at[y, x, half], dn_send.at[0], dn_recv.at[band], sibling).wait_recv()

            row_out[i % 2] = (mine_ref[i % 2] + sib_in[i].astype(F32)).astype(BF)
            pl.when(band != i)(dn_copy(i).start)
            pl.when(band == i)(dn_local(i).start)

        dk_ref[...] = jnp.zeros_like(dk_ref)
        small_ref[...] = jnp.zeros_like(small_ref)
        for copy in loads:
            copy.wait()
        for i in range(BANDS - 1, -1, -1):
            cols = pl.ds(i * CAP, CAP)
            push(do_ref.at[i], do_ref.at[i], do_send.at[i], do_recv.at[i], sibling).wait_recv()

            def one_head(h, carry):
                qt = q_ref[h, :, cols]
                dot_t = do_ref[i, pl.ds(pl.multiple_of(h * HEAD, HEAD), HEAD), :]
                dop = jnp.concatenate([jnp.zeros_like(dot_t), dot_t], axis=0)
                lse = lse_ref[h, i : i + 1, :]
                o = o_ref[i, pl.ds(pl.multiple_of(h * HEAD, HEAD), HEAD), :]
                delta = jnp.sum(dot_t.astype(F32) * o.astype(F32), axis=0, keepdims=True)
                dq = jnp.zeros((HEAD, CAP), F32)
                for j in range(i + 1):
                    at = pl.ds(j * CAP, CAP)
                    kv = kv_ref[h, at, :]
                    s = dot(kv, qt, NN)
                    dp = dot(kv, dop, NN)
                    keep = key_at < counts_of(edges_ref, y, j)
                    if i == j:
                        keep = keep & (key_at <= query_at)
                    p = jnp.where(keep, jnp.exp(s - lse), 0.0)
                    if i == j:
                        alone = (key_at == query_at) & (query_at >= counts_of(edges_ref, y, i))
                        p = jnp.where(alone, 1.0, p)
                    ds = (p * (dp - delta)).astype(BF)
                    dq = dq + dot(kt_ref[h, :, at], ds, NN)
                    dk_ref[h, at, :] += dot(ds, qt, NT) + dot(p.astype(BF), dop, NT)
                d_ref[pl.ds(pl.multiple_of(h * HEAD, HEAD), HEAD), cols] = (dq * 0.125).astype(BF)
                d_ref[pl.ds(pl.multiple_of(SHARE + h * 128, HEAD), 128), cols] = dk_ref[h, cols, :].T.astype(BF)
                return carry

            lax.fori_loop(0, MINE, one_head, 0)
            if i == BANDS - 1:
                rows_load.wait()
            dn = dot(d_ref[:, cols], wback_ref[...], TN)
            centered = n1_ref[cols, :].astype(F32) - vec(1)
            small_ref[0:1, :] += jnp.sum(dn, axis=0, keepdims=True)
            small_ref[1:2, :] += jnp.sum(dn * centered, axis=0, keepdims=True)
            mine_ref[2] = dn[:HALF]
            mine_ref[3] = dn[HALF:]
            if i + 2 < BANDS:
                sib_copy(i + 2).wait_send()
            sib_out[i % 2] = mine_ref[2 + (1 - core)].astype(BF)
            mine_ref[i % 2] = mine_ref[2 + core]
            sib_copy(i).start()
            if i < BANDS - 1:
                finish(i + 1)
            for _ in range(BACK_TICKS[BANDS - 1 - i]):
                tick(BLOCKS + 1)
        fq_ref[x, core, : 3 * SHARE] = dot(d_ref[...], n1_ref[...], NN).astype(BF)
        sums = dot(jnp.ones((8, d_ref.shape[1]), BF), d_ref[...], NT)[:1]
        small_ref[2:3, : 3 * SHARE] = sums
        fq_ref[x, core, 3 * SHARE :] = jnp.zeros((QROWS - 3 * SHARE, width), BF)
        fq_ref[x, core, 3 * SHARE : 3 * SHARE + 16] = jnp.concatenate(
            [small_ref[...], jnp.zeros((8, width), F32)], axis=0
        ).astype(BF)
        finish(0)

    pl.run_scoped(
        backward,
        VM((MINE, BANDS * CAP, 128), F32),
        VM((3 * SHARE, BANDS * CAP), BF),
        VM((4, HALF, width), F32),
        VM((BANDS * CAP, width), BF),
        VM((8, width), F32),
    )

    z_low, z_high = links["a"][0], links["b"][0]
    half1, half2, half3 = QROWS // 2, QROWS // 4, QROWS // 8
    starts = (
        (y * half1, (1 - y) * half1),
        (y * half1 + z_low * half2, y * half1 + (1 - z_low) * half2),
        (
            y * half1 + z_low * half2 + z_high * half3,
            y * half1 + z_low * half2 + (1 - z_high) * half3,
        ),
    )
    sizes, landing, axes = (half1, half2, half3), (q1, q2, q3), ("y", "a", "b")

    def rows_at(start, size):
        return fq_ref.at[x, core, pl.ds(pl.multiple_of(start, 16), size)]

    def q_copy(slot, arrival=False):
        send, recv = q_send.at[slot], q_recv.at[slot]
        if slot < 3:
            return push(rows_at(starts[slot][1], sizes[slot]), landing[slot], send, recv, links[axes[slot]][1])
        if slot < 6:
            level = 5 - slot
            piece = rows_at(starts[level][1 if arrival else 0], sizes[level])
            return push(piece, piece, send, recv, links[axes[level]][1])
        if slot == 6:
            piece = fq_ref.at[1 - x if arrival else x, core]
            return push(piece, piece, send, recv, links["x"][1])
        piece = fq_ref.at[:, 1 - core if arrival else core]
        return push(piece, piece, send, recv, sibling)

    def q_stage(stage):
        if stage > 0:
            q_copy(stage - 1, True).wait_recv()
            if stage <= 3:
                q_copy(stage - 1).wait_send()
                pl.semaphore_signal(
                    q_free.at[stage - 1], inc=1, device_id=links[axes[stage - 1]][1], device_id_type=MESH
                )
                start, size, land = starts[stage - 1][0], sizes[stage - 1], landing[stage - 1]

                def some(r, carry):
                    here = pl.ds(pl.multiple_of(start + r * 16, 16), 16)
                    there = pl.ds(pl.multiple_of(r * 16, 16), 16)
                    fq_ref[x, core, here] = (
                        fq_ref[x, core, here].astype(F32) + land[there].astype(F32)
                    ).astype(BF)
                    return carry

                lax.fori_loop(0, size // 16, some, 0)
        if stage < 8:
            if 3 <= stage < 6:
                pl.semaphore_wait(q_free.at[5 - stage], 1)
            q_copy(stage).start()

    q_next = 0
    while q_next < 9 or min(progress[k] for k in range(BLOCKS + 1)) < LAST:
        tick(BLOCKS + 1)
        if q_next < 9:
            q_stage(q_next)
            q_next += 1

    for i in range(BANDS):
        copy = push(part_for(i), do_ref.at[i], do_send.at[i], do_recv.at[i], sibling)
        pl.when(band != i)(copy.wait_send)
        if i < 2:
            sib_copy(i).wait_send()
            pl.when(band != i)(dn_copy(i).wait_send)
    for i in range(BANDS):
        from_y, from_x, from_core = i // 4, i // 2 % 2, i % 2
        arrived = push(row_out.at[0], dn_ref.at[from_y, from_x, pl.ds(from_core * HALF, HALF)],
                       dn_send.at[i], dn_recv.at[i], sibling)
        if i < 2:
            arrived.wait_recv()
        else:
            pl.when(band != i)(arrived.wait_recv)
    for first, other in chunks:
        first.drain()
        other.drain()
    for slot in range(3, 8):
        q_copy(slot).wait_send()


def layer_call(edges, exits, vec, h, cot, att, o, lse, wback, wout, n1, q, kv, kt, wup, wdown):
    width = h.shape[1]
    seq = BANDS * CAP
    vm = pl.BlockSpec(memory_space=VM)
    hbm = pl.BlockSpec(memory_space=pl.ANY)
    dma = pltpu.SemaphoreType.DMA
    eight = dma((BANDS,))
    credit = pltpu.SemaphoreType.REGULAR

    def room(*shape):
        return VM(shape, BF)

    def spots(rows, lanes, number):
        return [room(number, rows // 2**k, lanes) for k in range(5)]

    parts_d, parts_u = BLOCKS + 2, BLOCKS
    return pl.pallas_call(
        layer_kernel,
        name="layer",
        out_shape=[
            jax.ShapeDtypeStruct(h.shape, BF),
            jax.ShapeDtypeStruct(h.shape, F32),
            jax.ShapeDtypeStruct((2, 2, CAP, width), BF),
            jax.ShapeDtypeStruct((2, 2, QROWS, width), BF),
            jax.ShapeDtypeStruct((parts_d, 2, 256, width), BF),
            jax.ShapeDtypeStruct((parts_u, 2, width, 256), BF),
        ],
        in_specs=[pl.BlockSpec(memory_space=pltpu.SMEM)] + [vm] * 9 + [hbm] * 6,
        out_specs=[vm] * 4 + [hbm] * 2,
        scratch_shapes=[room(parts_d, 2, 256, width), room(parts_u, 2, width, 256)]
        + spots(256, width, parts_d)
        + spots(width, 256, parts_u)
        + [room(QROWS // 2, width), room(QROWS // 4, width), room(QROWS // 8, width)]
        + [
            room(MINE, 128, seq), room(MINE, seq, 128), room(MINE, HEAD, seq),
            room(2 * CAP, width), room(width, 2 * CAP), room(BANDS, SHARE, CAP),
            room(2, HALF, width), room(BANDS, HALF, width), room(2, HALF, width),
        ]
        + [dma((parts_d, 10))] * 2 + [dma((parts_u, 10))] * 2 + [dma((parts_d,)), dma((parts_u,))]
        + [eight] * 2
        + [credit((parts_d, 5)), credit((parts_u, 5)), credit((3,))]
        + [eight] * 6 + [dma((4,)), dma((2, 2))],
        compiler_params=pltpu.CompilerParams(
            collective_id=1, has_side_effects=True, vmem_limit_bytes=63 * 2**20
        ),
    )(edges, exits, vec, h, cot, att, o, lse, wback, wout, n1, q, kv, kt, wup, wdown)


SLOTS_IN = 4


def finish_kernel(
    vec_ref, h_ref, dmid_ref, dn_ref, fd_hbm, fu_hbm, fq_hbm,
    grad_ref, small_out, qw_hbm, kw_hbm, vw_hbm, ow_hbm, uw_hbm, dw_hbm,
    in_d, in_u, out_d, out_u, fq_ref, square, tail, load_d, load_u, store_d, store_u, load_q, store_q,
):
    width = h_ref.shape[1]
    tail_load = pltpu.make_async_copy(fd_hbm.at[BLOCKS + 1, 1], tail, load_q.at[1])
    tail_load.start()
    q_load = pltpu.make_async_copy(fq_hbm, fq_ref, load_q.at[0])
    pieces_d, pieces_u = [], []
    for f in range(BLOCKS + 2):
        for c in range(2):
            row = f * 512 + c * 256
            if f < BLOCKS:
                pieces_d.append((fd_hbm.at[f, c], dw_hbm.at[pl.ds(row, 256)]))
            elif row - BLOCKS * 512 < width:
                pieces_d.append((fd_hbm.at[f, c], ow_hbm.at[pl.ds(row - BLOCKS * 512, 256)]))
            if f < BLOCKS:
                pieces_u.append((fu_hbm.at[f, c], uw_hbm.at[:, pl.ds(row, 256)]))

    def run(pieces, buf_in, buf_out, load, store, scale, middle=None):
        def load_of(k):
            return pltpu.make_async_copy(pieces[k][0], buf_in.at[k % SLOTS_IN], load.at[k % SLOTS_IN])

        def store_of(k):
            return pltpu.make_async_copy(buf_out.at[k % SLOTS_IN], pieces[k][1], store.at[k % SLOTS_IN])

        return load_of, store_of

    d_load, d_store = run(pieces_d, in_d, out_d, load_d, store_d, None)
    u_load, u_store = run(pieces_u, in_u, out_u, load_u, store_u, None)
    for k in range(SLOTS_IN):
        d_load(k).start()
        u_load(k).start()
    q_load.start()
    tail_load.wait()
    count = tail[8 + 4 : 8 + 5, :3].astype(F32)
    total = 64.0 * count[:, 0:1] + 8.0 * count[:, 1:2] + count[:, 2:3]
    scale = 1.0 / total

    def convert(k, pieces, load_of, store_of, buf_in, buf_out):
        load_of(k).wait()
        if k >= SLOTS_IN:
            store_of(k - SLOTS_IN).wait()
        slot = k % SLOTS_IN
        rows = buf_in.shape[1]

        def some(r, carry):
            at = pl.ds(pl.multiple_of(r * 32, 32), 32)
            buf_out[slot, at, :] = buf_in[slot, at, :].astype(F32) * scale
            return carry

        lax.fori_loop(0, rows // 32, some, 0)
        store_of(k).start()
        if k + SLOTS_IN < len(pieces):
            load_of(k + SLOTS_IN).start()

    for k in range(max(len(pieces_d), len(pieces_u))):
        if k < len(pieces_d):
            convert(k, pieces_d, d_load, d_store, in_d, out_d)
        if k < len(pieces_u):
            convert(k, pieces_u, u_load, u_store, in_u, out_u)
    q_load.wait()
    outs = (qw_hbm, kw_hbm, vw_hbm)
    stores = []
    for which in range(3):
        for g in range(4):
            for h in range(MINE):
                at = h * HEAD if which == 0 else SHARE + h * 128 + (which - 1) * HEAD
                square[which, :, g * SHARE + h * HEAD : g * SHARE + (h + 1) * HEAD] = (
                    fq_ref[g // 2, g % 2, at : at + HEAD, :].astype(F32) * scale
                ).T
        copy = pltpu.make_async_copy(square.at[which], outs[which], store_q.at[which])
        copy.start()
        stores.append(copy)

    hidden = h_ref[...].astype(F32)
    center = hidden - jnp.mean(hidden, axis=-1, keepdims=True)
    spread = jnp.mean(center * center, axis=-1, keepdims=True)
    scale1 = lax.rsqrt(spread + 1e-05)
    xhat = center * scale1
    dn1 = jnp.concatenate([dn_ref[s, 0].astype(F32) + dn_ref[s, 1].astype(F32) for s in range(2)], axis=0)
    gain = vec_ref[:, :width]
    e1 = dn1 * gain
    grad_ref[...] = dmid_ref[...] + scale1 * (
        e1 - jnp.mean(e1, axis=-1, keepdims=True) - xhat * jnp.mean(e1 * xhat, axis=-1, keepdims=True)
    )

    row = lax.broadcasted_iota(jnp.int32, (3 * SHARE, width), 0)
    col = lax.broadcasted_iota(jnp.int32, (3 * SHARE, width), 1)
    inner = row - SHARE
    from_value = jnp.where((inner >= 0) & (inner % 128 >= HEAD), inner // 128 * HEAD + inner % 128 - HEAD, -width)
    gain1 = shift1 = query_b = value_b = jnp.zeros((1, width), F32)
    for g in range(4):
        block = fq_ref[g // 2, g % 2, 3 * SHARE : 3 * SHARE + 16, :]
        shift1 = shift1 + block[0:1].astype(F32)
        gain1 = gain1 + block[1:2].astype(F32)
        sums = block[:, : 3 * SHARE]
        pick_q = jnp.where((row == col - g * SHARE) & (row < SHARE), 1.0, 0.0).astype(BF)
        pick_v = jnp.where(from_value == col - g * SHARE, 1.0, 0.0).astype(BF)
        query_b = query_b + dot(sums, pick_q, NN)[2:3]
        value_b = value_b + dot(sums, pick_v, NN)[2:3]
    rest = tail[:16, :].astype(F32) * scale
    small = [
        gain1 / gain * scale, shift1 * scale, query_b * scale, value_b * scale,
        rest[9:10], rest[10:11], rest[11:12], rest[8:9],
    ]
    for k, value in enumerate(small):
        small_out[:, k * width : (k + 1) * width] = value
    for f in range(BLOCKS):
        small_out[:, 8 * width + f * BLOCK : 8 * width + (f + 1) * BLOCK] = rest[f : f + 1, :BLOCK]
    for copy in stores:
        copy.wait()
    for k in range(len(pieces_d) - SLOTS_IN, len(pieces_d)):
        d_store(k).wait()
    for k in range(len(pieces_u) - SLOTS_IN, len(pieces_u)):
        u_store(k).wait()


def finish_call(vec, h, dmid, dn, fd, fu, fq):
    width = h.shape[1]
    vm = pl.BlockSpec(memory_space=VM)
    hbm = pl.BlockSpec(memory_space=pl.ANY)
    dma = pltpu.SemaphoreType.DMA
    hidden = BLOCKS * BLOCK
    flat = jax.ShapeDtypeStruct((width, width), F32)
    return pl.pallas_call(
        finish_kernel,
        name="finish",
        out_shape=[
            jax.ShapeDtypeStruct(h.shape, F32),
            jax.ShapeDtypeStruct((1, 12 * width), F32),
            flat, flat, flat, flat,
            jax.ShapeDtypeStruct((width, hidden), F32),
            jax.ShapeDtypeStruct((hidden, width), F32),
        ],
        in_specs=[vm] * 4 + [hbm] * 3,
        out_specs=[vm] * 2 + [hbm] * 6,
        scratch_shapes=[
            VM((SLOTS_IN, 256, width), BF), VM((SLOTS_IN, width, 256), BF),
            VM((SLOTS_IN, 256, width), F32), VM((SLOTS_IN, width, 256), F32),
            VM((2, 2, QROWS, width), BF), VM((3, width, width), F32), VM((256, width), BF),
        ]
        + [dma((SLOTS_IN,))] * 4 + [dma((2,)), dma((3,))],
        compiler_params=pltpu.CompilerParams(vmem_limit_bytes=56 * 2**20),
    )(vec, h, dmid, dn, fd, fu, fq)


def norm_rows(values):
    center = values - jnp.mean(values, axis=-1, keepdims=True)
    spread = jnp.mean(center * center, axis=-1, keepdims=True)
    return center * lax.rsqrt(spread + 1e-05)


def norm_affine(values, gain_vec, shift_vec):
    return norm_rows(values) * gain_vec + shift_vec


def left_product(left_mat, right_mat):
    return lax.dot_general(
        left_mat, right_mat, (((0,), (0,)), ((), ())), preferred_element_type=jnp.float32
    )


def right_product(left_mat, weight):
    return lax.dot_general(
        left_mat, weight, (((1,), (1,)), ((), ())), preferred_element_type=jnp.float32
    )


def slot_tags(first_row, count_rows, layout):
    begins_flat, finishes_flat, slot_rows, band_cap, band_count = layout
    slot_index = first_row + jnp.arange(count_rows, dtype=jnp.int32)
    owner = slot_index // slot_rows
    within = slot_index - owner * slot_rows
    member = within // band_cap
    offset = within - member * band_cap
    flat_code = member * band_count + owner
    all_codes = jnp.arange(begins_flat.shape[0], dtype=jnp.int32)
    hit_table = flat_code[:, None] == all_codes[None, :]
    begins = jnp.sum(jnp.where(hit_table, begins_flat[None, :], 0), axis=1)
    finish = jnp.sum(jnp.where(hit_table, finishes_flat[None, :], 0), axis=1)
    position = begins + offset
    return (member, position, position < finish, slot_index)


def allowed_pairs(query_tags, key_tags):
    query_member, query_position, query_valid, query_slot = query_tags
    key_member, key_position, key_valid, key_slot = key_tags
    same_slot = query_slot[:, None] == key_slot[None, :]
    causal = (query_member[:, None] == key_member[None, :]) & (
        key_position[None, :] <= query_position[:, None]
    )
    return same_slot | query_valid[:, None] & key_valid[None, :] & causal


def on_device(
    residual_in,
    exit_layer,
    band_edges,
    norm1_gain,
    norm1_bias,
    query_weight,
    query_bias,
    key_weight,
    value_weight,
    value_bias,
    out_weight,
    out_bias,
    norm2_gain,
    norm2_bias,
    up_weight,
    up_bias,
    down_weight,
    down_bias,
    cotangent,
):
    slot_rows = residual_in.shape[1]
    model_width = residual_in.shape[2]
    head_size = model_width // HEADS
    score_scale = head_size ** (-0.5)
    band_here = lax.axis_index("band")
    band_count = lax.axis_size("band")
    band_cap = slot_rows // band_edges.shape[1]
    finishes = jnp.concatenate([band_edges[0][:, 1:], band_edges[0][:, -1:] + band_cap], axis=1)
    layout = (band_edges[0].reshape(-1), finishes.reshape(-1), slot_rows, band_cap, band_count)
    own_tags = slot_tags(band_here * slot_rows, slot_rows, layout)
    active = ((exit_layer[0] >= LAYER) & own_tags[2]).astype(jnp.float32)[:, None]
    total_active = lax.psum(jnp.sum(active), ("band", "batch"))
    hidden_in = residual_in[0].astype(jnp.float32)
    normed_one, norm_one_back = jax.vjp(
        norm_affine, hidden_in, norm1_gain.astype(jnp.float32), norm1_bias.astype(jnp.float32)
    )
    normed_low = normed_one.astype(jnp.bfloat16)
    queries = (
        jnp.dot(normed_low, query_weight, preferred_element_type=jnp.float32)
        + query_bias.astype(jnp.float32)
    ).astype(jnp.bfloat16)
    keys_own = jnp.dot(normed_low, key_weight, preferred_element_type=jnp.float32).astype(
        jnp.bfloat16
    )
    values_own = (
        jnp.dot(normed_low, value_weight, preferred_element_type=jnp.float32)
        + value_bias.astype(jnp.float32)
    ).astype(jnp.bfloat16)
    query_heads = queries.reshape(slot_rows, HEADS, head_size)
    start_state = (
        jnp.full((HEADS, slot_rows), -1e30, jnp.float32),
        jnp.zeros((HEADS, slot_rows), jnp.float32),
        jnp.zeros((slot_rows, HEADS, head_size), jnp.float32),
    )
    key_piece = lax.all_gather(keys_own, "band", axis=0, tiled=True)
    value_piece = lax.all_gather(values_own, "band", axis=0, tiled=True)
    piece_rows = key_piece.shape[0]
    step_rows = min(piece_rows, slot_rows)

    def one_step(step_index, inner_state):
        offset_row = step_index * step_rows
        key_block = lax.dynamic_slice_in_dim(key_piece, offset_row, step_rows, 0).reshape(
            step_rows, HEADS, head_size
        )
        value_block = lax.dynamic_slice_in_dim(value_piece, offset_row, step_rows, 0).reshape(
            step_rows, HEADS, head_size
        )
        mask = allowed_pairs(own_tags, slot_tags(offset_row, step_rows, layout))

        def accumulate(running):
            top_old, total_old, sum_old = running
            scores = (
                jnp.einsum(
                    "qhd,khd->hqk", query_heads, key_block, preferred_element_type=jnp.float32
                )
                * score_scale
            )
            scores = jnp.where(mask[None], scores, -1e30)
            top_new = jnp.maximum(top_old, jnp.max(scores, axis=-1))
            rescale = jnp.exp(top_old - top_new)
            weights_new = jnp.where(mask[None], jnp.exp(scores - top_new[..., None]), 0.0)
            total_new = total_old * rescale + jnp.sum(weights_new, axis=-1)
            sum_new = sum_old * rescale.T[..., None] + jnp.einsum(
                "hqk,khd->qhd",
                weights_new.astype(jnp.bfloat16),
                value_block,
                preferred_element_type=jnp.float32,
            )
            return (top_new, total_new, sum_new)

        return lax.cond(jnp.any(mask), accumulate, lambda running: running, inner_state)

    top_score, weight_total, weighted_sum = lax.fori_loop(
        0, piece_rows // step_rows, one_step, start_state
    )
    attended = weighted_sum / weight_total.T[..., None]
    log_total = top_score + jnp.log(weight_total)
    mixed_low = attended.reshape(slot_rows, model_width).astype(jnp.bfloat16)
    branch = jnp.dot(mixed_low, out_weight, preferred_element_type=jnp.float32) + out_bias.astype(
        jnp.float32
    )
    middle = hidden_in + active * branch
    normed_two, norm_two_back = jax.vjp(
        norm_affine, middle, norm2_gain.astype(jnp.float32), norm2_bias.astype(jnp.float32)
    )
    normed_two_low = normed_two.astype(jnp.bfloat16)
    pre_act = jnp.dot(
        normed_two_low, up_weight, preferred_element_type=jnp.float32
    ) + up_bias.astype(jnp.float32)
    activated, gelu_back = jax.vjp(jax.nn.gelu, pre_act)
    activated_low = activated.astype(jnp.bfloat16)
    down_out = jnp.dot(
        activated_low, down_weight, preferred_element_type=jnp.float32
    ) + down_bias.astype(jnp.float32)
    layer_out = (middle + active * down_out).astype(jnp.bfloat16)[None]
    out_grad = cotangent[0].astype(jnp.float32)
    down_grad = (active * out_grad).astype(jnp.bfloat16)
    down_weight_sum = left_product(activated_low, down_grad)
    down_bias_sum = jnp.sum(down_grad.astype(jnp.float32), axis=0)
    (pre_grad,) = gelu_back(right_product(down_grad, down_weight))
    pre_low = pre_grad.astype(jnp.bfloat16)
    up_weight_sum = left_product(normed_two_low, pre_low)
    up_bias_sum = jnp.sum(pre_low.astype(jnp.float32), axis=0)
    middle_norm, gain_two_sum, shift_two_sum = norm_two_back(right_product(pre_low, up_weight))
    middle_grad = out_grad + middle_norm
    branch_grad = (active * middle_grad).astype(jnp.bfloat16)
    out_weight_sum = left_product(mixed_low, branch_grad)
    out_bias_sum = jnp.sum(branch_grad.astype(jnp.float32), axis=0)
    mixed_grad = right_product(branch_grad, out_weight).astype(jnp.bfloat16)
    grad_heads = mixed_grad.reshape(slot_rows, HEADS, head_size)
    delta_row = jnp.sum(grad_heads.astype(jnp.float32) * attended, axis=-1).T

    def pair_terms(query_blk, grad_blk, logsum_blk, delta_blk, key_block, value_block, mask):
        scores = (
            jnp.einsum("qhd,khd->hqk", query_blk, key_block, preferred_element_type=jnp.float32)
            * score_scale
        )
        probability = jnp.where(mask[None], jnp.exp(scores - logsum_blk[..., None]), 0.0)
        prob_grad = jnp.einsum(
            "qhd,khd->hqk", grad_blk, value_block, preferred_element_type=jnp.float32
        )
        score_grad = (probability * (prob_grad - delta_blk[..., None])).astype(jnp.bfloat16)
        return (probability.astype(jnp.bfloat16), score_grad)

    all_rows = slot_rows * band_count
    start_back = (
        jnp.zeros((slot_rows, HEADS, head_size), jnp.float32),
        jnp.zeros((all_rows, model_width), jnp.float32),
        jnp.zeros((all_rows, model_width), jnp.float32),
    )
    fold_key_piece = lax.all_gather(keys_own, "band", axis=0, tiled=True)
    fold_value_piece = lax.all_gather(values_own, "band", axis=0, tiled=True)
    piece_rows = fold_key_piece.shape[0]
    fold_step_rows = min(piece_rows, slot_rows)

    def one_step(step_index, inner_state):
        offset_row = step_index * fold_step_rows
        key_block = lax.dynamic_slice_in_dim(fold_key_piece, offset_row, fold_step_rows, 0).reshape(
            fold_step_rows, HEADS, head_size
        )
        value_block = lax.dynamic_slice_in_dim(
            fold_value_piece, offset_row, fold_step_rows, 0
        ).reshape(fold_step_rows, HEADS, head_size)
        mask = allowed_pairs(own_tags, slot_tags(offset_row, fold_step_rows, layout))

        def accumulate(running):
            query_acc, key_sums, value_sums = running
            prob_low, score_grad = pair_terms(
                query_heads, grad_heads, log_total, delta_row, key_block, value_block, mask
            )
            query_acc = (
                query_acc
                + jnp.einsum(
                    "hqk,khd->qhd", score_grad, key_block, preferred_element_type=jnp.float32
                )
                * score_scale
            )
            key_term = (
                jnp.einsum(
                    "hqk,qhd->khd", score_grad, query_heads, preferred_element_type=jnp.float32
                ).reshape(fold_step_rows, model_width)
                * score_scale
            )
            value_term = jnp.einsum(
                "hqk,qhd->khd", prob_low, grad_heads, preferred_element_type=jnp.float32
            ).reshape(fold_step_rows, model_width)
            key_sums = lax.dynamic_update_slice_in_dim(
                key_sums,
                lax.dynamic_slice_in_dim(key_sums, offset_row, fold_step_rows, 0) + key_term,
                offset_row,
                0,
            )
            value_sums = lax.dynamic_update_slice_in_dim(
                value_sums,
                lax.dynamic_slice_in_dim(value_sums, offset_row, fold_step_rows, 0) + value_term,
                offset_row,
                0,
            )
            return (query_acc, key_sums, value_sums)

        return lax.cond(jnp.any(mask), accumulate, lambda running: running, inner_state)

    back_state = lax.fori_loop(0, piece_rows // fold_step_rows, one_step, start_back)
    query_sum, key_sums_all, value_sums_all = back_state
    key_sum, value_sum = (
        lax.psum_scatter(
            key_sums_all.astype(jnp.bfloat16), "band", scatter_dimension=0, tiled=True
        ).astype(jnp.float32),
        lax.psum_scatter(
            value_sums_all.astype(jnp.bfloat16), "band", scatter_dimension=0, tiled=True
        ).astype(jnp.float32),
    )
    query_low = query_sum.reshape(slot_rows, model_width).astype(jnp.bfloat16)
    key_low = key_sum.astype(jnp.bfloat16)
    value_low = value_sum.astype(jnp.bfloat16)
    query_weight_sum = left_product(normed_low, query_low)
    query_bias_sum = jnp.sum(query_low.astype(jnp.float32), axis=0)
    key_weight_sum = left_product(normed_low, key_low)
    value_weight_sum = left_product(normed_low, value_low)
    value_bias_sum = jnp.sum(value_low.astype(jnp.float32), axis=0)
    normed_grad = (
        right_product(query_low, query_weight)
        + right_product(key_low, key_weight)
        + right_product(value_low, value_weight)
    )
    input_norm, gain_one_sum, shift_one_sum = norm_one_back(normed_grad)
    input_grad = (middle_grad + input_norm)[None]
    (
        total_g1,
        total_b1,
        total_qw,
        total_qb,
        total_kw,
        total_vw,
        total_vb,
        total_ow,
        total_ob,
        total_g2,
        total_b2,
        total_uw,
        total_ub,
        total_dw,
        total_db,
    ) = lax.psum(
        (
            gain_one_sum,
            shift_one_sum,
            query_weight_sum,
            query_bias_sum,
            key_weight_sum,
            value_weight_sum,
            value_bias_sum,
            out_weight_sum,
            out_bias_sum,
            gain_two_sum,
            shift_two_sum,
            up_weight_sum,
            up_bias_sum,
            down_weight_sum,
            down_bias_sum,
        ),
        ("band", "batch"),
    )
    return (
        layer_out,
        input_grad,
        total_g1 / total_active,
        total_b1 / total_active,
        total_qw / total_active,
        total_qb / total_active,
        total_kw / total_active,
        total_vw / total_active,
        total_vb / total_active,
        total_ow / total_active,
        total_ob / total_active,
        total_g2 / total_active,
        total_b2 / total_active,
        total_uw / total_active,
        total_ub / total_active,
        total_dw / total_active,
        total_db / total_active,
    )


def fast_device(
    residual_in, exit_layer, band_edges, norm1_gain, norm1_bias, query_weight, query_bias,
    key_weight, value_weight, value_bias, out_weight, out_bias, norm2_gain, norm2_bias,
    up_weight, up_bias, down_weight, down_bias, cotangent,
):
    width = residual_in.shape[2]
    vec = jnp.concatenate(
        [norm1_gain, norm1_bias, query_bias, value_bias, out_bias, norm2_gain, norm2_bias, down_bias, up_bias]
    ).astype(F32)[None]
    h, cot = residual_in[0], cotangent[0]
    o, lse, att, wback, n1, q, kv, kt = attend_call(
        band_edges, vec, h, query_weight, key_weight, value_weight
    )
    layer, dmid, dn, fq, fd, fu = layer_call(
        band_edges, exit_layer, vec, h, cot, att, o, lse, wback, out_weight, n1, q, kv, kt, up_weight, down_weight
    )
    grad, small, qw, kw, vw, ow, uw, dw = finish_call(vec, h, dmid, dn, fd, fu, fq)
    g1, b1, qb, vb, ob, g2, b2, db = [small[0, k * width : (k + 1) * width] for k in range(8)]
    ub = small[0, 8 * width :]
    return (layer[None], grad[None], g1, b1, qw, qb, kw, vw, vb, ow, ob, g2, b2, uw, ub, dw, db)


def solution(mesh):
    placed = (
        (P("batch", "band", None), P("batch", "band"), P("batch", None, None))
        + (P(),) * 15
        + (P("batch", "band", None),)
    )
    fast = mesh.shape["band"] == BANDS and mesh.shape["batch"] == 4
    return jax.shard_map(
        fast_device if fast else on_device,
        mesh=mesh,
        in_specs=placed,
        out_specs=(P("batch", "band", None),) * 2 + (P(),) * 15,
        check_vma=False,
    )
```

```python
import functools

import jax
import jax.numpy as jnp
from jax import lax
from jax.experimental import pallas as pl
from jax.experimental.pallas import tpu as pltpu
from jax.sharding import PartitionSpec as P

MESH = pl.DeviceIdType.MESH
VM = pltpu.VMEM
BF = jnp.bfloat16
F32 = jnp.float32
HEADS = 12
LAYER = 6
HEAD = 64
BANDS = 8
CAP = 256
HALF = 128
MINE = 3
SHARE = MINE * HEAD
NEG = -1e30


def place():
    band = lax.axis_index("band")
    return band, band // 4, (band // 2) % 2, band % 2


def device(y, x, core):
    return (y * 4 + x * 2 + core, lax.axis_index("batch"))


def push(src, dst, send, recv, target):
    return pltpu.make_async_remote_copy(
        src_ref=src, dst_ref=dst, send_sem=send, recv_sem=recv, device_id=target, device_id_type=MESH
    )


def greet_band():
    band, _, _, _ = place()
    barrier = pltpu.get_barrier_semaphore()
    for step in range(1, BANDS):
        other = (band + step) % BANDS
        pl.semaphore_signal(
            barrier, inc=1, device_id=(other, lax.axis_index("batch")), device_id_type=MESH
        )
    pl.semaphore_wait(barrier, BANDS - 1)


def dot(a, b, dims):
    return lax.dot_general(a, b, ((dims[0], dims[1]), ((), ())), preferred_element_type=F32)


NN = ((1,), (0,))
NT = ((1,), (1,))
TN = ((0,), (0,))


def as_row(ref):
    return ref[...].astype(F32).reshape(1, -1)


def counts_of(edges_ref, seq, band):
    after = edges_ref[0, seq, jnp.minimum(band + 1, BANDS - 1)]
    return jnp.where(band == BANDS - 1, CAP, after - edges_ref[0, seq, band])


def attend_kernel(
    edges_ref, gain_ref, shift_ref, bq_ref, bv_ref, h_ref, wq_hbm, wk_hbm, wv_hbm,
    o_ref, lse_ref, att_ref, wback_ref, n1_hbm, n1t_hbm, q_hbm, kv_hbm, kt_hbm,
    rows_ref, n1_ref, n1t_ref, q_ref, kv_ref, kvt_ref, cols_ref, turned_ref,
    send, recv, out_send, out_recv, load, store,
):
    band, y, x, core = place()
    width = h_ref.shape[1]
    group = 2 * x + core
    wide = pl.ds(pl.multiple_of(x * 2 * SHARE + core * 128, 128), 256)
    loads = [
        pltpu.make_async_copy(ref.at[:, wide], cols_ref.at[k], load.at[k])
        for k, ref in enumerate((wq_hbm, wk_hbm, wv_hbm))
    ]
    for copy in loads:
        copy.start()
    greet_band()
    own = pl.ds(pl.multiple_of(y * CAP, CAP), CAP)
    half = pl.ds(pl.multiple_of(core * HALF, HALF), HALF)
    other_y, other_x, other_core = 1 - y, 1 - x, 1 - core
    sibling = device(y, x, other_core)
    copies = {}

    def go(name, src, dst, index, recv_index, target):
        copy = push(src, dst, send.at[index], recv.at[recv_index], target)
        copy.start()
        copies[name] = copy

    for k in range(2):
        from_rows = pl.ds(pl.multiple_of(other_y * CAP + k * HALF, HALF), HALF)
        go(("y", k), h_ref.at[from_rows], rows_ref.at[band, pl.ds(k * HALF, HALF)], 1 + k, 1 + core,
           device(other_y, x, k))
    for k in range(2):
        from_rows = pl.ds(pl.multiple_of(y * CAP + k * HALF, HALF), HALF)
        go(("x", k), h_ref.at[from_rows], rows_ref.at[band, pl.ds(k * HALF, HALF)], 3 + k, 3 + core,
           device(y, other_x, k))
    go("sib", h_ref.at[own], rows_ref.at[band], 0, 0, sibling)

    gain, shift = as_row(gain_ref), as_row(shift_ref)
    for k, copy in enumerate(loads):
        copy.wait()
        turned_ref[k] = cols_ref[k].T
        for h in range(MINE):
            part = turned_ref[k, pl.ds(pl.multiple_of(core * HEAD + h * HEAD, HEAD), HEAD), :]
            at = k * SHARE + h * HEAD
            wback_ref[at : at + HEAD, :] = part
    row = lax.broadcasted_iota(jnp.int32, (3 * SHARE, width), 0)
    col = lax.broadcasted_iota(jnp.int32, (3 * SHARE, width), 1) - group * SHARE
    pick_q = jnp.where((row == col) & (row < SHARE), 1.0, 0.0).astype(BF)
    pick_v = jnp.where((row - 2 * SHARE == col) & (row >= 2 * SHARE), 1.0, 0.0).astype(BF)

    def spread_row(ref):
        return jnp.broadcast_to(as_row(ref), (8, width)).astype(BF)

    bias = (dot(pick_q, spread_row(bq_ref), NT) + dot(pick_v, spread_row(bv_ref), NT))[:, :1]

    def project(rows, which):
        wide_rows = rows.astype(F32)
        center = wide_rows - jnp.mean(wide_rows, axis=-1, keepdims=True)
        spread = jnp.mean(center * center, axis=-1, keepdims=True)
        n1 = (center * lax.rsqrt(spread + 1e-05) * gain + shift).astype(BF)
        at = pl.ds(pl.multiple_of(which * CAP, CAP), CAP)
        n1_ref[at, :] = n1
        n1t_ref[:, at] = n1.T
        all_t = dot(wback_ref[...], n1, NT) + bias
        qt = (all_t[:SHARE] * 0.125).astype(BF)
        kvt = all_t[SHARE:].astype(BF)
        for h in range(MINE):
            one = jnp.concatenate(
                [kvt[h * HEAD : (h + 1) * HEAD], kvt[SHARE + h * HEAD : SHARE + (h + 1) * HEAD]], axis=0
            )
            kvt_ref[h, :, at] = one
            kv_ref[h, at, :] = one.T
            q_ref[h, :HEAD, at] = qt[h * HEAD : (h + 1) * HEAD]
            q_ref[h, HEAD:, at] = jnp.zeros((HEAD, CAP), BF)

    def project_two(first_y, first_x):
        def one(k, carry):
            which = first_y * 4 + first_x * 2 + k
            project(rows_ref[which], which)
            return carry

        lax.fori_loop(0, 2, one, 0)

    rows_ref[band] = h_ref[own, :]

    def wait_recv(index, which, size=HALF):
        ref = rows_ref.at[which] if size == CAP else rows_ref.at[which, half]
        push(ref, ref, send.at[0], recv.at[index], sibling).wait_recv()

    wait_recv(0, y * 4 + x * 2 + other_core, CAP)
    project_two(y, x)
    for k in range(2):
        from_band = other_y * 4 + x * 2 + k
        wait_recv(1 + k, from_band)
        piece = rows_ref.at[from_band, half]
        go(("fx", k), piece, piece, 5 + k, 5 + k, device(y, other_x, core))
        go(("fs", k), piece, piece, 7 + k, 7 + k, sibling)
    for k in range(2):
        from_band = y * 4 + other_x * 2 + k
        wait_recv(3 + k, from_band)
        piece = rows_ref.at[from_band, half]
        go(("fs", 2 + k), piece, piece, 9 + k, 9 + k, sibling)
    for k in range(2):
        copies[("fs", k)].wait_recv()
    project_two(other_y, x)
    for k in range(2):
        copies[("fs", 2 + k)].wait_recv()
    project_two(y, other_x)
    for k in range(2):
        from_band = other_y * 4 + other_x * 2 + k
        copies[("fx", k)].wait_recv()
        piece = rows_ref.at[from_band, half]
        go(("fs", 4 + k), piece, piece, 11 + k, 11 + k, sibling)
    for k in range(2):
        copies[("fs", 4 + k)].wait_recv()
    project_two(other_y, other_x)
    stores = [
        pltpu.make_async_copy(src, dst, store.at[k])
        for k, (src, dst) in enumerate(
            ((n1_ref, n1_hbm), (n1t_ref, n1t_hbm), (q_ref, q_hbm), (kv_ref, kv_hbm), (kvt_ref.at[:, :HEAD], kt_hbm))
        )
    ]
    for copy in stores:
        copy.start()

    key_at = lax.broadcasted_iota(jnp.int32, (CAP, CAP), 0)
    query_at = lax.broadcasted_iota(jnp.int32, (CAP, CAP), 1)
    lane = lax.broadcasted_iota(jnp.int32, (1, CAP), 1)
    share = pl.ds(pl.multiple_of(group * SHARE, SHARE), SHARE)
    side = pl.ds(pl.multiple_of(y * CAP, CAP), CAP)
    for i in range(BANDS - 1, -1, -1):
        cols = pl.ds(i * CAP, CAP)

        def one_head(h, carry):
            qt = q_ref[h, :, cols]
            scores = []
            for j in range(i + 1):
                s = dot(kv_ref[h, j * CAP : (j + 1) * CAP, :], qt, NN)
                keep = key_at < counts_of(edges_ref, y, j)
                if i == j:
                    keep = keep & (key_at <= query_at)
                scores.append(jnp.where(keep, s, NEG))
            top = functools.reduce(jnp.maximum, [jnp.max(s, axis=0, keepdims=True) for s in scores])
            total = jnp.zeros((1, CAP), F32)
            mix = jnp.zeros((HEAD, CAP), F32)
            for j in range(i + 1):
                p = jnp.exp(scores[j] - top)
                total = total + jnp.sum(p, axis=0, keepdims=True)
                mix = mix + dot(kvt_ref[h, HEAD:, j * CAP : (j + 1) * CAP], p.astype(BF), NN)
            valid = lane < counts_of(edges_ref, y, i)
            mix = jnp.where(valid, mix / total, kvt_ref[h, HEAD:, cols].astype(F32))
            o_ref[i, pl.ds(pl.multiple_of(h * HEAD, HEAD), HEAD), :] = mix.astype(BF)
            lse_ref[h, i : i + 1, :] = jnp.where(valid, top + jnp.log(total), -NEG)
            return carry

        lax.fori_loop(0, MINE, one_head, 0)
        copy = push(o_ref.at[i], att_ref.at[share, side], out_send.at[i], out_recv.at[band],
                    (i, lax.axis_index("batch")))
        pl.when(band != i)(copy.start)
        local = pltpu.make_async_copy(o_ref.at[i], att_ref.at[share, side], out_recv.at[band])
        pl.when(band == i)(local.start)
    for i in range(BANDS):
        from_y, from_x, from_core = i // 4, (i // 2) % 2, i % 2
        ref = att_ref.at[pl.ds((2 * from_x + from_core) * SHARE, SHARE), pl.ds(from_y * CAP, CAP)]
        copy = push(o_ref.at[i], ref, out_send.at[i], out_recv.at[i], sibling)
        copy.wait_recv()
        pl.when(band != i)(copy.wait_send)
    for copy in copies.values():
        copy.wait_send()
    for copy in stores:
        copy.wait()


def attend_call(edges, gain, shift, bq, bv, h, wq, wk, wv):
    width = h.shape[1]
    seq = BANDS * CAP
    vm = pl.BlockSpec(memory_space=VM)
    hbm = pl.BlockSpec(memory_space=pl.ANY)
    return pl.pallas_call(
        attend_kernel,
        name="attend",
        out_shape=[
            jax.ShapeDtypeStruct((BANDS, SHARE, CAP), BF),
            jax.ShapeDtypeStruct((MINE, BANDS, CAP), F32),
            jax.ShapeDtypeStruct((width, 2 * CAP), BF),
            jax.ShapeDtypeStruct((3 * SHARE, width), BF),
            jax.ShapeDtypeStruct((seq, width), BF),
            jax.ShapeDtypeStruct((width, seq), BF),
            jax.ShapeDtypeStruct((MINE, 128, seq), BF),
            jax.ShapeDtypeStruct((MINE, seq, 128), BF),
            jax.ShapeDtypeStruct((MINE, HEAD, seq), BF),
        ],
        in_specs=[pl.BlockSpec(memory_space=pltpu.SMEM)] + [vm] * 5 + [hbm] * 3,
        out_specs=[vm] * 4 + [hbm] * 5,
        scratch_shapes=[
            VM((BANDS, CAP, width), BF),
            VM((seq, width), BF),
            VM((width, seq), BF),
            VM((MINE, 128, seq), BF),
            VM((MINE, seq, 128), BF),
            VM((MINE, 128, seq), BF),
            VM((3, width, 256), BF),
            VM((3, 256, width), BF),
            pltpu.SemaphoreType.DMA((13,)),
            pltpu.SemaphoreType.DMA((13,)),
            pltpu.SemaphoreType.DMA((BANDS,)),
            pltpu.SemaphoreType.DMA((BANDS,)),
            pltpu.SemaphoreType.DMA((3,)),
            pltpu.SemaphoreType.DMA((5,)),
        ],
        compiler_params=pltpu.CompilerParams(
            collective_id=0, has_side_effects=True, vmem_limit_bytes=56 * 2**20
        ),
    )(edges, gain, shift, bq, bv, h, wq, wk, wv)


BLOCK = 512
BLOCKS = 6
QLANES = 640
D_AXES = ('xyab', 'yabx', 'xyab', 'xyab', 'yaxb', 'xyab', 'xyab', 'xyab')
U_AXES = ('axyb', 'xayb', 'axyb', 'xaby', 'xaby', 'yaxb')
Q_AXES = ('yab', 'yab', 'yab')
SCHEDULE = {'m0': (0, 8), 'a0': (), 'm1': (0, 8, 1, 9), 'a1': (), 'm2': (1, 9, 2, 10), 'a2': (0, 8, 2, 10), 'm3': (3, 11, 1, 9), 'a3': (3, 0, 11, 8, 10), 'm4': (1, 4, 12, 8, 2, 9), 'a4': (0, 4, 12), 'm5': (3, 1, 2, 8, 5, 13, 9, 0, 11), 'a5': (5, 10, 13, 2, 4), 'e': (8, 3, 9, 10, 0, 12, 1, 11, 2, 13, 4, 5, 3), 'o': (6, 7, 9), 'b7': (10, 0, 6, 7, 12, 8, 11, 1, 2, 4, 5, 13, 9, 3, 10), 'b6': (0, 12, 11, 10, 6, 1, 2, 4, 5, 7), 'b5': (9, 12, 8, 3, 11, 13, 1, 6, 4, 5, 2), 'b4': (7, 0, 12, 10, 8, 3), 'b3': (0, 8, 1, 11, 13, 6, 9, 5, 4, 7, 1, 3, 9), 'b2': (12, 2), 'b1': (10, 2), 'b0': (11, 10), 'q0': (13, 14, 6, 5), 'q1': (3, 15, 4), 'q2': (3, 7, 16), 'end': (12, 14, 6, 5, 7, 14, 6, 15, 11, 7, 13, 11, 14, 4, 15, 12, 4, 13, 16, 12, 14, 6, 5, 15, 7, 16, 5, 14, 13, 15, 6, 16, 13, 6, 14, 15, 7, 7, 16, 15, 16, 14, 14, 16, 15, 15, 16, 16)}


def partners():
    band, y, x, core = place()
    z = lax.axis_index("batch")
    return {
        "core": (core, device(y, x, 1 - core)),
        "x": (x, device(y, 1 - x, core)),
        "y": (y, device(1 - y, x, core)),
        "a": (z % 2, (band, z + 1 - 2 * (z % 2))),
        "b": (z // 2, (band, (z + 2) % 4)),
    }


class Chain:
    def __init__(self, send, recv, free, store):
        self.send, self.recv, self.free, self.finish = send, recv, free, store
        self.links = partners()
        self.steps = []
        self.at = 0

    def halve(self, piece, rows, axes, landing):
        start, keep, give = 0, [], []
        for axis in axes:
            rows //= 2
            bit = self.links[axis][0]
            keep.append((start + bit * rows, rows))
            give.append((start + (1 - bit) * rows, rows))
            start = start + bit * rows
        for level, axis in enumerate(axes):
            self.steps.append((axis, piece(give[level]), landing[level], landing[level], piece(keep[level]), None))
        first = len(self.steps) - len(axes)
        for level in range(len(axes) - 1, -1, -1):
            mine = piece(keep[level])
            self.steps.append((axes[level], mine, mine, piece(give[level]), None, first + level))

    def copy(self, number, arrival=False):
        axis, src, dst, got, _, _ = self.steps[number]
        if arrival:
            src = dst = got
        return push(src, dst, self.send.at[number], self.recv.at[number], self.links[axis][1])

    def add(self, target, source):
        rows, lanes = source.shape
        size = 32 if lanes < 512 and rows % 32 == 0 else 16

        def some(r, carry):
            at = pl.ds(pl.multiple_of(r * size, size), size)
            target[at, :] = (target[at, :].astype(F32) + source[at, :].astype(F32)).astype(BF)
            return carry

        lax.fori_loop(0, rows // size, some, 0)

    def advance(self):
        number, self.at = self.at, self.at + 1
        if number > 0:
            axis, _, _, got, add, _ = self.steps[number - 1]
            self.copy(number - 1, True).wait_recv()
            if add is not None:
                self.copy(number - 1).wait_send()
                pl.semaphore_signal(
                    self.free.at[number - 1], inc=1, device_id=self.links[axis][1], device_id_type=MESH
                )
                self.add(add, got)
        if number < len(self.steps):
            freed = self.steps[number][5]
            if freed is not None:
                pl.semaphore_wait(self.free.at[freed], 1)
            self.copy(number).start()
        else:
            self.finish.start()

    def drain(self):
        for number, step in enumerate(self.steps):
            if step[4] is None:
                self.copy(number).wait_send()
        self.finish.wait()


def weight_chain(total, landing, send, recv, free, index, axes, out, out_sem):
    core = lax.axis_index("band") % 2
    chain = Chain(
        send.at[index], recv.at[index], free.at[index],
        pltpu.make_async_copy(total.at[index], out.at[index], out_sem.at[index]),
    )
    mine, other, first = total.at[index, core], total.at[index, 1 - core], landing[0].at[index]
    chain.steps.append(("core", other, first, first, mine, None))

    def piece(span):
        return total.at[index, core, pl.ds(pl.multiple_of(span[0], 16), span[1])]

    chain.halve(piece, total.shape[2], axes, [spot.at[index] for spot in landing[1:]])
    chain.steps.append(("core", mine, mine, other, None, 0))
    return chain


def head_chain(total, landing, send, recv, free, index, axes, out, out_sem):
    _, _, x, core = place()
    chain = Chain(
        send.at[index], recv.at[index], free.at[index],
        pltpu.make_async_copy(total.at[:, :, index], out.at[:, :, index], out_sem.at[index]),
    )

    def piece(span):
        return total.at[x, core, index, pl.ds(pl.multiple_of(span[0], 16), span[1])]

    chain.halve(piece, total.shape[3], axes, [spot.at[index] for spot in landing])
    mine = total.at[x, core, index]
    chain.steps.append(("x", mine, mine, total.at[1 - x, core, index], None, None))
    both = total.at[:, core, index]
    chain.steps.append(("core", both, both, total.at[:, 1 - core, index], None, None))
    return chain


def layer_kernel(
    edges_ref, exit_ref, shift1_ref, bo_ref, g2_ref, b2_ref, bd_ref, ub_ref,
    h_ref, cot_ref, att_ref, o_ref, lse_ref, wback_ref, wout_ref,
    n1_hbm, n1t_hbm, q_hbm, kv_hbm, kt_hbm, wup_hbm, wdown_hbm,
    dn_ref, layer_hbm, dmid_hbm, fq_hbm, fd_hbm, fu_hbm,
    gd_ref, gu_ref, fq_ref, d0, d1, d2, d3, d4, u0, u1, u2, u3, u4, q1, q2, q3,
    layer_ref, dmid_ref, q_ref, kv_ref, kt_ref, dz_ref, da_ref, do_ref, sib_out, sib_in, row_out,
    d_send, d_recv, d_free, d_out, u_send, u_recv, u_free, u_out, q_send, q_recv, q_free, q_out,
    do_send, do_recv, sib_send, sib_recv, dn_send, dn_recv, load, wload, out_sem,
):
    band, y, x, core = place()
    batch = lax.axis_index("batch")
    links = partners()
    sibling = links["core"][1]
    width = h_ref.shape[1]
    loads = [
        pltpu.make_async_copy(q_hbm, q_ref, load.at[0]),
        pltpu.make_async_copy(kv_hbm, kv_ref, load.at[1]),
        pltpu.make_async_copy(kt_hbm, kt_ref, load.at[2]),
    ]
    barrier = pltpu.get_barrier_semaphore()
    for step in range(1, BANDS):
        pl.semaphore_signal(barrier, inc=1, device_id=((band + step) % BANDS, batch), device_id_type=MESH)
    for axis in ("a", "b"):
        pl.semaphore_signal(barrier, inc=1, device_id=links[axis][1], device_id_type=MESH)

    chains = [
        weight_chain(gd_ref, (d0, d1, d2, d3, d4), d_send, d_recv, d_free, k, D_AXES[k], fd_hbm, d_out)
        for k in range(BLOCKS + 2)
    ] + [
        weight_chain(gu_ref, (u0, u1, u2, u3, u4), u_send, u_recv, u_free, k, U_AXES[k], fu_hbm, u_out)
        for k in range(BLOCKS)
    ] + [
        head_chain(fq_ref, (q1, q2, q3), q_send, q_recv, q_free, k, Q_AXES[k], fq_hbm, q_out) for k in range(3)
    ]
    layer_out = pltpu.make_async_copy(layer_ref, layer_hbm, out_sem.at[0])
    dmid_out = pltpu.make_async_copy(dmid_ref, dmid_hbm, out_sem.at[1])

    def serve(point):
        for k in SCHEDULE.get(point, ()):
            chains[k].advance()

    lane = lax.broadcasted_iota(jnp.int32, (1, 2 * CAP), 1)
    limit = jnp.where(lane < CAP, counts_of(edges_ref, 0, band), counts_of(edges_ref, 1, band) + CAP)
    active_row = jnp.where((exit_ref[...] >= LAYER) & (lane < limit), 1.0, 0.0)
    active = jnp.broadcast_to(active_row, (8, 2 * CAP)).T[:, :1]

    def feed_forward(mid_ref, sum_ref, dn2_ref, n2_ref, n2t_ref, wu, wd, pre_ref, dact_ref, act_ref, dpre_ref, part_ref, row_ref):
        def weights(f):
            at = pl.ds(f * BLOCK, BLOCK)
            return (
                pltpu.make_async_copy(wup_hbm.at[:, at], wu.at[f % 2], wload.at[0, f % 2]),
                pltpu.make_async_copy(wdown_hbm.at[at], wd.at[f % 2], wload.at[1, f % 2]),
            )

        for copy in weights(0):
            copy.start()
        for copy in loads:
            copy.start()
        branch = dot(att_ref[...], wout_ref[...], TN) + as_row(bo_ref)
        middle = h_ref[...].astype(F32) + active * branch
        mid_ref[...] = middle
        center = middle - jnp.mean(middle, axis=-1, keepdims=True)
        spread = jnp.mean(center * center, axis=-1, keepdims=True)
        scale2 = lax.rsqrt(spread + 1e-05)
        n2 = (center * scale2 * as_row(g2_ref) + as_row(b2_ref)).astype(BF)
        n2_ref[...] = n2
        n2t_ref[...] = n2.T
        dz_ref[...] = (active * cot_ref[...].astype(F32)).astype(BF)
        up_row = as_row(ub_ref)
        row_ref[...] = jnp.zeros_like(row_ref)
        sum_ref[...] = jnp.zeros_like(sum_ref)
        dn2_ref[...] = jnp.zeros_like(dn2_ref)
        for f in range(BLOCKS):
            if f + 1 < BLOCKS:
                for copy in weights(f + 1):
                    copy.start()
            for copy in weights(f):
                copy.wait()
            slot = f % 2
            pre_ref[...] = dot(n2_ref[...], wu[slot], NN)
            dact_ref[...] = dot(dz_ref[...], wd[slot], NT)
            up_bias = up_row[:, f * BLOCK : (f + 1) * BLOCK]
            part_ref[...] = jnp.zeros_like(part_ref)

            def rows(r, carry):
                at = pl.ds(pl.multiple_of(r * 64, 64), 64)
                pre = pre_ref[at, :] + up_bias
                square = pre * pre
                t = jnp.tanh(0.7978845608028654 * pre * (1.0 + 0.044715 * square))
                half = 0.5 * (1.0 + t)
                slope = half + (0.5 * 0.7978845608028654) * pre * (1.0 - t * t) * (1.0 + 0.134145 * square)
                act_ref[at, :] = (pre * half).astype(BF)
                dpre = (dact_ref[at, :] * slope).astype(BF)
                dpre_ref[at, :] = dpre
                part_ref[...] += jnp.sum(dpre.astype(F32).reshape(8, 8, BLOCK), axis=0)
                return carry

            lax.fori_loop(0, 2 * CAP // 64, rows, 0)
            down = dot(act_ref[...], dz_ref[...], TN).astype(BF)
            gd_ref[f, 0] = down[: BLOCK // 2]
            gd_ref[f, 1] = down[BLOCK // 2 :]
            up = dot(n2t_ref[...], dpre_ref[...], NN).astype(BF)
            gu_ref[f, 0] = up[:, : BLOCK // 2]
            gu_ref[f, 1] = up[:, BLOCK // 2 :]
            row_ref[f : f + 1, :BLOCK] = jnp.sum(part_ref[...], axis=0, keepdims=True)
            if f == 0:
                pl.semaphore_wait(barrier, BANDS + 1)
            serve(f'm{f}')
            sum_ref[...] += dot(act_ref[...], wd[slot], NN)
            dn2_ref[...] += dot(dpre_ref[...], wu[slot], NT)
            serve(f'a{f}')
        middle = mid_ref[...]
        layer_ref[...] = (middle + active * (sum_ref[...] + as_row(bd_ref))).astype(BF)
        center = middle - jnp.mean(middle, axis=-1, keepdims=True)
        spread = jnp.mean(center * center, axis=-1, keepdims=True)
        scale2 = lax.rsqrt(spread + 1e-05)
        xhat = center * scale2
        dn2 = dn2_ref[...]
        e2 = dn2 * as_row(g2_ref)
        cot = cot_ref[...].astype(F32)
        dmid = cot + scale2 * (
            e2 - jnp.mean(e2, axis=-1, keepdims=True) - xhat * jnp.mean(e2 * xhat, axis=-1, keepdims=True)
        )
        dmid_ref[...] = dmid
        layer_out.start()
        dmid_out.start()
        da = (active * dmid).astype(BF)
        n2_ref[...] = da
        da_ref[...] = dot(wout_ref[...], da, NT).astype(BF)
        for i in range(BANDS):
            copy = push(part_for(i), do_ref.at[band], do_send.at[i], do_recv.at[band], (i, batch))
            pl.when(band != i)(copy.start)
            local = pltpu.make_async_copy(part_for(i), do_ref.at[band], do_recv.at[band])
            pl.when(band == i)(local.start)
        serve('e')
        out = dot(att_ref[...], n2_ref[...], NN).astype(BF)
        gd_ref[BLOCKS, 0] = out[:256]
        gd_ref[BLOCKS, 1] = out[256:512]
        gd_ref[BLOCKS + 1, 0] = out[512:]
        count = jnp.sum(active_row)
        big = jnp.floor(count * (1.0 / 64.0))
        mid = jnp.floor((count - 64.0 * big) * 0.125)
        small = count - 64.0 * big - 8.0 * mid
        at = lax.broadcasted_iota(jnp.int32, (1, width), 1)
        digits = jnp.where(at == 0, big, jnp.where(at == 1, mid, jnp.where(at == 2, small, 0.0)))

        def total(v):
            return jnp.sum(v, axis=0, keepdims=True)

        sums = [
            total(dz_ref[...].astype(F32)), total(da.astype(F32)), total(dn2 * xhat), total(dn2), digits,
        ]
        for k, row in enumerate(sums):
            row_ref[8 + k : 9 + k, :] = row
        gd_ref[BLOCKS + 1, 1, :16, :] = row_ref[...].astype(BF)

    def part_for(i):
        to_y, to_x, to_core = i // 4, (i // 2) % 2, i % 2
        return da_ref.at[pl.ds((2 * to_x + to_core) * SHARE, SHARE), pl.ds(to_y * CAP, CAP)]

    gd_ref[BLOCKS + 1, 1] = jnp.zeros(gd_ref.shape[2:], BF)
    rows2 = 2 * CAP
    pl.run_scoped(
        feed_forward,
        VM((rows2, width), F32), VM((rows2, width), F32), VM((rows2, width), F32),
        VM((rows2, width), BF), VM((width, rows2), BF),
        VM((2, width, BLOCK), BF), VM((2, BLOCK, width), BF),
        VM((rows2, BLOCK), F32), VM((rows2, BLOCK), F32), VM((rows2, BLOCK), BF), VM((rows2, BLOCK), BF),
        VM((8, BLOCK), F32), VM((16, width), F32),
    )
    serve('o')

    half = pl.ds(pl.multiple_of(core * HALF, HALF), HALF)
    key_at = lax.broadcasted_iota(jnp.int32, (CAP, CAP), 0)
    query_at = lax.broadcasted_iota(jnp.int32, (CAP, CAP), 1)

    def sib_copy(i):
        return push(sib_out.at[i % 2], sib_in.at[i], sib_send.at[i], sib_recv.at[i], sibling)

    def dn_copy(i):
        return push(row_out.at[i % 2], dn_ref.at[y, x, half], dn_send.at[i], dn_recv.at[band], (i, batch))

    def dn_local(i):
        return pltpu.make_async_copy(row_out.at[i % 2], dn_ref.at[y, x, half], dn_recv.at[band])

    def backward(dk_ref, d_ref, mine_ref, n1_ref, n1t_ref, small_ref):
        turned_load = pltpu.make_async_copy(n1t_hbm, n1t_ref, load.at[3])
        turned_load.start()

        def rows_load(i):
            return pltpu.make_async_copy(n1_hbm.at[pl.ds(i * CAP, CAP)], n1_ref.at[i % 2], load.at[4 + i % 2])

        rows_load(BANDS - 1).start()

        def finish(i):
            sib_copy(i).wait_recv()
            if i + 2 < BANDS:
                pl.when(band != i + 2)(dn_copy(i + 2).wait_send)

                @pl.when(band == i + 2)
                def _():
                    push(row_out.at[0], dn_ref.at[y, x, half], dn_send.at[0], dn_recv.at[band], sibling).wait_recv()

            row_out[i % 2] = (mine_ref[i % 2] + sib_in[i].astype(F32)).astype(BF)
            pl.when(band != i)(dn_copy(i).start)
            pl.when(band == i)(dn_local(i).start)

        dk_ref[...] = jnp.zeros_like(dk_ref)
        small_ref[...] = jnp.zeros_like(small_ref)
        for copy in loads:
            copy.wait()
        for i in range(BANDS - 1, -1, -1):
            cols = pl.ds(i * CAP, CAP)
            push(do_ref.at[i], do_ref.at[i], do_send.at[i], do_recv.at[i], sibling).wait_recv()

            def one_head(h, carry):
                qt = q_ref[h, :, cols]
                dot_t = do_ref[i, pl.ds(pl.multiple_of(h * HEAD, HEAD), HEAD), :]
                dop = jnp.concatenate([jnp.zeros_like(dot_t), dot_t], axis=0)
                lse = lse_ref[h, i : i + 1, :]
                o = o_ref[i, pl.ds(pl.multiple_of(h * HEAD, HEAD), HEAD), :]
                delta = jnp.sum(dot_t.astype(F32) * o.astype(F32), axis=0, keepdims=True)
                dq = jnp.zeros((HEAD, CAP), F32)
                for j in range(i + 1):
                    at = pl.ds(j * CAP, CAP)
                    kv = kv_ref[h, at, :]
                    s = dot(kv, qt, NN)
                    dp = dot(kv, dop, NN)
                    keep = key_at < counts_of(edges_ref, y, j)
                    if i == j:
                        keep = keep & (key_at <= query_at)
                    p = jnp.where(keep, jnp.exp(s - lse), 0.0)
                    if i == j:
                        alone = (key_at == query_at) & (query_at >= counts_of(edges_ref, y, i))
                        p = jnp.where(alone, 1.0, p)
                    ds = (p * (dp - delta)).astype(BF)
                    dq = dq + dot(kt_ref[h, :, at], ds, NN)
                    dk_ref[h, at, :] += dot(ds, qt, NT) + dot(p.astype(BF), dop, NT)
                d_ref[pl.ds(pl.multiple_of(h * HEAD, HEAD), HEAD), cols] = (dq * 0.125).astype(BF)
                pair = dk_ref[h, cols, :].T.astype(BF)
                d_ref[pl.ds(pl.multiple_of(SHARE + h * HEAD, HEAD), HEAD), cols] = pair[:HEAD]
                d_ref[pl.ds(pl.multiple_of(2 * SHARE + h * HEAD, HEAD), HEAD), cols] = pair[HEAD:]
                return carry

            lax.fori_loop(0, MINE, one_head, 0)
            rows_load(i).wait()
            if i > 0:
                rows_load(i - 1).start()
            dn = dot(d_ref[:, cols], wback_ref[...], TN)
            centered = n1_ref[i % 2].astype(F32) - as_row(shift1_ref)
            small_ref[0:1, :] += jnp.sum(dn, axis=0, keepdims=True)
            small_ref[1:2, :] += jnp.sum(dn * centered, axis=0, keepdims=True)
            mine_ref[2] = dn[:HALF]
            mine_ref[3] = dn[HALF:]
            if i + 2 < BANDS:
                sib_copy(i + 2).wait_send()
            sib_out[i % 2] = mine_ref[2 + (1 - core)].astype(BF)
            mine_ref[i % 2] = mine_ref[2 + core]
            sib_copy(i).start()
            if i < BANDS - 1:
                finish(i + 1)
            serve(f'b{i}')
        turned_load.wait()
        small_ref[2:3, : 3 * SHARE] = dot(jnp.ones((8, d_ref.shape[1]), BF), d_ref[...], NT)[:1]
        turned = small_ref[...].T.astype(BF)
        for k in range(3):
            rows = slice(k * 256, (k + 1) * 256)
            fq_ref[x, core, k, :, : 3 * SHARE] = dot(n1t_ref[rows, :], d_ref[...], NT).astype(BF)
            fq_ref[x, core, k, :, 3 * SHARE :] = jnp.concatenate(
                [turned[rows], jnp.zeros((256, QLANES - 3 * SHARE - 8), BF)], axis=1
            )
            serve(f'q{k}')
        finish(0)

    pl.run_scoped(
        backward,
        VM((MINE, BANDS * CAP, 128), F32),
        VM((3 * SHARE, BANDS * CAP), BF),
        VM((4, HALF, width), F32),
        VM((2, CAP, width), BF),
        VM((width, BANDS * CAP), BF),
        VM((8, width), F32),
    )
    serve('end')
    left = [[k] * (len(chain.steps) + 1 - chain.at) for k, chain in enumerate(chains)]
    while any(left):
        for k, rest in enumerate(left):
            if rest:
                chains[rest.pop()].advance()

    for i in range(BANDS):
        copy = push(part_for(i), do_ref.at[i], do_send.at[i], do_recv.at[i], sibling)
        pl.when(band != i)(copy.wait_send)
        if i < 2:
            sib_copy(i).wait_send()
            pl.when(band != i)(dn_copy(i).wait_send)
    for i in range(BANDS):
        from_y, from_x, from_core = i // 4, i // 2 % 2, i % 2
        arrived = push(row_out.at[0], dn_ref.at[from_y, from_x, pl.ds(from_core * HALF, HALF)],
                       dn_send.at[i], dn_recv.at[i], sibling)
        if i < 2:
            arrived.wait_recv()
        else:
            pl.when(band != i)(arrived.wait_recv)
    for chain in chains:
        chain.drain()
    layer_out.wait()
    dmid_out.wait()


def layer_call(edges, exits, vecs, h, cot, att, o, lse, wback, wout, n1, n1t, q, kv, kt, wup, wdown):
    width = h.shape[1]
    seq = BANDS * CAP
    vm = pl.BlockSpec(memory_space=VM)
    hbm = pl.BlockSpec(memory_space=pl.ANY)
    dma, credit = pltpu.SemaphoreType.DMA, pltpu.SemaphoreType.REGULAR
    eight = dma((BANDS,))

    def room(*shape):
        return VM(shape, BF)

    def spots(number, rows, lanes, levels):
        return [room(number, rows // 2**k, lanes) for k in levels]

    def sems(number, steps, levels):
        return [dma((number, steps)), dma((number, steps)), credit((number, levels)), dma((number,))]

    parts_d, parts_u = BLOCKS + 2, BLOCKS
    return pl.pallas_call(
        layer_kernel,
        name="layer",
        out_shape=[
            jax.ShapeDtypeStruct((2, 2, CAP, width), BF),
            jax.ShapeDtypeStruct(h.shape, BF),
            jax.ShapeDtypeStruct(h.shape, F32),
            jax.ShapeDtypeStruct((2, 2, 3, 256, QLANES), BF),
            jax.ShapeDtypeStruct((parts_d, 2, 256, width), BF),
            jax.ShapeDtypeStruct((parts_u, 2, width, 256), BF),
        ],
        in_specs=[pl.BlockSpec(memory_space=pltpu.SMEM)] + [vm] * 14 + [hbm] * 7,
        out_specs=[vm] + [hbm] * 5,
        scratch_shapes=[room(parts_d, 2, 256, width), room(parts_u, 2, width, 256), room(2, 2, 3, 256, QLANES)]
        + spots(parts_d, 256, width, range(5))
        + spots(parts_u, width, 256, range(5))
        + spots(3, 256, QLANES, range(1, 4))
        + [
            room(*h.shape), VM(h.shape, F32),
            room(MINE, 128, seq), room(MINE, seq, 128), room(MINE, HEAD, seq),
            room(2 * CAP, width), room(width, 2 * CAP), room(BANDS, SHARE, CAP),
            room(2, HALF, width), room(BANDS, HALF, width), room(2, HALF, width),
        ]
        + sems(parts_d, 10, 5) + sems(parts_u, 10, 5) + sems(3, 8, 3)
        + [eight] * 6 + [dma((6,)), dma((2, 2)), dma((2,))],
        compiler_params=pltpu.CompilerParams(
            collective_id=1, has_side_effects=True, vmem_limit_bytes=63 * 2**20
        ),
    )(edges, exits, *vecs, h, cot, att, o, lse, wback, wout, n1, n1t, q, kv, kt, wup, wdown)


SLOTS = 6


def finish_kernel(
    gain_ref, h_ref, dmid_ref, dn_ref, fd_hbm, fu_hbm, fq_hbm,
    grad_ref, g1_ref, b1_ref, qb_ref, vb_ref, ob_ref, g2_ref, b2_ref, ub_ref, db_ref,
    qw_hbm, kw_hbm, vw_hbm, ow_hbm, uw_hbm, dw_hbm,
    in_d, in_u, in_q, out_d, out_u, square, load_d, load_u, load_q, store_d, store_u, store_q,
):
    width = h_ref.shape[1]
    tail = (BLOCKS + 1, 1)
    halves_d = [tail] + [(f, c) for f in range(BLOCKS + 2) for c in range(2) if (f, c) != tail]
    halves_u = [(f, c) for f in range(BLOCKS) for c in range(2)]

    def load_of(kind, f, c):
        src, dst, sem = ((fd_hbm, in_d, load_d), (fu_hbm, in_u, load_u))[kind]
        return pltpu.make_async_copy(src.at[f, c], dst.at[f, c], sem.at[f, c])

    def q_load(g, k):
        return pltpu.make_async_copy(
            fq_hbm.at[g // 2, g % 2, k], in_q.at[g // 2, g % 2, k], load_q.at[g, k]
        )

    for k in range(max(len(halves_d), len(halves_u))):
        if k < len(halves_d):
            load_of(0, *halves_d[k]).start()
        if k < len(halves_u):
            load_of(1, *halves_u[k]).start()
    for k in range(3):
        for g in range(4):
            q_load(g, k).start()

    load_of(0, *tail).wait()
    rest = in_d[tail[0], tail[1], :16, :].astype(F32)
    count = rest[12:13, :3]
    total = 64.0 * count[:, 0:1] + 8.0 * count[:, 1:2] + count[:, 2:3]
    scale = 1.0 / total

    def store_of(kind, k):
        if kind == 0:
            f, c = halves_d[1:][k]
            row = f * BLOCK + c * 256
            target = dw_hbm.at[pl.ds(row, 256)] if f < BLOCKS else ow_hbm.at[pl.ds(row - BLOCKS * BLOCK, 256)]
            return pltpu.make_async_copy(out_d.at[k % SLOTS], target, store_d.at[k % SLOTS])
        f, c = halves_u[k]
        target = uw_hbm.at[:, pl.ds(f * BLOCK + c * 256, 256)]
        return pltpu.make_async_copy(out_u.at[k % SLOTS], target, store_u.at[k % SLOTS])

    def convert(kind, k):
        f, c = halves_u[k] if kind else halves_d[1:][k]
        source, out = ((in_d, out_d), (in_u, out_u))[kind]
        load_of(kind, f, c).wait()
        if k >= SLOTS:
            store_of(kind, k - SLOTS).wait()
        step = 32 if kind == 0 else 96

        def some(r, carry):
            at = pl.ds(pl.multiple_of(r * step, step), step)
            out[k % SLOTS, at, :] = source[f, c, at, :].astype(F32) * scale
            return carry

        lax.fori_loop(0, source.shape[2] // step, some, 0)
        store_of(kind, k).start()

    number_d, number_u = len(halves_d) - 1, len(halves_u)
    for k in range(max(number_d, number_u)):
        if k < number_d:
            convert(0, k)
        if k < number_u:
            convert(1, k)

    outs = (qw_hbm, kw_hbm, vw_hbm)

    def q_store(which, k):
        rows = pl.ds(k * 256, 256)
        return pltpu.make_async_copy(square.at[which, rows], outs[which].at[rows], store_q.at[which, k])

    for k in range(3):
        for g in range(4):
            q_load(g, k).wait()
        for which in range(3):
            square[which, k * 256 : (k + 1) * 256, :] = jnp.concatenate(
                [
                    in_q[g // 2, g % 2, k, :, which * SHARE : (which + 1) * SHARE].astype(F32) * scale
                    for g in range(4)
                ],
                axis=1,
            )
            q_store(which, k).start()

    hidden = h_ref[...].astype(F32)
    center = hidden - jnp.mean(hidden, axis=-1, keepdims=True)
    spread = jnp.mean(center * center, axis=-1, keepdims=True)
    scale1 = lax.rsqrt(spread + 1e-05)
    xhat = center * scale1
    dn1 = jnp.concatenate([dn_ref[s, 0].astype(F32) + dn_ref[s, 1].astype(F32) for s in range(2)], axis=0)
    gain = as_row(gain_ref)
    e1 = dn1 * gain
    grad_ref[...] = dmid_ref[...] + scale1 * (
        e1 - jnp.mean(e1, axis=-1, keepdims=True) - xhat * jnp.mean(e1 * xhat, axis=-1, keepdims=True)
    )

    row = lax.broadcasted_iota(jnp.int32, (width, width), 0)
    col = lax.broadcasted_iota(jnp.int32, (width, width), 1)
    gain1 = shift1 = query_b = value_b = jnp.zeros((1, width), F32)
    for g in range(4):
        block = jnp.concatenate(
            [in_q[g // 2, g % 2, k, :, 3 * SHARE - HEAD :].T for k in range(3)], axis=1
        )[HEAD : HEAD + 16]
        shift1 = shift1 + block[0:1].astype(F32)
        gain1 = gain1 + block[1:2].astype(F32)
        pick_q = jnp.where((row == col - g * SHARE) & (row < SHARE), 1.0, 0.0).astype(BF)
        pick_v = jnp.where(
            (row - 2 * SHARE == col - g * SHARE) & (row >= 2 * SHARE) & (row < 3 * SHARE), 1.0, 0.0
        ).astype(BF)
        query_b = query_b + dot(block, pick_q, NN)[2:3]
        value_b = value_b + dot(block, pick_v, NN)[2:3]
    for ref, value in (
        (g1_ref, gain1 / gain), (b1_ref, shift1), (qb_ref, query_b), (vb_ref, value_b),
        (ob_ref, rest[9:10]), (g2_ref, rest[10:11]), (b2_ref, rest[11:12]), (db_ref, rest[8:9]),
    ):
        ref[...] = (value * scale).reshape(width)
    ub_ref[...] = (jnp.concatenate([rest[f : f + 1, :BLOCK] for f in range(BLOCKS)], axis=1) * scale).reshape(
        BLOCKS * BLOCK
    )
    for k in range(3):
        for which in range(3):
            q_store(which, k).wait()
    for k in range(number_d - SLOTS, number_d):
        store_of(0, k).wait()
    for k in range(number_u - SLOTS, number_u):
        store_of(1, k).wait()


def finish_call(gain, h, dmid, dn, fd, fu, fq):
    width = h.shape[1]
    vm = pl.BlockSpec(memory_space=VM)
    hbm = pl.BlockSpec(memory_space=pl.ANY)
    dma = pltpu.SemaphoreType.DMA
    hidden = BLOCKS * BLOCK
    flat = jax.ShapeDtypeStruct((width, width), F32)
    line = jax.ShapeDtypeStruct((width,), F32)
    return pl.pallas_call(
        finish_kernel,
        name="finish",
        out_shape=[jax.ShapeDtypeStruct(h.shape, F32)]
        + [line] * 7
        + [jax.ShapeDtypeStruct((hidden,), F32), line]
        + [flat] * 4
        + [jax.ShapeDtypeStruct((width, hidden), F32), jax.ShapeDtypeStruct((hidden, width), F32)],
        in_specs=[vm] * 4 + [hbm] * 3,
        out_specs=[vm] * 10 + [hbm] * 6,
        scratch_shapes=[
            VM(fd.shape, BF), VM(fu.shape, BF), VM(fq.shape, BF),
            VM((SLOTS, 256, width), F32), VM((SLOTS, width, 256), F32), VM((3, width, width), F32),
            dma(fd.shape[:2]), dma(fu.shape[:2]), dma((4, 3)), dma((SLOTS,)), dma((SLOTS,)), dma((3, 3)),
        ],
        compiler_params=pltpu.CompilerParams(vmem_limit_bytes=56 * 2**20),
    )(gain, h, dmid, dn, fd, fu, fq)


def norm_rows(values):
    center = values - jnp.mean(values, axis=-1, keepdims=True)
    spread = jnp.mean(center * center, axis=-1, keepdims=True)
    return center * lax.rsqrt(spread + 1e-05)


def norm_affine(values, gain_vec, shift_vec):
    return norm_rows(values) * gain_vec + shift_vec


def left_product(left_mat, right_mat):
    return lax.dot_general(
        left_mat, right_mat, (((0,), (0,)), ((), ())), preferred_element_type=jnp.float32
    )


def right_product(left_mat, weight):
    return lax.dot_general(
        left_mat, weight, (((1,), (1,)), ((), ())), preferred_element_type=jnp.float32
    )


def slot_tags(first_row, count_rows, layout):
    begins_flat, finishes_flat, slot_rows, band_cap, band_count = layout
    slot_index = first_row + jnp.arange(count_rows, dtype=jnp.int32)
    owner = slot_index // slot_rows
    within = slot_index - owner * slot_rows
    member = within // band_cap
    offset = within - member * band_cap
    flat_code = member * band_count + owner
    all_codes = jnp.arange(begins_flat.shape[0], dtype=jnp.int32)
    hit_table = flat_code[:, None] == all_codes[None, :]
    begins = jnp.sum(jnp.where(hit_table, begins_flat[None, :], 0), axis=1)
    finish = jnp.sum(jnp.where(hit_table, finishes_flat[None, :], 0), axis=1)
    position = begins + offset
    return (member, position, position < finish, slot_index)


def allowed_pairs(query_tags, key_tags):
    query_member, query_position, query_valid, query_slot = query_tags
    key_member, key_position, key_valid, key_slot = key_tags
    same_slot = query_slot[:, None] == key_slot[None, :]
    causal = (query_member[:, None] == key_member[None, :]) & (
        key_position[None, :] <= query_position[:, None]
    )
    return same_slot | query_valid[:, None] & key_valid[None, :] & causal


def on_device(
    residual_in,
    exit_layer,
    band_edges,
    norm1_gain,
    norm1_bias,
    query_weight,
    query_bias,
    key_weight,
    value_weight,
    value_bias,
    out_weight,
    out_bias,
    norm2_gain,
    norm2_bias,
    up_weight,
    up_bias,
    down_weight,
    down_bias,
    cotangent,
):
    slot_rows = residual_in.shape[1]
    model_width = residual_in.shape[2]
    head_size = model_width // HEADS
    score_scale = head_size ** (-0.5)
    band_here = lax.axis_index("band")
    band_count = lax.axis_size("band")
    band_cap = slot_rows // band_edges.shape[1]
    finishes = jnp.concatenate([band_edges[0][:, 1:], band_edges[0][:, -1:] + band_cap], axis=1)
    layout = (band_edges[0].reshape(-1), finishes.reshape(-1), slot_rows, band_cap, band_count)
    own_tags = slot_tags(band_here * slot_rows, slot_rows, layout)
    active = ((exit_layer[0] >= LAYER) & own_tags[2]).astype(jnp.float32)[:, None]
    total_active = lax.psum(jnp.sum(active), ("band", "batch"))
    hidden_in = residual_in[0].astype(jnp.float32)
    normed_one, norm_one_back = jax.vjp(
        norm_affine, hidden_in, norm1_gain.astype(jnp.float32), norm1_bias.astype(jnp.float32)
    )
    normed_low = normed_one.astype(jnp.bfloat16)
    queries = (
        jnp.dot(normed_low, query_weight, preferred_element_type=jnp.float32)
        + query_bias.astype(jnp.float32)
    ).astype(jnp.bfloat16)
    keys_own = jnp.dot(normed_low, key_weight, preferred_element_type=jnp.float32).astype(
        jnp.bfloat16
    )
    values_own = (
        jnp.dot(normed_low, value_weight, preferred_element_type=jnp.float32)
        + value_bias.astype(jnp.float32)
    ).astype(jnp.bfloat16)
    query_heads = queries.reshape(slot_rows, HEADS, head_size)
    start_state = (
        jnp.full((HEADS, slot_rows), -1e30, jnp.float32),
        jnp.zeros((HEADS, slot_rows), jnp.float32),
        jnp.zeros((slot_rows, HEADS, head_size), jnp.float32),
    )
    key_piece = lax.all_gather(keys_own, "band", axis=0, tiled=True)
    value_piece = lax.all_gather(values_own, "band", axis=0, tiled=True)
    piece_rows = key_piece.shape[0]
    step_rows = min(piece_rows, slot_rows)

    def one_step(step_index, inner_state):
        offset_row = step_index * step_rows
        key_block = lax.dynamic_slice_in_dim(key_piece, offset_row, step_rows, 0).reshape(
            step_rows, HEADS, head_size
        )
        value_block = lax.dynamic_slice_in_dim(value_piece, offset_row, step_rows, 0).reshape(
            step_rows, HEADS, head_size
        )
        mask = allowed_pairs(own_tags, slot_tags(offset_row, step_rows, layout))

        def accumulate(running):
            top_old, total_old, sum_old = running
            scores = (
                jnp.einsum(
                    "qhd,khd->hqk", query_heads, key_block, preferred_element_type=jnp.float32
                )
                * score_scale
            )
            scores = jnp.where(mask[None], scores, -1e30)
            top_new = jnp.maximum(top_old, jnp.max(scores, axis=-1))
            rescale = jnp.exp(top_old - top_new)
            weights_new = jnp.where(mask[None], jnp.exp(scores - top_new[..., None]), 0.0)
            total_new = total_old * rescale + jnp.sum(weights_new, axis=-1)
            sum_new = sum_old * rescale.T[..., None] + jnp.einsum(
                "hqk,khd->qhd",
                weights_new.astype(jnp.bfloat16),
                value_block,
                preferred_element_type=jnp.float32,
            )
            return (top_new, total_new, sum_new)

        return lax.cond(jnp.any(mask), accumulate, lambda running: running, inner_state)

    top_score, weight_total, weighted_sum = lax.fori_loop(
        0, piece_rows // step_rows, one_step, start_state
    )
    attended = weighted_sum / weight_total.T[..., None]
    log_total = top_score + jnp.log(weight_total)
    mixed_low = attended.reshape(slot_rows, model_width).astype(jnp.bfloat16)
    branch = jnp.dot(mixed_low, out_weight, preferred_element_type=jnp.float32) + out_bias.astype(
        jnp.float32
    )
    middle = hidden_in + active * branch
    normed_two, norm_two_back = jax.vjp(
        norm_affine, middle, norm2_gain.astype(jnp.float32), norm2_bias.astype(jnp.float32)
    )
    normed_two_low = normed_two.astype(jnp.bfloat16)
    pre_act = jnp.dot(
        normed_two_low, up_weight, preferred_element_type=jnp.float32
    ) + up_bias.astype(jnp.float32)
    activated, gelu_back = jax.vjp(jax.nn.gelu, pre_act)
    activated_low = activated.astype(jnp.bfloat16)
    down_out = jnp.dot(
        activated_low, down_weight, preferred_element_type=jnp.float32
    ) + down_bias.astype(jnp.float32)
    layer_out = (middle + active * down_out).astype(jnp.bfloat16)[None]
    out_grad = cotangent[0].astype(jnp.float32)
    down_grad = (active * out_grad).astype(jnp.bfloat16)
    down_weight_sum = left_product(activated_low, down_grad)
    down_bias_sum = jnp.sum(down_grad.astype(jnp.float32), axis=0)
    (pre_grad,) = gelu_back(right_product(down_grad, down_weight))
    pre_low = pre_grad.astype(jnp.bfloat16)
    up_weight_sum = left_product(normed_two_low, pre_low)
    up_bias_sum = jnp.sum(pre_low.astype(jnp.float32), axis=0)
    middle_norm, gain_two_sum, shift_two_sum = norm_two_back(right_product(pre_low, up_weight))
    middle_grad = out_grad + middle_norm
    branch_grad = (active * middle_grad).astype(jnp.bfloat16)
    out_weight_sum = left_product(mixed_low, branch_grad)
    out_bias_sum = jnp.sum(branch_grad.astype(jnp.float32), axis=0)
    mixed_grad = right_product(branch_grad, out_weight).astype(jnp.bfloat16)
    grad_heads = mixed_grad.reshape(slot_rows, HEADS, head_size)
    delta_row = jnp.sum(grad_heads.astype(jnp.float32) * attended, axis=-1).T

    def pair_terms(query_blk, grad_blk, logsum_blk, delta_blk, key_block, value_block, mask):
        scores = (
            jnp.einsum("qhd,khd->hqk", query_blk, key_block, preferred_element_type=jnp.float32)
            * score_scale
        )
        probability = jnp.where(mask[None], jnp.exp(scores - logsum_blk[..., None]), 0.0)
        prob_grad = jnp.einsum(
            "qhd,khd->hqk", grad_blk, value_block, preferred_element_type=jnp.float32
        )
        score_grad = (probability * (prob_grad - delta_blk[..., None])).astype(jnp.bfloat16)
        return (probability.astype(jnp.bfloat16), score_grad)

    all_rows = slot_rows * band_count
    start_back = (
        jnp.zeros((slot_rows, HEADS, head_size), jnp.float32),
        jnp.zeros((all_rows, model_width), jnp.float32),
        jnp.zeros((all_rows, model_width), jnp.float32),
    )
    fold_key_piece = lax.all_gather(keys_own, "band", axis=0, tiled=True)
    fold_value_piece = lax.all_gather(values_own, "band", axis=0, tiled=True)
    piece_rows = fold_key_piece.shape[0]
    fold_step_rows = min(piece_rows, slot_rows)

    def one_step(step_index, inner_state):
        offset_row = step_index * fold_step_rows
        key_block = lax.dynamic_slice_in_dim(fold_key_piece, offset_row, fold_step_rows, 0).reshape(
            fold_step_rows, HEADS, head_size
        )
        value_block = lax.dynamic_slice_in_dim(
            fold_value_piece, offset_row, fold_step_rows, 0
        ).reshape(fold_step_rows, HEADS, head_size)
        mask = allowed_pairs(own_tags, slot_tags(offset_row, fold_step_rows, layout))

        def accumulate(running):
            query_acc, key_sums, value_sums = running
            prob_low, score_grad = pair_terms(
                query_heads, grad_heads, log_total, delta_row, key_block, value_block, mask
            )
            query_acc = (
                query_acc
                + jnp.einsum(
                    "hqk,khd->qhd", score_grad, key_block, preferred_element_type=jnp.float32
                )
                * score_scale
            )
            key_term = (
                jnp.einsum(
                    "hqk,qhd->khd", score_grad, query_heads, preferred_element_type=jnp.float32
                ).reshape(fold_step_rows, model_width)
                * score_scale
            )
            value_term = jnp.einsum(
                "hqk,qhd->khd", prob_low, grad_heads, preferred_element_type=jnp.float32
            ).reshape(fold_step_rows, model_width)
            key_sums = lax.dynamic_update_slice_in_dim(
                key_sums,
                lax.dynamic_slice_in_dim(key_sums, offset_row, fold_step_rows, 0) + key_term,
                offset_row,
                0,
            )
            value_sums = lax.dynamic_update_slice_in_dim(
                value_sums,
                lax.dynamic_slice_in_dim(value_sums, offset_row, fold_step_rows, 0) + value_term,
                offset_row,
                0,
            )
            return (query_acc, key_sums, value_sums)

        return lax.cond(jnp.any(mask), accumulate, lambda running: running, inner_state)

    back_state = lax.fori_loop(0, piece_rows // fold_step_rows, one_step, start_back)
    query_sum, key_sums_all, value_sums_all = back_state
    key_sum, value_sum = (
        lax.psum_scatter(
            key_sums_all.astype(jnp.bfloat16), "band", scatter_dimension=0, tiled=True
        ).astype(jnp.float32),
        lax.psum_scatter(
            value_sums_all.astype(jnp.bfloat16), "band", scatter_dimension=0, tiled=True
        ).astype(jnp.float32),
    )
    query_low = query_sum.reshape(slot_rows, model_width).astype(jnp.bfloat16)
    key_low = key_sum.astype(jnp.bfloat16)
    value_low = value_sum.astype(jnp.bfloat16)
    query_weight_sum = left_product(normed_low, query_low)
    query_bias_sum = jnp.sum(query_low.astype(jnp.float32), axis=0)
    key_weight_sum = left_product(normed_low, key_low)
    value_weight_sum = left_product(normed_low, value_low)
    value_bias_sum = jnp.sum(value_low.astype(jnp.float32), axis=0)
    normed_grad = (
        right_product(query_low, query_weight)
        + right_product(key_low, key_weight)
        + right_product(value_low, value_weight)
    )
    input_norm, gain_one_sum, shift_one_sum = norm_one_back(normed_grad)
    input_grad = (middle_grad + input_norm)[None]
    (
        total_g1,
        total_b1,
        total_qw,
        total_qb,
        total_kw,
        total_vw,
        total_vb,
        total_ow,
        total_ob,
        total_g2,
        total_b2,
        total_uw,
        total_ub,
        total_dw,
        total_db,
    ) = lax.psum(
        (
            gain_one_sum,
            shift_one_sum,
            query_weight_sum,
            query_bias_sum,
            key_weight_sum,
            value_weight_sum,
            value_bias_sum,
            out_weight_sum,
            out_bias_sum,
            gain_two_sum,
            shift_two_sum,
            up_weight_sum,
            up_bias_sum,
            down_weight_sum,
            down_bias_sum,
        ),
        ("band", "batch"),
    )
    return (
        layer_out,
        input_grad,
        total_g1 / total_active,
        total_b1 / total_active,
        total_qw / total_active,
        total_qb / total_active,
        total_kw / total_active,
        total_vw / total_active,
        total_vb / total_active,
        total_ow / total_active,
        total_ob / total_active,
        total_g2 / total_active,
        total_b2 / total_active,
        total_uw / total_active,
        total_ub / total_active,
        total_dw / total_active,
        total_db / total_active,
    )


def fast_device(
    residual_in, exit_layer, band_edges, norm1_gain, norm1_bias, query_weight, query_bias,
    key_weight, value_weight, value_bias, out_weight, out_bias, norm2_gain, norm2_bias,
    up_weight, up_bias, down_weight, down_bias, cotangent,
):
    h, cot = residual_in[0], cotangent[0]
    o, lse, att, wback, n1, n1t, q, kv, kt = attend_call(
        band_edges, norm1_gain, norm1_bias, query_bias, value_bias, h, query_weight, key_weight, value_weight
    )
    vecs = (norm1_bias, out_bias, norm2_gain, norm2_bias, down_bias, up_bias)
    dn, layer, dmid, fq, fd, fu = layer_call(
        band_edges, exit_layer, vecs, h, cot, att, o, lse, wback, out_weight,
        n1, n1t, q, kv, kt, up_weight, down_weight,
    )
    grad, g1, b1, qb, vb, ob, g2, b2, ub, db, qw, kw, vw, ow, uw, dw = finish_call(
        norm1_gain, h, dmid, dn, fd, fu, fq
    )
    return (layer[None], grad[None], g1, b1, qw, qb, kw, vw, vb, ow, ob, g2, b2, uw, ub, dw, db)


def solution(mesh):
    placed = (
        (P("batch", "band", None), P("batch", "band"), P("batch", None, None))
        + (P(),) * 15
        + (P("batch", "band", None),)
    )
    fast = mesh.shape["band"] == BANDS and mesh.shape["batch"] == 4
    return jax.shard_map(
        fast_device if fast else on_device,
        mesh=mesh,
        in_specs=placed,
        out_specs=(P("batch", "band", None),) * 2 + (P(),) * 15,
        check_vma=False,
    )
```

```python
import functools

import jax
import jax.numpy as jnp
from jax import lax
from jax.experimental import pallas as pl
from jax.experimental.pallas import tpu as pltpu
from jax.sharding import PartitionSpec as P

MESH = pl.DeviceIdType.MESH
VM = pltpu.VMEM
BF = jnp.bfloat16
F32 = jnp.float32
HEADS = 12
LAYER = 6
HEAD = 64
BANDS = 8
CAP = 256
HALF = 128
MINE = 3
SHARE = MINE * HEAD
NEG = -1e30


def place():
    band = lax.axis_index("band")
    return band, band // 4, (band // 2) % 2, band % 2


def device(y, x, core):
    return (y * 4 + x * 2 + core, lax.axis_index("batch"))


def push(src, dst, send, recv, target):
    return pltpu.make_async_remote_copy(
        src_ref=src, dst_ref=dst, send_sem=send, recv_sem=recv, device_id=target, device_id_type=MESH
    )


def greet_band():
    band, _, _, _ = place()
    barrier = pltpu.get_barrier_semaphore()
    for step in range(1, BANDS):
        other = (band + step) % BANDS
        pl.semaphore_signal(
            barrier, inc=1, device_id=(other, lax.axis_index("batch")), device_id_type=MESH
        )
    pl.semaphore_wait(barrier, BANDS - 1)


def dot(a, b, dims):
    return lax.dot_general(a, b, ((dims[0], dims[1]), ((), ())), preferred_element_type=F32)


NN = ((1,), (0,))
NT = ((1,), (1,))
TN = ((0,), (0,))


def as_row(ref):
    return ref[...].astype(F32).reshape(1, -1)


def counts_of(edges_ref, seq, band):
    after = edges_ref[0, seq, jnp.minimum(band + 1, BANDS - 1)]
    return jnp.where(band == BANDS - 1, CAP, after - edges_ref[0, seq, band])


def attend_kernel(
    edges_ref, gain_ref, shift_ref, bq_ref, bv_ref, h_ref, wq_hbm, wk_hbm, wv_hbm,
    o_ref, lse_ref, att_ref, wback_ref, n1_hbm, n1t_hbm, q_hbm, kv_hbm, kt_hbm,
    rows_ref, n1_ref, n1t_ref, q_ref, kv_ref, kvt_ref, cols_ref, turned_ref,
    send, recv, out_send, out_recv, load, store,
):
    band, y, x, core = place()
    width = h_ref.shape[1]
    group = 2 * x + core
    wide = pl.ds(pl.multiple_of(x * 2 * SHARE + core * 128, 128), 256)
    loads = [
        pltpu.make_async_copy(ref.at[:, wide], cols_ref.at[k], load.at[k])
        for k, ref in enumerate((wq_hbm, wk_hbm, wv_hbm))
    ]
    for copy in loads:
        copy.start()
    greet_band()
    own = pl.ds(pl.multiple_of(y * CAP, CAP), CAP)
    half = pl.ds(pl.multiple_of(core * HALF, HALF), HALF)
    other_y, other_x, other_core = 1 - y, 1 - x, 1 - core
    sibling = device(y, x, other_core)
    copies = {}

    def go(name, src, dst, index, recv_index, target):
        copy = push(src, dst, send.at[index], recv.at[recv_index], target)
        copy.start()
        copies[name] = copy

    for k in range(2):
        from_rows = pl.ds(pl.multiple_of(other_y * CAP + k * HALF, HALF), HALF)
        go(("y", k), h_ref.at[from_rows], rows_ref.at[band, pl.ds(k * HALF, HALF)], 1 + k, 1 + core,
           device(other_y, x, k))
    for k in range(2):
        from_rows = pl.ds(pl.multiple_of(y * CAP + k * HALF, HALF), HALF)
        go(("x", k), h_ref.at[from_rows], rows_ref.at[band, pl.ds(k * HALF, HALF)], 3 + k, 3 + core,
           device(y, other_x, k))
    go("sib", h_ref.at[own], rows_ref.at[band], 0, 0, sibling)

    gain, shift = as_row(gain_ref), as_row(shift_ref)
    for k, copy in enumerate(loads):
        copy.wait()
        turned_ref[k] = cols_ref[k].T
        for h in range(MINE):
            part = turned_ref[k, pl.ds(pl.multiple_of(core * HEAD + h * HEAD, HEAD), HEAD), :]
            at = k * SHARE + h * HEAD
            wback_ref[at : at + HEAD, :] = part
    row = lax.broadcasted_iota(jnp.int32, (3 * SHARE, width), 0)
    col = lax.broadcasted_iota(jnp.int32, (3 * SHARE, width), 1) - group * SHARE
    pick_q = jnp.where((row == col) & (row < SHARE), 1.0, 0.0).astype(BF)
    pick_v = jnp.where((row - 2 * SHARE == col) & (row >= 2 * SHARE), 1.0, 0.0).astype(BF)

    def spread_row(ref):
        return jnp.broadcast_to(as_row(ref), (8, width)).astype(BF)

    bias = (dot(pick_q, spread_row(bq_ref), NT) + dot(pick_v, spread_row(bv_ref), NT))[:, :1]

    def project(rows, which):
        wide_rows = rows.astype(F32)
        center = wide_rows - jnp.mean(wide_rows, axis=-1, keepdims=True)
        spread = jnp.mean(center * center, axis=-1, keepdims=True)
        n1 = (center * lax.rsqrt(spread + 1e-05) * gain + shift).astype(BF)
        at = pl.ds(pl.multiple_of(which * CAP, CAP), CAP)
        n1_ref[at, :] = n1
        n1t_ref[:, at] = n1.T
        all_t = dot(wback_ref[...], n1, NT) + bias
        qt = (all_t[:SHARE] * 0.125).astype(BF)
        kvt = all_t[SHARE:].astype(BF)
        for h in range(MINE):
            one = jnp.concatenate(
                [kvt[h * HEAD : (h + 1) * HEAD], kvt[SHARE + h * HEAD : SHARE + (h + 1) * HEAD]], axis=0
            )
            kvt_ref[h, :, at] = one
            kv_ref[h, at, :] = one.T
            q_ref[h, :HEAD, at] = qt[h * HEAD : (h + 1) * HEAD]
            q_ref[h, HEAD:, at] = jnp.zeros((HEAD, CAP), BF)

    def project_two(first_y, first_x):
        def one(k, carry):
            which = first_y * 4 + first_x * 2 + k
            project(rows_ref[which], which)
            return carry

        lax.fori_loop(0, 2, one, 0)

    rows_ref[band] = h_ref[own, :]

    def wait_recv(index, which, size=HALF):
        ref = rows_ref.at[which] if size == CAP else rows_ref.at[which, half]
        push(ref, ref, send.at[0], recv.at[index], sibling).wait_recv()

    wait_recv(0, y * 4 + x * 2 + other_core, CAP)
    project_two(y, x)
    for k in range(2):
        from_band = other_y * 4 + x * 2 + k
        wait_recv(1 + k, from_band)
        piece = rows_ref.at[from_band, half]
        go(("fx", k), piece, piece, 5 + k, 5 + k, device(y, other_x, core))
        go(("fs", k), piece, piece, 7 + k, 7 + k, sibling)
    for k in range(2):
        from_band = y * 4 + other_x * 2 + k
        wait_recv(3 + k, from_band)
        piece = rows_ref.at[from_band, half]
        go(("fs", 2 + k), piece, piece, 9 + k, 9 + k, sibling)
    for k in range(2):
        copies[("fs", k)].wait_recv()
    project_two(other_y, x)
    for k in range(2):
        copies[("fs", 2 + k)].wait_recv()
    project_two(y, other_x)
    for k in range(2):
        from_band = other_y * 4 + other_x * 2 + k
        copies[("fx", k)].wait_recv()
        piece = rows_ref.at[from_band, half]
        go(("fs", 4 + k), piece, piece, 11 + k, 11 + k, sibling)
    for k in range(2):
        copies[("fs", 4 + k)].wait_recv()
    project_two(other_y, other_x)
    stores = [
        pltpu.make_async_copy(src, dst, store.at[k])
        for k, (src, dst) in enumerate(
            ((n1_ref, n1_hbm), (n1t_ref, n1t_hbm), (q_ref, q_hbm), (kv_ref, kv_hbm), (kvt_ref.at[:, :HEAD], kt_hbm))
        )
    ]
    for copy in stores:
        copy.start()

    key_at = lax.broadcasted_iota(jnp.int32, (CAP, CAP), 0)
    query_at = lax.broadcasted_iota(jnp.int32, (CAP, CAP), 1)
    lane = lax.broadcasted_iota(jnp.int32, (1, CAP), 1)
    share = pl.ds(pl.multiple_of(group * SHARE, SHARE), SHARE)
    side = pl.ds(pl.multiple_of(y * CAP, CAP), CAP)
    for i in range(BANDS - 1, -1, -1):
        cols = pl.ds(i * CAP, CAP)

        def one_head(h, carry):
            qt = q_ref[h, :, cols]
            scores = []
            for j in range(i + 1):
                s = dot(kv_ref[h, j * CAP : (j + 1) * CAP, :], qt, NN)
                keep = key_at < counts_of(edges_ref, y, j)
                if i == j:
                    keep = keep & (key_at <= query_at)
                scores.append(jnp.where(keep, s, NEG))
            top = functools.reduce(jnp.maximum, [jnp.max(s, axis=0, keepdims=True) for s in scores])
            total = jnp.zeros((1, CAP), F32)
            mix = jnp.zeros((HEAD, CAP), F32)
            for j in range(i + 1):
                p = jnp.exp(scores[j] - top)
                total = total + jnp.sum(p, axis=0, keepdims=True)
                mix = mix + dot(kvt_ref[h, HEAD:, j * CAP : (j + 1) * CAP], p.astype(BF), NN)
            valid = lane < counts_of(edges_ref, y, i)
            mix = jnp.where(valid, mix / total, kvt_ref[h, HEAD:, cols].astype(F32))
            o_ref[i, pl.ds(pl.multiple_of(h * HEAD, HEAD), HEAD), :] = mix.astype(BF)
            lse_ref[h, i : i + 1, :] = jnp.where(valid, top + jnp.log(total), -NEG)
            return carry

        lax.fori_loop(0, MINE, one_head, 0)
        copy = push(o_ref.at[i], att_ref.at[share, side], out_send.at[i], out_recv.at[band],
                    (i, lax.axis_index("batch")))
        pl.when(band != i)(copy.start)
        local = pltpu.make_async_copy(o_ref.at[i], att_ref.at[share, side], out_recv.at[band])
        pl.when(band == i)(local.start)
    for i in range(BANDS):
        from_y, from_x, from_core = i // 4, (i // 2) % 2, i % 2
        ref = att_ref.at[pl.ds((2 * from_x + from_core) * SHARE, SHARE), pl.ds(from_y * CAP, CAP)]
        copy = push(o_ref.at[i], ref, out_send.at[i], out_recv.at[i], sibling)
        copy.wait_recv()
        pl.when(band != i)(copy.wait_send)
    for copy in copies.values():
        copy.wait_send()
    for copy in stores:
        copy.wait()


def attend_call(edges, gain, shift, bq, bv, h, wq, wk, wv):
    width = h.shape[1]
    seq = BANDS * CAP
    vm = pl.BlockSpec(memory_space=VM)
    hbm = pl.BlockSpec(memory_space=pl.ANY)
    return pl.pallas_call(
        attend_kernel,
        name="attend",
        out_shape=[
            jax.ShapeDtypeStruct((BANDS, SHARE, CAP), BF),
            jax.ShapeDtypeStruct((MINE, BANDS, CAP), F32),
            jax.ShapeDtypeStruct((width, 2 * CAP), BF),
            jax.ShapeDtypeStruct((3 * SHARE, width), BF),
            jax.ShapeDtypeStruct((seq, width), BF),
            jax.ShapeDtypeStruct((width, seq), BF),
            jax.ShapeDtypeStruct((MINE, 128, seq), BF),
            jax.ShapeDtypeStruct((MINE, seq, 128), BF),
            jax.ShapeDtypeStruct((MINE, HEAD, seq), BF),
        ],
        in_specs=[pl.BlockSpec(memory_space=pltpu.SMEM)] + [vm] * 5 + [hbm] * 3,
        out_specs=[vm] * 4 + [hbm] * 5,
        scratch_shapes=[
            VM((BANDS, CAP, width), BF),
            VM((seq, width), BF),
            VM((width, seq), BF),
            VM((MINE, 128, seq), BF),
            VM((MINE, seq, 128), BF),
            VM((MINE, 128, seq), BF),
            VM((3, width, 256), BF),
            VM((3, 256, width), BF),
            pltpu.SemaphoreType.DMA((13,)),
            pltpu.SemaphoreType.DMA((13,)),
            pltpu.SemaphoreType.DMA((BANDS,)),
            pltpu.SemaphoreType.DMA((BANDS,)),
            pltpu.SemaphoreType.DMA((3,)),
            pltpu.SemaphoreType.DMA((5,)),
        ],
        compiler_params=pltpu.CompilerParams(
            collective_id=0, has_side_effects=True, vmem_limit_bytes=56 * 2**20
        ),
    )(edges, gain, shift, bq, bv, h, wq, wk, wv)


BLOCK = 512
BLOCKS = 6
QLANES = 640
D_AXES = ('xyba', 'yxba', 'xyab', 'xbay', 'axyb', 'xyab', 'yxab', 'ayxb')
U_AXES = ('bayx', 'xbya', 'abyx', 'yxba', 'yxab', 'xyba')
Q_AXES = ('yab-xay', 'aby-bxa', 'yab-ayx')
SCHEDULE = {'m0': (0, 8), 'm1': (1, 9, 0), 'a1': (8,), 'm2': (2, 10, 1, 9), 'm3': (3, 11, 2, 10), 'p4': (0,), 'g4': (3,), 'm4': (4, 12, 11), 'p5': (1,), 'g5': (9, 4), 'm5': (5, 13, 12, 8, 0), 'a5': (10,), 'e': (5, 13, 2, 11), 'o': (6,), 's': (7, 3, 9, 4, 12, 1, 6, 8, 7, 0, 10), 'b70': (3,), 'b71': (2, 1, 9), 'b72': (5, 7, 0, 3), 'd7': (6,), 'b60': (13, 2, 8, 10, 1, 9), 'b61': (5, 11, 0), 'b62': (4, 7), 'd6': (12, 2, 3), 'b50': (5,), 'b51': (13, 6, 1), 'b52': (11, 12, 8, 10, 2, 9), 'd5': (7, 3, 4, 0), 'b40': (5,), 'b41': (6, 13, 11, 8, 1), 'b42': (12, 10), 'b30': (2,), 'b32': (9,), 'd3': (0,), 'b20': (7, 5), 'b22': (1,), 'd2': (13, 0), 'b10': (3,), 'b12': (2, 1), 'd1': (4, 8, 12), 'd0': (6, 5, 2), 'q0': (14, 11, 9), 'q1': (15,), 'q2': (16, 4, 7, 9), 'end': (10, 6, 13, 3, 15, 14, 3, 16, 12, 10, 7, 10, 8, 14, 13, 8, 16, 15, 5, 12, 5, 11, 7, 12, 15, 4, 7, 14, 6, 16, 11, 11, 13, 15, 14, 13, 4, 6, 16, 4, 6, 15, 14, 16, 15, 14, 15, 16, 14, 16)}


def partners():
    band, y, x, core = place()
    z = lax.axis_index("batch")
    return {
        "core": (core, device(y, x, 1 - core)),
        "x": (x, device(y, 1 - x, core)),
        "y": (y, device(1 - y, x, core)),
        "a": (z % 2, (band, z + 1 - 2 * (z % 2))),
        "b": (z // 2, (band, (z + 2) % 4)),
    }


class Chain:
    def __init__(self, send, recv, free, store):
        self.send, self.recv, self.free, self.finish = send, recv, free, store
        self.links = partners()
        self.steps = []
        self.at = 0

    def halve(self, piece, rows, axes, landing):
        start, spans = 0, {}
        first = len(self.steps)
        for level, axis in enumerate(axes[:-1]):
            rows //= 2
            bit = self.links[axis][0]
            keep, give = (start + bit * rows, rows), (start + (1 - bit) * rows, rows)
            self.steps.append(
                (axis, piece(give), landing[level], landing[level], piece(keep), first + level, None)
            )
            start = keep[0]
            spans[axis] = (keep, give, first + level)
        mine = piece((start, rows))
        self.steps.append((axes[-1], mine, landing[-1], landing[-1], mine, None, None))
        return spans

    def copy(self, number, arrival=False):
        axis, src, dst, got = self.steps[number][:4]
        if arrival:
            src = dst = got
        return push(src, dst, self.send.at[number], self.recv.at[number], self.links[axis][1])

    def add(self, target, source):
        rows, lanes = source.shape
        size = 32 if lanes < 512 and rows % 32 == 0 else 16

        def some(r, carry):
            at = pl.ds(pl.multiple_of(r * size, size), size)
            target[at, :] = (target[at, :].astype(F32) + source[at, :].astype(F32)).astype(BF)
            return carry

        lax.fori_loop(0, rows // size, some, 0)

    def advance(self):
        number, self.at = self.at, self.at + 1
        if number > 0:
            axis, _, _, got, add, frees, _ = self.steps[number - 1]
            self.copy(number - 1, True).wait_recv()
            if add is not None:
                self.copy(number - 1).wait_send()
                if frees is not None:
                    pl.semaphore_signal(
                        self.free.at[frees], inc=1, device_id=self.links[axis][1], device_id_type=MESH
                    )
                self.add(add, got)
        if number < len(self.steps):
            freed = self.steps[number][6]
            if freed is not None:
                pl.semaphore_wait(self.free.at[freed], 1)
            self.copy(number).start()
        else:
            self.finish.start()

    def drain(self):
        for number, step in enumerate(self.steps):
            if step[4] is None:
                self.copy(number).wait_send()
        self.finish.wait()


def weight_chain(total, landing, send, recv, free, index, axes, out, out_sem):
    core = lax.axis_index("band") % 2
    chain = Chain(
        send.at[index], recv.at[index], free.at[index],
        pltpu.make_async_copy(total.at[index], out.at[index], out_sem.at[index]),
    )
    mine, other, first = total.at[index, core], total.at[index, 1 - core], landing[0].at[index]
    chain.steps.append(("core", other, first, first, mine, 0, None))

    def piece(span):
        return total.at[index, core, pl.ds(pl.multiple_of(span[0], 16), span[1])]

    spans = chain.halve(piece, total.shape[2], axes, [spot.at[index] for spot in landing[1:]])
    for axis in axes[-2::-1]:
        keep, give, level = spans[axis]
        chain.steps.append((axis, piece(keep), piece(keep), piece(give), None, None, level))
    chain.steps.append(("core", mine, mine, other, None, None, 0))
    return chain


def head_chain(total, landing, send, recv, free, index, axes, out, out_sem):
    _, _, x, core = place()
    chain = Chain(
        send.at[index], recv.at[index], free.at[index],
        pltpu.make_async_copy(total.at[:, :, index], out.at[:, :, index], out_sem.at[index]),
    )

    def piece(span, which="own"):
        rows = pl.ds(pl.multiple_of(span[0], 16), span[1])
        if which == "both":
            return total.at[:, core, index, rows]
        return total.at[x if which == "own" else 1 - x, core, index, rows]

    axes, tail = axes.split("-")
    spans = chain.halve(piece, total.shape[3], axes, [spot.at[index] for spot in landing])
    held, which = spans[axes[-2]][0], "own"
    for axis in tail:
        if axis == "x":
            mine = piece(held)
            chain.steps.append(("x", mine, mine, piece(held, "other"), None, None, None))
            which = "both"
            continue
        keep, give, level = spans[axis]
        chain.steps.append((axis, piece(keep, which), piece(keep, which), piece(give, which), None, None, level))
        outer = axes.index(axis) - 1
        held = spans[axes[outer]][0] if outer >= 0 else (0, total.shape[3])
    both = total.at[:, core, index]
    chain.steps.append(("core", both, both, total.at[:, 1 - core, index], None, None, None))
    return chain


def layer_kernel(
    edges_ref, exit_ref, shift1_ref, bo_ref, g2_ref, b2_ref, bd_ref, ub_ref,
    h_ref, cot_ref, att_ref, o_ref, lse_ref, wback_ref, wout_ref,
    n1_hbm, n1t_hbm, q_hbm, kv_hbm, kt_hbm, wup_hbm, wdown_hbm,
    dn_ref, layer_hbm, dmid_hbm, fq_hbm, fd_hbm, fu_hbm,
    gd_ref, gu_ref, fq_ref, d0, d1, d2, d3, d4, u0, u1, u2, u3, u4, q1, q2, q3,
    layer_ref, dmid_ref, q_ref, kv_ref, kt_ref, dz_ref, da_ref, do_ref, sib_out, sib_in, row_out,
    d_send, d_recv, d_free, d_out, u_send, u_recv, u_free, u_out, q_send, q_recv, q_free, q_out,
    do_send, do_recv, sib_send, sib_recv, dn_send, dn_recv, load, wload, out_sem,
):
    band, y, x, core = place()
    batch = lax.axis_index("batch")
    links = partners()
    sibling = links["core"][1]
    width = h_ref.shape[1]
    loads = [
        pltpu.make_async_copy(q_hbm, q_ref, load.at[0]),
        pltpu.make_async_copy(kv_hbm, kv_ref, load.at[1]),
        pltpu.make_async_copy(kt_hbm, kt_ref, load.at[2]),
    ]
    barrier = pltpu.get_barrier_semaphore()
    for step in range(1, BANDS):
        pl.semaphore_signal(barrier, inc=1, device_id=((band + step) % BANDS, batch), device_id_type=MESH)
    for axis in ("a", "b"):
        pl.semaphore_signal(barrier, inc=1, device_id=links[axis][1], device_id_type=MESH)

    chains = [
        weight_chain(gd_ref, (d0, d1, d2, d3, d4), d_send, d_recv, d_free, k, D_AXES[k], fd_hbm, d_out)
        for k in range(BLOCKS + 2)
    ] + [
        weight_chain(gu_ref, (u0, u1, u2, u3, u4), u_send, u_recv, u_free, k, U_AXES[k], fu_hbm, u_out)
        for k in range(BLOCKS)
    ] + [
        head_chain(fq_ref, (q1, q2, q3), q_send, q_recv, q_free, k, Q_AXES[k], fq_hbm, q_out) for k in range(3)
    ]
    layer_out = pltpu.make_async_copy(layer_ref, layer_hbm, out_sem.at[0])
    dmid_out = pltpu.make_async_copy(dmid_ref, dmid_hbm, out_sem.at[1])

    def serve(point):
        for k in SCHEDULE.get(point, ()):
            chains[k].advance()

    lane = lax.broadcasted_iota(jnp.int32, (1, 2 * CAP), 1)
    limit = jnp.where(lane < CAP, counts_of(edges_ref, 0, band), counts_of(edges_ref, 1, band) + CAP)
    active_row = jnp.where((exit_ref[...] >= LAYER) & (lane < limit), 1.0, 0.0)
    active = jnp.broadcast_to(active_row, (8, 2 * CAP)).T[:, :1]

    def feed_forward(mid_ref, sum_ref, dn2_ref, n2_ref, n2t_ref, wu, wd, pre_ref, dact_ref, act_ref, dpre_ref, part_ref, row_ref):
        def weights(f):
            at = pl.ds(f * BLOCK, BLOCK)
            return (
                pltpu.make_async_copy(wup_hbm.at[:, at], wu.at[f % 2], wload.at[0, f % 2]),
                pltpu.make_async_copy(wdown_hbm.at[at], wd.at[f % 2], wload.at[1, f % 2]),
            )

        for copy in weights(0):
            copy.start()
        for copy in loads:
            copy.start()
        branch = dot(att_ref[...], wout_ref[...], TN) + as_row(bo_ref)
        middle = h_ref[...].astype(F32) + active * branch
        mid_ref[...] = middle
        center = middle - jnp.mean(middle, axis=-1, keepdims=True)
        spread = jnp.mean(center * center, axis=-1, keepdims=True)
        scale2 = lax.rsqrt(spread + 1e-05)
        n2 = (center * scale2 * as_row(g2_ref) + as_row(b2_ref)).astype(BF)
        n2_ref[...] = n2
        n2t_ref[...] = n2.T
        dz_ref[...] = (active * cot_ref[...].astype(F32)).astype(BF)
        up_row = as_row(ub_ref)
        row_ref[...] = jnp.zeros_like(row_ref)
        sum_ref[...] = jnp.zeros_like(sum_ref)
        dn2_ref[...] = jnp.zeros_like(dn2_ref)
        for f in range(BLOCKS):
            if f + 1 < BLOCKS:
                for copy in weights(f + 1):
                    copy.start()
            for copy in weights(f):
                copy.wait()
            slot = f % 2
            pre_ref[...] = dot(n2_ref[...], wu[slot], NN)
            dact_ref[...] = dot(dz_ref[...], wd[slot], NT)
            serve(f'p{f}')
            up_bias = up_row[:, f * BLOCK : (f + 1) * BLOCK]
            part_ref[...] = jnp.zeros_like(part_ref)

            def rows(r, carry):
                at = pl.ds(pl.multiple_of(r * 64, 64), 64)
                pre = pre_ref[at, :] + up_bias
                square = pre * pre
                t = jnp.tanh(0.7978845608028654 * pre * (1.0 + 0.044715 * square))
                half = 0.5 * (1.0 + t)
                slope = half + (0.5 * 0.7978845608028654) * pre * (1.0 - t * t) * (1.0 + 0.134145 * square)
                act_ref[at, :] = (pre * half).astype(BF)
                dpre = (dact_ref[at, :] * slope).astype(BF)
                dpre_ref[at, :] = dpre
                part_ref[...] += jnp.sum(dpre.astype(F32).reshape(8, 8, BLOCK), axis=0)
                return carry

            lax.fori_loop(0, 2 * CAP // 64, rows, 0)
            serve(f'g{f}')
            down = dot(act_ref[...], dz_ref[...], TN).astype(BF)
            gd_ref[f, 0] = down[: BLOCK // 2]
            gd_ref[f, 1] = down[BLOCK // 2 :]
            up = dot(n2t_ref[...], dpre_ref[...], NN).astype(BF)
            gu_ref[f, 0] = up[:, : BLOCK // 2]
            gu_ref[f, 1] = up[:, BLOCK // 2 :]
            row_ref[f : f + 1, :BLOCK] = jnp.sum(part_ref[...], axis=0, keepdims=True)
            if f == 0:
                pl.semaphore_wait(barrier, BANDS + 1)
            serve(f'm{f}')
            sum_ref[...] += dot(act_ref[...], wd[slot], NN)
            dn2_ref[...] += dot(dpre_ref[...], wu[slot], NT)
            serve(f'a{f}')
        middle = mid_ref[...]
        center = middle - jnp.mean(middle, axis=-1, keepdims=True)
        spread = jnp.mean(center * center, axis=-1, keepdims=True)
        scale2 = lax.rsqrt(spread + 1e-05)
        xhat = center * scale2
        dn2 = dn2_ref[...]
        e2 = dn2 * as_row(g2_ref)
        dmid = cot_ref[...].astype(F32) + scale2 * (
            e2 - jnp.mean(e2, axis=-1, keepdims=True) - xhat * jnp.mean(e2 * xhat, axis=-1, keepdims=True)
        )
        dmid_ref[...] = dmid
        da = (active * dmid).astype(BF)
        n2_ref[...] = da
        da_ref[...] = dot(wout_ref[...], da, NT).astype(BF)
        for i in range(BANDS):
            copy = push(part_for(i), do_ref.at[band], do_send.at[i], do_recv.at[band], (i, batch))
            pl.when(band != i)(copy.start)
            local = pltpu.make_async_copy(part_for(i), do_ref.at[band], do_recv.at[band])
            pl.when(band == i)(local.start)
        dmid_out.start()
        row_ref[10:11, :] = jnp.sum(dn2 * xhat, axis=0, keepdims=True)
        serve('e')
        out = dot(att_ref[...], n2_ref[...], NN).astype(BF)
        gd_ref[BLOCKS, 0] = out[:256]
        gd_ref[BLOCKS, 1] = out[256:512]
        gd_ref[BLOCKS + 1, 0] = out[512:]
        serve('o')
        layer_ref[...] = (mid_ref[...] + active * (sum_ref[...] + as_row(bd_ref))).astype(BF)
        layer_out.start()
        count = jnp.sum(active_row)
        big = jnp.floor(count * (1.0 / 64.0))
        mid = jnp.floor((count - 64.0 * big) * 0.125)
        small = count - 64.0 * big - 8.0 * mid
        at = lax.broadcasted_iota(jnp.int32, (1, width), 1)
        digits = jnp.where(at == 0, big, jnp.where(at == 1, mid, jnp.where(at == 2, small, 0.0)))
        row_ref[8:9, :] = jnp.sum(dz_ref[...].astype(F32), axis=0, keepdims=True)
        row_ref[9:10, :] = jnp.sum(n2_ref[...].astype(F32), axis=0, keepdims=True)
        row_ref[11:12, :] = jnp.sum(dn2_ref[...], axis=0, keepdims=True)
        row_ref[12:13, :] = digits
        gd_ref[BLOCKS + 1, 1, :16, :] = row_ref[...].astype(BF)
        serve('s')

    def part_for(i):
        to_y, to_x, to_core = i // 4, (i // 2) % 2, i % 2
        return da_ref.at[pl.ds((2 * to_x + to_core) * SHARE, SHARE), pl.ds(to_y * CAP, CAP)]

    gd_ref[BLOCKS + 1, 1] = jnp.zeros(gd_ref.shape[2:], BF)
    rows2 = 2 * CAP
    pl.run_scoped(
        feed_forward,
        VM((rows2, width), F32), VM((rows2, width), F32), VM((rows2, width), F32),
        VM((rows2, width), BF), VM((width, rows2), BF),
        VM((2, width, BLOCK), BF), VM((2, BLOCK, width), BF),
        VM((rows2, BLOCK), F32), VM((rows2, BLOCK), F32), VM((rows2, BLOCK), BF), VM((rows2, BLOCK), BF),
        VM((8, BLOCK), F32), VM((16, width), F32),
    )
    half = pl.ds(pl.multiple_of(core * HALF, HALF), HALF)
    key_at = lax.broadcasted_iota(jnp.int32, (CAP, CAP), 0)
    query_at = lax.broadcasted_iota(jnp.int32, (CAP, CAP), 1)

    def sib_copy(i):
        return push(sib_out.at[i % 2], sib_in.at[i], sib_send.at[i], sib_recv.at[i], sibling)

    def dn_copy(i):
        return push(row_out.at[i % 2], dn_ref.at[y, x, half], dn_send.at[i], dn_recv.at[band], (i, batch))

    def dn_local(i):
        return pltpu.make_async_copy(row_out.at[i % 2], dn_ref.at[y, x, half], dn_recv.at[band])

    def backward(dk_ref, d_ref, mine_ref, n1_ref, n1t_ref, small_ref):
        turned_load = pltpu.make_async_copy(n1t_hbm, n1t_ref, load.at[3])
        turned_load.start()

        def rows_load(i):
            return pltpu.make_async_copy(n1_hbm.at[pl.ds(i * CAP, CAP)], n1_ref.at[i % 2], load.at[4 + i % 2])

        rows_load(BANDS - 1).start()

        def finish(i):
            sib_copy(i).wait_recv()
            if i + 2 < BANDS:
                pl.when(band != i + 2)(dn_copy(i + 2).wait_send)

                @pl.when(band == i + 2)
                def _():
                    push(row_out.at[0], dn_ref.at[y, x, half], dn_send.at[0], dn_recv.at[band], sibling).wait_recv()

            row_out[i % 2] = (mine_ref[i % 2] + sib_in[i].astype(F32)).astype(BF)
            pl.when(band != i)(dn_copy(i).start)
            pl.when(band == i)(dn_local(i).start)

        dk_ref[...] = jnp.zeros_like(dk_ref)
        small_ref[...] = jnp.zeros_like(small_ref)
        for copy in loads:
            copy.wait()
        for i in range(BANDS - 1, -1, -1):
            cols = pl.ds(i * CAP, CAP)
            push(do_ref.at[i], do_ref.at[i], do_send.at[i], do_recv.at[i], sibling).wait_recv()

            def one_head(h, carry):
                qt = q_ref[h, :, cols]
                dot_t = do_ref[i, pl.ds(h * HEAD, HEAD), :]
                dop = jnp.concatenate([jnp.zeros_like(dot_t), dot_t], axis=0)
                lse = lse_ref[h, i : i + 1, :]
                o = o_ref[i, pl.ds(h * HEAD, HEAD), :]
                delta = jnp.sum(dot_t.astype(F32) * o.astype(F32), axis=0, keepdims=True)
                dq = jnp.zeros((HEAD, CAP), F32)
                for j in range(i + 1):
                    at = pl.ds(j * CAP, CAP)
                    kv = kv_ref[h, at, :]
                    s = dot(kv, qt, NN)
                    dp = dot(kv, dop, NN)
                    keep = key_at < counts_of(edges_ref, y, j)
                    if i == j:
                        keep = keep & (key_at <= query_at)
                    p = jnp.where(keep, jnp.exp(s - lse), 0.0)
                    if i == j:
                        alone = (key_at == query_at) & (query_at >= counts_of(edges_ref, y, i))
                        p = jnp.where(alone, 1.0, p)
                    ds = (p * (dp - delta)).astype(BF)
                    dq = dq + dot(kt_ref[h, :, at], ds, NN)
                    dk_ref[h, at, :] += dot(ds, qt, NT) + dot(p.astype(BF), dop, NT)
                d_ref[pl.ds(h * HEAD, HEAD), cols] = (dq * 0.125).astype(BF)
                pair = dk_ref[h, cols, :].T.astype(BF)
                d_ref[pl.ds(SHARE + h * HEAD, HEAD), cols] = pair[:HEAD]
                d_ref[pl.ds(2 * SHARE + h * HEAD, HEAD), cols] = pair[HEAD:]
                return carry

            for h in range(MINE):
                one_head(h, 0)
                serve(f'b{i}{h}')
            rows_load(i).wait()
            if i > 0:
                rows_load(i - 1).start()
            dn = dot(d_ref[:, cols], wback_ref[...], TN)
            centered = n1_ref[i % 2].astype(F32) - as_row(shift1_ref)
            small_ref[0:1, :] += jnp.sum(dn, axis=0, keepdims=True)
            small_ref[1:2, :] += jnp.sum(dn * centered, axis=0, keepdims=True)
            mine_ref[2] = dn[:HALF]
            mine_ref[3] = dn[HALF:]
            if i + 2 < BANDS:
                sib_copy(i + 2).wait_send()
            sib_out[i % 2] = mine_ref[2 + (1 - core)].astype(BF)
            mine_ref[i % 2] = mine_ref[2 + core]
            sib_copy(i).start()
            if i < BANDS - 1:
                finish(i + 1)
            serve(f'd{i}')
        turned_load.wait()
        small_ref[2:3, : 3 * SHARE] = dot(jnp.ones((8, d_ref.shape[1]), BF), d_ref[...], NT)[:1]
        turned = small_ref[...].T.astype(BF)
        for k in range(3):
            rows = slice(k * 256, (k + 1) * 256)
            fq_ref[x, core, k, :, : 3 * SHARE] = dot(n1t_ref[rows, :], d_ref[...], NT).astype(BF)
            fq_ref[x, core, k, :, 3 * SHARE :] = jnp.concatenate(
                [turned[rows], jnp.zeros((256, QLANES - 3 * SHARE - 8), BF)], axis=1
            )
            serve(f'q{k}')
        finish(0)

    pl.run_scoped(
        backward,
        VM((MINE, BANDS * CAP, 128), F32),
        VM((3 * SHARE, BANDS * CAP), BF),
        VM((4, HALF, width), F32),
        VM((2, CAP, width), BF),
        VM((width, BANDS * CAP), BF),
        VM((8, width), F32),
    )
    serve('end')
    left = [[k] * (len(chain.steps) + 1 - chain.at) for k, chain in enumerate(chains)]
    while any(left):
        for k, rest in enumerate(left):
            if rest:
                chains[rest.pop()].advance()

    for i in range(BANDS):
        copy = push(part_for(i), do_ref.at[i], do_send.at[i], do_recv.at[i], sibling)
        pl.when(band != i)(copy.wait_send)
        if i < 2:
            sib_copy(i).wait_send()
            pl.when(band != i)(dn_copy(i).wait_send)
    for i in range(BANDS):
        from_y, from_x, from_core = i // 4, i // 2 % 2, i % 2
        arrived = push(row_out.at[0], dn_ref.at[from_y, from_x, pl.ds(from_core * HALF, HALF)],
                       dn_send.at[i], dn_recv.at[i], sibling)
        if i < 2:
            arrived.wait_recv()
        else:
            pl.when(band != i)(arrived.wait_recv)
    for chain in chains:
        chain.drain()
    layer_out.wait()
    dmid_out.wait()


def layer_call(edges, exits, vecs, h, cot, att, o, lse, wback, wout, n1, n1t, q, kv, kt, wup, wdown):
    width = h.shape[1]
    seq = BANDS * CAP
    vm = pl.BlockSpec(memory_space=VM)
    hbm = pl.BlockSpec(memory_space=pl.ANY)
    dma, credit = pltpu.SemaphoreType.DMA, pltpu.SemaphoreType.REGULAR
    eight = dma((BANDS,))

    def room(*shape):
        return VM(shape, BF)

    def spots(number, rows, lanes, levels):
        return [room(number, rows // 2**k, lanes) for k in levels]

    def sems(number, steps, levels):
        return [dma((number, steps)), dma((number, steps)), credit((number, levels)), dma((number,))]

    parts_d, parts_u = BLOCKS + 2, BLOCKS
    return pl.pallas_call(
        layer_kernel,
        name="layer",
        out_shape=[
            jax.ShapeDtypeStruct((2, 2, CAP, width), BF),
            jax.ShapeDtypeStruct(h.shape, BF),
            jax.ShapeDtypeStruct(h.shape, F32),
            jax.ShapeDtypeStruct((2, 2, 3, 256, QLANES), BF),
            jax.ShapeDtypeStruct((parts_d, 2, 256, width), BF),
            jax.ShapeDtypeStruct((parts_u, 2, width, 256), BF),
        ],
        in_specs=[pl.BlockSpec(memory_space=pltpu.SMEM)] + [vm] * 14 + [hbm] * 7,
        out_specs=[vm] + [hbm] * 5,
        scratch_shapes=[room(parts_d, 2, 256, width), room(parts_u, 2, width, 256), room(2, 2, 3, 256, QLANES)]
        + spots(parts_d, 256, width, (0, 1, 2, 3, 3))
        + spots(parts_u, width, 256, (0, 1, 2, 3, 3))
        + spots(3, 256, QLANES, (1, 2, 2))
        + [
            room(*h.shape), VM(h.shape, F32),
            room(MINE, 128, seq), room(MINE, seq, 128), room(MINE, HEAD, seq),
            room(2 * CAP, width), room(width, 2 * CAP), room(BANDS, SHARE, CAP),
            room(2, HALF, width), room(BANDS, HALF, width), room(2, HALF, width),
        ]
        + sems(parts_d, 9, 5) + sems(parts_u, 9, 5) + sems(3, 7, 3)
        + [eight] * 6 + [dma((6,)), dma((2, 2)), dma((2,))],
        compiler_params=pltpu.CompilerParams(
            collective_id=1, has_side_effects=True, vmem_limit_bytes=63 * 2**20
        ),
    )(edges, exits, *vecs, h, cot, att, o, lse, wback, wout, n1, n1t, q, kv, kt, wup, wdown)


SLOTS = 6


def finish_kernel(
    gain_ref, h_ref, dmid_ref, dn_ref, fd_hbm, fu_hbm, fq_hbm,
    grad_ref, g1_ref, b1_ref, qb_ref, vb_ref, ob_ref, g2_ref, b2_ref, ub_ref, db_ref,
    qw_hbm, kw_hbm, vw_hbm, ow_hbm, uw_hbm, dw_hbm,
    in_d, in_u, in_q, out_d, out_u, square, load_d, load_u, load_q, store_d, store_u, store_q,
):
    width = h_ref.shape[1]
    tail = (BLOCKS + 1, 1)
    halves_d = [tail] + [(f, c) for f in range(BLOCKS + 2) for c in range(2) if (f, c) != tail]
    halves_u = [(f, c) for f in range(BLOCKS) for c in range(2)]

    def load_of(kind, f, c):
        src, dst, sem = ((fd_hbm, in_d, load_d), (fu_hbm, in_u, load_u))[kind]
        return pltpu.make_async_copy(src.at[f, c], dst.at[f, c], sem.at[f, c])

    def q_load(g, k):
        return pltpu.make_async_copy(
            fq_hbm.at[g // 2, g % 2, k], in_q.at[g // 2, g % 2, k], load_q.at[g, k]
        )

    for k in range(max(len(halves_d), len(halves_u))):
        if k < len(halves_d):
            load_of(0, *halves_d[k]).start()
        if k < len(halves_u):
            load_of(1, *halves_u[k]).start()
    for k in range(3):
        for g in range(4):
            q_load(g, k).start()

    load_of(0, *tail).wait()
    rest = in_d[tail[0], tail[1], :16, :].astype(F32)
    count = rest[12:13, :3]
    total = 64.0 * count[:, 0:1] + 8.0 * count[:, 1:2] + count[:, 2:3]
    scale = 1.0 / total

    def store_of(kind, k):
        if kind == 0:
            f, c = halves_d[1:][k]
            row = f * BLOCK + c * 256
            target = dw_hbm.at[pl.ds(row, 256)] if f < BLOCKS else ow_hbm.at[pl.ds(row - BLOCKS * BLOCK, 256)]
            return pltpu.make_async_copy(out_d.at[k % SLOTS], target, store_d.at[k % SLOTS])
        f, c = halves_u[k]
        target = uw_hbm.at[:, pl.ds(f * BLOCK + c * 256, 256)]
        return pltpu.make_async_copy(out_u.at[k % SLOTS], target, store_u.at[k % SLOTS])

    def convert(kind, k):
        f, c = halves_u[k] if kind else halves_d[1:][k]
        source, out = ((in_d, out_d), (in_u, out_u))[kind]
        load_of(kind, f, c).wait()
        if k >= SLOTS:
            store_of(kind, k - SLOTS).wait()
        step = 32 if kind == 0 else 96

        def some(r, carry):
            at = pl.ds(pl.multiple_of(r * step, step), step)
            out[k % SLOTS, at, :] = source[f, c, at, :].astype(F32) * scale
            return carry

        lax.fori_loop(0, source.shape[2] // step, some, 0)
        store_of(kind, k).start()

    number_d, number_u = len(halves_d) - 1, len(halves_u)
    for k in range(max(number_d, number_u)):
        if k < number_d:
            convert(0, k)
        if k < number_u:
            convert(1, k)

    outs = (qw_hbm, kw_hbm, vw_hbm)

    def q_store(which, k):
        rows = pl.ds(k * 256, 256)
        return pltpu.make_async_copy(square.at[which, rows], outs[which].at[rows], store_q.at[which, k])

    for k in range(3):
        for g in range(4):
            q_load(g, k).wait()
        for which in range(3):
            square[which, k * 256 : (k + 1) * 256, :] = jnp.concatenate(
                [
                    in_q[g // 2, g % 2, k, :, which * SHARE : (which + 1) * SHARE].astype(F32) * scale
                    for g in range(4)
                ],
                axis=1,
            )
            q_store(which, k).start()

    hidden = h_ref[...].astype(F32)
    center = hidden - jnp.mean(hidden, axis=-1, keepdims=True)
    spread = jnp.mean(center * center, axis=-1, keepdims=True)
    scale1 = lax.rsqrt(spread + 1e-05)
    xhat = center * scale1
    dn1 = jnp.concatenate([dn_ref[s, 0].astype(F32) + dn_ref[s, 1].astype(F32) for s in range(2)], axis=0)
    gain = as_row(gain_ref)
    e1 = dn1 * gain
    grad_ref[...] = dmid_ref[...] + scale1 * (
        e1 - jnp.mean(e1, axis=-1, keepdims=True) - xhat * jnp.mean(e1 * xhat, axis=-1, keepdims=True)
    )

    row = lax.broadcasted_iota(jnp.int32, (width, width), 0)
    col = lax.broadcasted_iota(jnp.int32, (width, width), 1)
    gain1 = shift1 = query_b = value_b = jnp.zeros((1, width), F32)
    for g in range(4):
        block = jnp.concatenate(
            [in_q[g // 2, g % 2, k, :, 3 * SHARE - HEAD :].T for k in range(3)], axis=1
        )[HEAD : HEAD + 16]
        shift1 = shift1 + block[0:1].astype(F32)
        gain1 = gain1 + block[1:2].astype(F32)
        pick_q = jnp.where((row == col - g * SHARE) & (row < SHARE), 1.0, 0.0).astype(BF)
        pick_v = jnp.where(
            (row - 2 * SHARE == col - g * SHARE) & (row >= 2 * SHARE) & (row < 3 * SHARE), 1.0, 0.0
        ).astype(BF)
        query_b = query_b + dot(block, pick_q, NN)[2:3]
        value_b = value_b + dot(block, pick_v, NN)[2:3]
    for ref, value in (
        (g1_ref, gain1 / gain), (b1_ref, shift1), (qb_ref, query_b), (vb_ref, value_b),
        (ob_ref, rest[9:10]), (g2_ref, rest[10:11]), (b2_ref, rest[11:12]), (db_ref, rest[8:9]),
    ):
        ref[...] = (value * scale).reshape(width)
    ub_ref[...] = (jnp.concatenate([rest[f : f + 1, :BLOCK] for f in range(BLOCKS)], axis=1) * scale).reshape(
        BLOCKS * BLOCK
    )
    for k in range(3):
        for which in range(3):
            q_store(which, k).wait()
    for k in range(number_d - SLOTS, number_d):
        store_of(0, k).wait()
    for k in range(number_u - SLOTS, number_u):
        store_of(1, k).wait()


def finish_call(gain, h, dmid, dn, fd, fu, fq):
    width = h.shape[1]
    vm = pl.BlockSpec(memory_space=VM)
    hbm = pl.BlockSpec(memory_space=pl.ANY)
    dma = pltpu.SemaphoreType.DMA
    hidden = BLOCKS * BLOCK
    flat = jax.ShapeDtypeStruct((width, width), F32)
    line = jax.ShapeDtypeStruct((width,), F32)
    return pl.pallas_call(
        finish_kernel,
        name="finish",
        out_shape=[jax.ShapeDtypeStruct(h.shape, F32)]
        + [line] * 7
        + [jax.ShapeDtypeStruct((hidden,), F32), line]
        + [flat] * 4
        + [jax.ShapeDtypeStruct((width, hidden), F32), jax.ShapeDtypeStruct((hidden, width), F32)],
        in_specs=[vm] * 4 + [hbm] * 3,
        out_specs=[vm] * 10 + [hbm] * 6,
        scratch_shapes=[
            VM(fd.shape, BF), VM(fu.shape, BF), VM(fq.shape, BF),
            VM((SLOTS, 256, width), F32), VM((SLOTS, width, 256), F32), VM((3, width, width), F32),
            dma(fd.shape[:2]), dma(fu.shape[:2]), dma((4, 3)), dma((SLOTS,)), dma((SLOTS,)), dma((3, 3)),
        ],
        compiler_params=pltpu.CompilerParams(vmem_limit_bytes=56 * 2**20),
    )(gain, h, dmid, dn, fd, fu, fq)


def norm_rows(values):
    center = values - jnp.mean(values, axis=-1, keepdims=True)
    spread = jnp.mean(center * center, axis=-1, keepdims=True)
    return center * lax.rsqrt(spread + 1e-05)


def norm_affine(values, gain_vec, shift_vec):
    return norm_rows(values) * gain_vec + shift_vec


def left_product(left_mat, right_mat):
    return lax.dot_general(
        left_mat, right_mat, (((0,), (0,)), ((), ())), preferred_element_type=jnp.float32
    )


def right_product(left_mat, weight):
    return lax.dot_general(
        left_mat, weight, (((1,), (1,)), ((), ())), preferred_element_type=jnp.float32
    )


def slot_tags(first_row, count_rows, layout):
    begins_flat, finishes_flat, slot_rows, band_cap, band_count = layout
    slot_index = first_row + jnp.arange(count_rows, dtype=jnp.int32)
    owner = slot_index // slot_rows
    within = slot_index - owner * slot_rows
    member = within // band_cap
    offset = within - member * band_cap
    flat_code = member * band_count + owner
    all_codes = jnp.arange(begins_flat.shape[0], dtype=jnp.int32)
    hit_table = flat_code[:, None] == all_codes[None, :]
    begins = jnp.sum(jnp.where(hit_table, begins_flat[None, :], 0), axis=1)
    finish = jnp.sum(jnp.where(hit_table, finishes_flat[None, :], 0), axis=1)
    position = begins + offset
    return (member, position, position < finish, slot_index)


def allowed_pairs(query_tags, key_tags):
    query_member, query_position, query_valid, query_slot = query_tags
    key_member, key_position, key_valid, key_slot = key_tags
    same_slot = query_slot[:, None] == key_slot[None, :]
    causal = (query_member[:, None] == key_member[None, :]) & (
        key_position[None, :] <= query_position[:, None]
    )
    return same_slot | query_valid[:, None] & key_valid[None, :] & causal


def on_device(
    residual_in,
    exit_layer,
    band_edges,
    norm1_gain,
    norm1_bias,
    query_weight,
    query_bias,
    key_weight,
    value_weight,
    value_bias,
    out_weight,
    out_bias,
    norm2_gain,
    norm2_bias,
    up_weight,
    up_bias,
    down_weight,
    down_bias,
    cotangent,
):
    slot_rows = residual_in.shape[1]
    model_width = residual_in.shape[2]
    head_size = model_width // HEADS
    score_scale = head_size ** (-0.5)
    band_here = lax.axis_index("band")
    band_count = lax.axis_size("band")
    band_cap = slot_rows // band_edges.shape[1]
    finishes = jnp.concatenate([band_edges[0][:, 1:], band_edges[0][:, -1:] + band_cap], axis=1)
    layout = (band_edges[0].reshape(-1), finishes.reshape(-1), slot_rows, band_cap, band_count)
    own_tags = slot_tags(band_here * slot_rows, slot_rows, layout)
    active = ((exit_layer[0] >= LAYER) & own_tags[2]).astype(jnp.float32)[:, None]
    total_active = lax.psum(jnp.sum(active), ("band", "batch"))
    hidden_in = residual_in[0].astype(jnp.float32)
    normed_one, norm_one_back = jax.vjp(
        norm_affine, hidden_in, norm1_gain.astype(jnp.float32), norm1_bias.astype(jnp.float32)
    )
    normed_low = normed_one.astype(jnp.bfloat16)
    queries = (
        jnp.dot(normed_low, query_weight, preferred_element_type=jnp.float32)
        + query_bias.astype(jnp.float32)
    ).astype(jnp.bfloat16)
    keys_own = jnp.dot(normed_low, key_weight, preferred_element_type=jnp.float32).astype(
        jnp.bfloat16
    )
    values_own = (
        jnp.dot(normed_low, value_weight, preferred_element_type=jnp.float32)
        + value_bias.astype(jnp.float32)
    ).astype(jnp.bfloat16)
    query_heads = queries.reshape(slot_rows, HEADS, head_size)
    start_state = (
        jnp.full((HEADS, slot_rows), -1e30, jnp.float32),
        jnp.zeros((HEADS, slot_rows), jnp.float32),
        jnp.zeros((slot_rows, HEADS, head_size), jnp.float32),
    )
    key_piece = lax.all_gather(keys_own, "band", axis=0, tiled=True)
    value_piece = lax.all_gather(values_own, "band", axis=0, tiled=True)
    piece_rows = key_piece.shape[0]
    step_rows = min(piece_rows, slot_rows)

    def one_step(step_index, inner_state):
        offset_row = step_index * step_rows
        key_block = lax.dynamic_slice_in_dim(key_piece, offset_row, step_rows, 0).reshape(
            step_rows, HEADS, head_size
        )
        value_block = lax.dynamic_slice_in_dim(value_piece, offset_row, step_rows, 0).reshape(
            step_rows, HEADS, head_size
        )
        mask = allowed_pairs(own_tags, slot_tags(offset_row, step_rows, layout))

        def accumulate(running):
            top_old, total_old, sum_old = running
            scores = (
                jnp.einsum(
                    "qhd,khd->hqk", query_heads, key_block, preferred_element_type=jnp.float32
                )
                * score_scale
            )
            scores = jnp.where(mask[None], scores, -1e30)
            top_new = jnp.maximum(top_old, jnp.max(scores, axis=-1))
            rescale = jnp.exp(top_old - top_new)
            weights_new = jnp.where(mask[None], jnp.exp(scores - top_new[..., None]), 0.0)
            total_new = total_old * rescale + jnp.sum(weights_new, axis=-1)
            sum_new = sum_old * rescale.T[..., None] + jnp.einsum(
                "hqk,khd->qhd",
                weights_new.astype(jnp.bfloat16),
                value_block,
                preferred_element_type=jnp.float32,
            )
            return (top_new, total_new, sum_new)

        return lax.cond(jnp.any(mask), accumulate, lambda running: running, inner_state)

    top_score, weight_total, weighted_sum = lax.fori_loop(
        0, piece_rows // step_rows, one_step, start_state
    )
    attended = weighted_sum / weight_total.T[..., None]
    log_total = top_score + jnp.log(weight_total)
    mixed_low = attended.reshape(slot_rows, model_width).astype(jnp.bfloat16)
    branch = jnp.dot(mixed_low, out_weight, preferred_element_type=jnp.float32) + out_bias.astype(
        jnp.float32
    )
    middle = hidden_in + active * branch
    normed_two, norm_two_back = jax.vjp(
        norm_affine, middle, norm2_gain.astype(jnp.float32), norm2_bias.astype(jnp.float32)
    )
    normed_two_low = normed_two.astype(jnp.bfloat16)
    pre_act = jnp.dot(
        normed_two_low, up_weight, preferred_element_type=jnp.float32
    ) + up_bias.astype(jnp.float32)
    activated, gelu_back = jax.vjp(jax.nn.gelu, pre_act)
    activated_low = activated.astype(jnp.bfloat16)
    down_out = jnp.dot(
        activated_low, down_weight, preferred_element_type=jnp.float32
    ) + down_bias.astype(jnp.float32)
    layer_out = (middle + active * down_out).astype(jnp.bfloat16)[None]
    out_grad = cotangent[0].astype(jnp.float32)
    down_grad = (active * out_grad).astype(jnp.bfloat16)
    down_weight_sum = left_product(activated_low, down_grad)
    down_bias_sum = jnp.sum(down_grad.astype(jnp.float32), axis=0)
    (pre_grad,) = gelu_back(right_product(down_grad, down_weight))
    pre_low = pre_grad.astype(jnp.bfloat16)
    up_weight_sum = left_product(normed_two_low, pre_low)
    up_bias_sum = jnp.sum(pre_low.astype(jnp.float32), axis=0)
    middle_norm, gain_two_sum, shift_two_sum = norm_two_back(right_product(pre_low, up_weight))
    middle_grad = out_grad + middle_norm
    branch_grad = (active * middle_grad).astype(jnp.bfloat16)
    out_weight_sum = left_product(mixed_low, branch_grad)
    out_bias_sum = jnp.sum(branch_grad.astype(jnp.float32), axis=0)
    mixed_grad = right_product(branch_grad, out_weight).astype(jnp.bfloat16)
    grad_heads = mixed_grad.reshape(slot_rows, HEADS, head_size)
    delta_row = jnp.sum(grad_heads.astype(jnp.float32) * attended, axis=-1).T

    def pair_terms(query_blk, grad_blk, logsum_blk, delta_blk, key_block, value_block, mask):
        scores = (
            jnp.einsum("qhd,khd->hqk", query_blk, key_block, preferred_element_type=jnp.float32)
            * score_scale
        )
        probability = jnp.where(mask[None], jnp.exp(scores - logsum_blk[..., None]), 0.0)
        prob_grad = jnp.einsum(
            "qhd,khd->hqk", grad_blk, value_block, preferred_element_type=jnp.float32
        )
        score_grad = (probability * (prob_grad - delta_blk[..., None])).astype(jnp.bfloat16)
        return (probability.astype(jnp.bfloat16), score_grad)

    all_rows = slot_rows * band_count
    start_back = (
        jnp.zeros((slot_rows, HEADS, head_size), jnp.float32),
        jnp.zeros((all_rows, model_width), jnp.float32),
        jnp.zeros((all_rows, model_width), jnp.float32),
    )
    fold_key_piece = lax.all_gather(keys_own, "band", axis=0, tiled=True)
    fold_value_piece = lax.all_gather(values_own, "band", axis=0, tiled=True)
    piece_rows = fold_key_piece.shape[0]
    fold_step_rows = min(piece_rows, slot_rows)

    def one_step(step_index, inner_state):
        offset_row = step_index * fold_step_rows
        key_block = lax.dynamic_slice_in_dim(fold_key_piece, offset_row, fold_step_rows, 0).reshape(
            fold_step_rows, HEADS, head_size
        )
        value_block = lax.dynamic_slice_in_dim(
            fold_value_piece, offset_row, fold_step_rows, 0
        ).reshape(fold_step_rows, HEADS, head_size)
        mask = allowed_pairs(own_tags, slot_tags(offset_row, fold_step_rows, layout))

        def accumulate(running):
            query_acc, key_sums, value_sums = running
            prob_low, score_grad = pair_terms(
                query_heads, grad_heads, log_total, delta_row, key_block, value_block, mask
            )
            query_acc = (
                query_acc
                + jnp.einsum(
                    "hqk,khd->qhd", score_grad, key_block, preferred_element_type=jnp.float32
                )
                * score_scale
            )
            key_term = (
                jnp.einsum(
                    "hqk,qhd->khd", score_grad, query_heads, preferred_element_type=jnp.float32
                ).reshape(fold_step_rows, model_width)
                * score_scale
            )
            value_term = jnp.einsum(
                "hqk,qhd->khd", prob_low, grad_heads, preferred_element_type=jnp.float32
            ).reshape(fold_step_rows, model_width)
            key_sums = lax.dynamic_update_slice_in_dim(
                key_sums,
                lax.dynamic_slice_in_dim(key_sums, offset_row, fold_step_rows, 0) + key_term,
                offset_row,
                0,
            )
            value_sums = lax.dynamic_update_slice_in_dim(
                value_sums,
                lax.dynamic_slice_in_dim(value_sums, offset_row, fold_step_rows, 0) + value_term,
                offset_row,
                0,
            )
            return (query_acc, key_sums, value_sums)

        return lax.cond(jnp.any(mask), accumulate, lambda running: running, inner_state)

    back_state = lax.fori_loop(0, piece_rows // fold_step_rows, one_step, start_back)
    query_sum, key_sums_all, value_sums_all = back_state
    key_sum, value_sum = (
        lax.psum_scatter(
            key_sums_all.astype(jnp.bfloat16), "band", scatter_dimension=0, tiled=True
        ).astype(jnp.float32),
        lax.psum_scatter(
            value_sums_all.astype(jnp.bfloat16), "band", scatter_dimension=0, tiled=True
        ).astype(jnp.float32),
    )
    query_low = query_sum.reshape(slot_rows, model_width).astype(jnp.bfloat16)
    key_low = key_sum.astype(jnp.bfloat16)
    value_low = value_sum.astype(jnp.bfloat16)
    query_weight_sum = left_product(normed_low, query_low)
    query_bias_sum = jnp.sum(query_low.astype(jnp.float32), axis=0)
    key_weight_sum = left_product(normed_low, key_low)
    value_weight_sum = left_product(normed_low, value_low)
    value_bias_sum = jnp.sum(value_low.astype(jnp.float32), axis=0)
    normed_grad = (
        right_product(query_low, query_weight)
        + right_product(key_low, key_weight)
        + right_product(value_low, value_weight)
    )
    input_norm, gain_one_sum, shift_one_sum = norm_one_back(normed_grad)
    input_grad = (middle_grad + input_norm)[None]
    (
        total_g1,
        total_b1,
        total_qw,
        total_qb,
        total_kw,
        total_vw,
        total_vb,
        total_ow,
        total_ob,
        total_g2,
        total_b2,
        total_uw,
        total_ub,
        total_dw,
        total_db,
    ) = lax.psum(
        (
            gain_one_sum,
            shift_one_sum,
            query_weight_sum,
            query_bias_sum,
            key_weight_sum,
            value_weight_sum,
            value_bias_sum,
            out_weight_sum,
            out_bias_sum,
            gain_two_sum,
            shift_two_sum,
            up_weight_sum,
            up_bias_sum,
            down_weight_sum,
            down_bias_sum,
        ),
        ("band", "batch"),
    )
    return (
        layer_out,
        input_grad,
        total_g1 / total_active,
        total_b1 / total_active,
        total_qw / total_active,
        total_qb / total_active,
        total_kw / total_active,
        total_vw / total_active,
        total_vb / total_active,
        total_ow / total_active,
        total_ob / total_active,
        total_g2 / total_active,
        total_b2 / total_active,
        total_uw / total_active,
        total_ub / total_active,
        total_dw / total_active,
        total_db / total_active,
    )


def fast_device(
    residual_in, exit_layer, band_edges, norm1_gain, norm1_bias, query_weight, query_bias,
    key_weight, value_weight, value_bias, out_weight, out_bias, norm2_gain, norm2_bias,
    up_weight, up_bias, down_weight, down_bias, cotangent,
):
    h, cot = residual_in[0], cotangent[0]
    o, lse, att, wback, n1, n1t, q, kv, kt = attend_call(
        band_edges, norm1_gain, norm1_bias, query_bias, value_bias, h, query_weight, key_weight, value_weight
    )
    vecs = (norm1_bias, out_bias, norm2_gain, norm2_bias, down_bias, up_bias)
    dn, layer, dmid, fq, fd, fu = layer_call(
        band_edges, exit_layer, vecs, h, cot, att, o, lse, wback, out_weight,
        n1, n1t, q, kv, kt, up_weight, down_weight,
    )
    grad, g1, b1, qb, vb, ob, g2, b2, ub, db, qw, kw, vw, ow, uw, dw = finish_call(
        norm1_gain, h, dmid, dn, fd, fu, fq
    )
    return (layer[None], grad[None], g1, b1, qw, qb, kw, vw, vb, ow, ob, g2, b2, uw, ub, dw, db)


def solution(mesh):
    placed = (
        (P("batch", "band", None), P("batch", "band"), P("batch", None, None))
        + (P(),) * 15
        + (P("batch", "band", None),)
    )
    fast = mesh.shape["band"] == BANDS and mesh.shape["batch"] == 4
    return jax.shard_map(
        fast_device if fast else on_device,
        mesh=mesh,
        in_specs=placed,
        out_specs=(P("batch", "band", None),) * 2 + (P(),) * 15,
        check_vma=False,
    )
```

```python
import functools

import jax
import jax.numpy as jnp
from jax import lax
from jax.experimental import pallas as pl
from jax.experimental.pallas import tpu as pltpu
from jax.sharding import PartitionSpec as P

MESH = pl.DeviceIdType.MESH
VM = pltpu.VMEM
BF = jnp.bfloat16
F32 = jnp.float32
HEADS = 12
LAYER = 6
HEAD = 64
BANDS = 8
CAP = 256
HALF = 128
MINE = 3
SHARE = MINE * HEAD
NEG = -1e30


def place():
    band = lax.axis_index("band")
    return band, band // 4, (band // 2) % 2, band % 2


def device(y, x, core):
    return (y * 4 + x * 2 + core, lax.axis_index("batch"))


def push(src, dst, send, recv, target):
    return pltpu.make_async_remote_copy(
        src_ref=src, dst_ref=dst, send_sem=send, recv_sem=recv, device_id=target, device_id_type=MESH
    )


def dot(a, b, dims):
    return lax.dot_general(a, b, ((dims[0], dims[1]), ((), ())), preferred_element_type=F32)


NN = ((1,), (0,))
NT = ((1,), (1,))
TN = ((0,), (0,))


def as_row(ref):
    return ref[...].astype(F32).reshape(1, -1)


def counts_of(edges_ref, seq, band):
    after = edges_ref[0, seq, jnp.minimum(band + 1, BANDS - 1)]
    return jnp.where(band == BANDS - 1, CAP, after - edges_ref[0, seq, band])


def greet():
    band, _, _, _ = place()
    batch = lax.axis_index("batch")
    links = partners()
    barrier = pltpu.get_barrier_semaphore()
    for step in range(1, BANDS):
        pl.semaphore_signal(barrier, inc=1, device_id=((band + step) % BANDS, batch), device_id_type=MESH)
    for axis in ("a", "b"):
        pl.semaphore_signal(barrier, inc=1, device_id=links[axis][1], device_id_type=MESH)
    pl.semaphore_wait(barrier, BANDS + 1)


def attend(
    edges_ref, gain_ref, shift_ref, bq_ref, bv_ref, h_ref, wq_hbm, wk_hbm, wv_hbm,
    o_ref, lse_ref, att_ref, wback_ref, n1t_hbm, q_ref, kv_ref, kvt_ref, rows_at,
    send, recv, out_send, out_recv, load, store,
    n1t_ref, cols_ref, turned_ref, top_ref, total_ref, mix_ref,
):
    band, y, x, core = place()
    width = h_ref.shape[1]
    group = 2 * x + core
    wide = pl.ds(pl.multiple_of(x * 2 * SHARE + core * 128, 128), 256)
    loads = [
        pltpu.make_async_copy(ref.at[:, wide], cols_ref.at[k], load.at[k])
        for k, ref in enumerate((wq_hbm, wk_hbm, wv_hbm))
    ]
    for copy in loads:
        copy.start()
    greet()
    own = pl.ds(pl.multiple_of(y * CAP, CAP), CAP)
    half = pl.ds(pl.multiple_of(core * HALF, HALF), HALF)
    other_y, other_x, other_core = 1 - y, 1 - x, 1 - core
    sibling = device(y, x, other_core)
    copies = {}

    def go(name, src, dst, index, recv_index, target):
        copy = push(src, dst, send.at[index], recv.at[recv_index], target)
        copy.start()
        copies[name] = copy

    for k in range(2):
        from_rows = pl.ds(pl.multiple_of(other_y * CAP + k * HALF, HALF), HALF)
        go(("y", k), h_ref.at[from_rows], rows_at(band).at[pl.ds(k * HALF, HALF)], 1 + k, 1 + core,
           device(other_y, x, k))
    for k in range(2):
        from_rows = pl.ds(pl.multiple_of(y * CAP + k * HALF, HALF), HALF)
        go(("x", k), h_ref.at[from_rows], rows_at(band).at[pl.ds(k * HALF, HALF)], 3 + k, 3 + core,
           device(y, other_x, k))
    go("sib", h_ref.at[own], rows_at(band), 0, 0, sibling)

    gain, shift = as_row(gain_ref), as_row(shift_ref)
    for k, copy in enumerate(loads):
        copy.wait()
        turned_ref[k] = cols_ref[k].T
        for h in range(MINE):
            part = turned_ref[k, pl.ds(pl.multiple_of(core * HEAD + h * HEAD, HEAD), HEAD), :]
            at = k * SHARE + h * HEAD
            wback_ref[at : at + HEAD, :] = part
    row = lax.broadcasted_iota(jnp.int32, (3 * SHARE, width), 0)
    col = lax.broadcasted_iota(jnp.int32, (3 * SHARE, width), 1) - group * SHARE
    pick_q = jnp.where((row == col) & (row < SHARE), 1.0, 0.0).astype(BF)
    pick_v = jnp.where((row - 2 * SHARE == col) & (row >= 2 * SHARE), 1.0, 0.0).astype(BF)

    def spread_row(ref):
        return jnp.broadcast_to(as_row(ref), (8, width)).astype(BF)

    bias = (dot(pick_q, spread_row(bq_ref), NT) + dot(pick_v, spread_row(bv_ref), NT))[:, :1]

    def project(rows, which):
        wide_rows = rows.astype(F32)
        center = wide_rows - jnp.mean(wide_rows, axis=-1, keepdims=True)
        spread = jnp.mean(center * center, axis=-1, keepdims=True)
        n1 = (center * lax.rsqrt(spread + 1e-05) * gain + shift).astype(BF)
        at = pl.ds(pl.multiple_of(which * CAP, CAP), CAP)
        n1t_ref[:, at] = n1.T
        all_t = dot(wback_ref[...], n1, NT) + bias
        qt = (all_t[:SHARE] * 0.125).astype(BF)
        kvt = all_t[SHARE:].astype(BF)
        for h in range(MINE):
            one = jnp.concatenate(
                [kvt[h * HEAD : (h + 1) * HEAD], kvt[SHARE + h * HEAD : SHARE + (h + 1) * HEAD]], axis=0
            )
            kvt_ref[h, which] = one
            kv_ref[h, which] = one.T
            q_ref[h, which, :HEAD] = qt[h * HEAD : (h + 1) * HEAD]
            q_ref[h, which, HEAD:] = jnp.zeros((HEAD, CAP), BF)

    def project_two(first_y, first_x):
        def one(k, carry):
            which = first_y * 4 + first_x * 2 + k
            project(rows_at(which)[...], which)
            return carry

        lax.fori_loop(0, 2, one, 0)

    rows_at(band)[...] = h_ref[own, :]

    def wait_recv(index, which, size=HALF):
        ref = rows_at(which) if size == CAP else rows_at(which).at[half]
        push(ref, ref, send.at[0], recv.at[index], sibling).wait_recv()

    wait_recv(0, y * 4 + x * 2 + other_core, CAP)
    project_two(y, x)
    for k in range(2):
        from_band = other_y * 4 + x * 2 + k
        wait_recv(1 + k, from_band)
        piece = rows_at(from_band).at[half]
        go(("fx", k), piece, piece, 5 + k, 5 + k, device(y, other_x, core))
        go(("fs", k), piece, piece, 7 + k, 7 + k, sibling)
    for k in range(2):
        from_band = y * 4 + other_x * 2 + k
        wait_recv(3 + k, from_band)
        piece = rows_at(from_band).at[half]
        go(("fs", 2 + k), piece, piece, 9 + k, 9 + k, sibling)
    for k in range(2):
        copies[("fs", k)].wait_recv()
    project_two(other_y, x)
    for k in range(2):
        copies[("fs", 2 + k)].wait_recv()
    project_two(y, other_x)

    key_at = lax.broadcasted_iota(jnp.int32, (CAP, CAP), 0)
    query_at = lax.broadcasted_iota(jnp.int32, (CAP, CAP), 1)
    lane = lax.broadcasted_iota(jnp.int32, (1, CAP), 1)
    share = pl.ds(pl.multiple_of(group * SHARE, SHARE), SHARE)
    side = pl.ds(pl.multiple_of(y * CAP, CAP), CAP)

    def absorb(i, keys, fresh):
        scores, tops, totals, mixes = [], [], [], []
        keeps = []
        for number, j in enumerate(keys):
            keep = key_at < counts_of(edges_ref, y, j)
            if fresh and number == len(keys) - 1:
                keep = keep & (key_at <= query_at)
            keeps.append(keep)
        for h in range(MINE):
            qt = q_ref[h, i]
            scores.append([jnp.where(keep, dot(kv_ref[h, j], qt, NN), NEG) for j, keep in zip(keys, keeps)])
        for h in range(MINE):
            top = functools.reduce(jnp.maximum, [jnp.max(s, axis=0, keepdims=True) for s in scores[h]])
            if fresh:
                total = jnp.zeros((1, CAP), F32)
                mix = jnp.zeros((HEAD, CAP), F32)
            else:
                before = top_ref[h, i]
                top = jnp.maximum(top, before)
                rescale = jnp.exp(before - top)
                total = total_ref[h, i] * rescale
                mix = mix_ref[h, i] * rescale
            for s, j in zip(scores[h], keys):
                p = jnp.exp(s - top)
                total = total + jnp.sum(p, axis=0, keepdims=True)
                mix = mix + dot(kvt_ref[h, j, HEAD:], p.astype(BF), NN)
            tops.append(top)
            totals.append(total)
            mixes.append(mix)
        for h in range(MINE):
            top_ref[h, i] = tops[h]
            total_ref[h, i] = totals[h]
            mix_ref[h, i] = mixes[h]

    def settle(pair):
        for r in range(2):
            i = 2 * pair + r
            valid = lane < counts_of(edges_ref, y, i)
            for h in range(MINE):
                total = total_ref[h, i]
                mix = jnp.where(valid, mix_ref[h, i] / total, kvt_ref[h, i, HEAD:].astype(F32))
                o_ref[i, h * HEAD : (h + 1) * HEAD, :] = mix.astype(BF)
                lse_ref[h, i] = jnp.where(valid, top_ref[h, i] + jnp.log(total), -NEG)
            copy = push(o_ref.at[i], att_ref.at[share, side], out_send.at[i], out_recv.at[band],
                        (i, lax.axis_index("batch")))
            pl.when(band != i)(copy.start)
            local = pltpu.make_async_copy(o_ref.at[i], att_ref.at[share, side], out_recv.at[band])
            pl.when(band == i)(local.start)

    late = 3 - (2 * y + x)
    early = [jnp.where(late <= k, k + 1, k) for k in range(3)]
    for a in range(3):
        before = [2 * early[b] + r for b in range(a) for r in range(2)]
        absorb(2 * early[a], before + [2 * early[a]], True)
        absorb(2 * early[a] + 1, before + [2 * early[a], 2 * early[a] + 1], True)
    for k in range(2):
        from_band = other_y * 4 + other_x * 2 + k
        copies[("fx", k)].wait_recv()
        piece = rows_at(from_band).at[half]
        go(("fs", 4 + k), piece, piece, 11 + k, 11 + k, sibling)
    for a in range(3):
        pl.when(early[a] < late)(functools.partial(settle, early[a]))
    for k in range(2):
        copies[("fs", 4 + k)].wait_recv()
    project_two(other_y, other_x)
    keep_turned = pltpu.make_async_copy(n1t_ref, n1t_hbm, store)
    keep_turned.start()
    for a in range(3):
        query, key = jnp.maximum(early[a], late), jnp.minimum(early[a], late)
        if a == 0:
            absorb(2 * late, [2 * late], True)
            absorb(2 * late + 1, [2 * late, 2 * late + 1], True)
        for r in range(2):
            absorb(2 * query + r, [2 * key, 2 * key + 1], False)
        pl.when(early[a] > late)(functools.partial(settle, early[a]))
    settle(late)
    for i in range(BANDS):
        from_y, from_x, from_core = i // 4, (i // 2) % 2, i % 2
        ref = att_ref.at[pl.ds((2 * from_x + from_core) * SHARE, SHARE), pl.ds(from_y * CAP, CAP)]
        copy = push(o_ref.at[i], ref, out_send.at[i], out_recv.at[i], sibling)
        copy.wait_recv()
        pl.when(band != i)(copy.wait_send)
    for copy in copies.values():
        copy.wait_send()
    keep_turned.wait()


BLOCK = 512
BLOCKS = 6
QLANES = 640
D_AXES = ('xyab', 'xyab', 'aybx', 'xaby', 'yxab', 'yxba', 'xyab', 'yxab')
U_AXES = ('yxba', 'xbay', 'yabx', 'axby', 'axyb', 'xayb')
Q_AXES = ('aby-bxa', 'yab-axy', 'ayb-yax')
TOGETHER = 0
EVENTS = ('b7', 'd7', 'b6', 'd6', 'b5', 'd5', 'b4', 'd4', 'b3', 'd3', 'b2', 'd2', 'b1', 'd1', 'b0', 'd0', 'q0', 'q1', 'q2')
SCHEDULE = {'m0': (0, 8), 'm1': (1, 9, 0), 'a1': (8,), 'm2': (2, 10, 1, 9), 'm3': (3, 11, 2, 10), 'm4': (4, 12, 3, 11, 0), 'a4': (8,), 'g5': (4,), 'm5': (5, 13, 12), 'a5': (1,), 'e': (5, 13, 2, 9, 10, 0), 'o': (6,), 's': (7, 11, 3, 4, 6, 8, 7, 12, 1, 10, 9, 0, 3), 'b71': (1, 8), 'b72': (5, 13, 9, 10, 0), 'd7': (11,), 'b60': (2, 3, 4), 'b62': (7, 1, 8, 9), 'd6': (6, 13), 'b50': (0, 12), 'b51': (11, 3), 'b52': (5, 2, 4, 10, 1), 'b40': (8, 9), 'b42': (6, 7, 13), 'b30': (3,), 'b31': (2, 0), 'b32': (5, 12, 11), 'b20': (4,), 'b21': (6, 1, 8), 'b22': (7, 10), 'd1': (3,), 'd0': (9,), 'q0': (14, 5, 13, 0), 'q1': (15, 2, 4), 'q2': (16, 8, 12, 0), 'end': (1, 10, 11, 8, 1, 6, 14, 13, 7, 5, 3, 16, 15, 6, 3, 2, 12, 14, 13, 7, 9, 10, 15, 9, 4, 16, 10, 11, 6, 2, 5, 14, 2, 12, 15, 4, 13, 4, 11, 16, 13, 7, 11, 5, 5, 14, 6, 12, 16, 6, 15, 12, 7, 14, 7, 16, 15, 14, 14, 16, 15, 16, 15)}


def partners():
    band, y, x, core = place()
    z = lax.axis_index("batch")
    return {
        "core": (core, device(y, x, 1 - core)),
        "x": (x, device(y, 1 - x, core)),
        "y": (y, device(1 - y, x, core)),
        "a": (z % 2, (band, z + 1 - 2 * (z % 2))),
        "b": (z // 2, (band, (z + 2) % 4)),
    }


class Chain:
    def __init__(self, send, recv, free, store):
        self.send, self.recv, self.free, self.finish = send, recv, free, store
        self.links = partners()
        self.steps = []
        self.at = 0

    def halve(self, piece, rows, axes, landing):
        start, spans = 0, {}
        first = len(self.steps)
        for level, axis in enumerate(axes[:-1]):
            rows //= 2
            bit = self.links[axis][0]
            keep, give = (start + bit * rows, rows), (start + (1 - bit) * rows, rows)
            self.steps.append(
                (axis, piece(give), landing[level], landing[level], piece(keep), first + level, None)
            )
            start = keep[0]
            spans[axis] = (keep, give, first + level)
        mine = piece((start, rows))
        self.steps.append((axes[-1], mine, landing[-1], landing[-1], mine, None, None))
        return spans

    def copy(self, number, arrival=False):
        axis, src, dst, got = self.steps[number][:4]
        if arrival:
            src = dst = got
        return push(src, dst, self.send.at[number], self.recv.at[number], self.links[axis][1])

    def add(self, target, source):
        rows, lanes = source.shape
        size = 32 if lanes < 512 and rows % 32 == 0 else 16

        def some(r, carry):
            at = pl.ds(pl.multiple_of(r * size, size), size)
            target[at, :] = (target[at, :].astype(F32) + source[at, :].astype(F32)).astype(BF)
            return carry

        lax.fori_loop(0, rows // size, some, 0)

    def advance(self):
        number, self.at = self.at, self.at + 1
        if number > 0:
            axis, _, _, got, add, frees, _ = self.steps[number - 1]
            self.copy(number - 1, True).wait_recv()
            if add is not None:
                self.copy(number - 1).wait_send()
                if frees is not None:
                    pl.semaphore_signal(
                        self.free.at[frees], inc=1, device_id=self.links[axis][1], device_id_type=MESH
                    )
                self.add(add, got)
        if number < len(self.steps):
            freed = self.steps[number][6]
            if freed is not None:
                pl.semaphore_wait(self.free.at[freed], 1)
            self.copy(number).start()
        else:
            self.finish.start()

    def drain(self):
        for number, step in enumerate(self.steps):
            if step[4] is None:
                self.copy(number).wait_send()
        self.finish.wait()


def weight_chain(total, landing, send, recv, free, index, axes, out, out_sem):
    core = lax.axis_index("band") % 2
    chain = Chain(
        send.at[index], recv.at[index], free.at[index],
        pltpu.make_async_copy(total.at[index], out.at[index], out_sem.at[index]),
    )
    mine, other, first = total.at[index, core], total.at[index, 1 - core], landing[0].at[index]
    chain.steps.append(("core", other, first, first, mine, 0, None))

    def piece(span):
        return total.at[index, core, pl.ds(pl.multiple_of(span[0], 16), span[1])]

    spans = chain.halve(piece, total.shape[2], axes, [spot.at[index] for spot in landing[1:]])
    for axis in axes[-2::-1]:
        keep, give, level = spans[axis]
        chain.steps.append((axis, piece(keep), piece(keep), piece(give), None, None, level))
    chain.steps.append(("core", mine, mine, other, None, None, 0))
    return chain


def head_chain(total, landing, send, recv, free, index, axes, out, out_sem):
    _, _, x, core = place()
    chain = Chain(
        send.at[index], recv.at[index], free.at[index],
        pltpu.make_async_copy(total.at[:, :, index], out.at[:, :, index], out_sem.at[index]),
    )

    def piece(span, which="own"):
        rows = pl.ds(pl.multiple_of(span[0], 16), span[1])
        if which == "both":
            return total.at[:, core, index, rows]
        return total.at[x if which == "own" else 1 - x, core, index, rows]

    axes, tail = axes.split("-")
    spans = chain.halve(piece, total.shape[3], axes, [spot.at[index] for spot in landing])
    held, which = spans[axes[-2]][0], "own"
    for axis in tail:
        if axis == "x":
            mine = piece(held)
            chain.steps.append(("x", mine, mine, piece(held, "other"), None, None, None))
            which = "both"
            continue
        keep, give, level = spans[axis]
        chain.steps.append((axis, piece(keep, which), piece(keep, which), piece(give, which), None, None, level))
        outer = axes.index(axis) - 1
        held = spans[axes[outer]][0] if outer >= 0 else (0, total.shape[3])
    both = total.at[:, core, index]
    chain.steps.append(("core", both, both, total.at[:, 1 - core, index], None, None, None))
    return chain


def layer_kernel(
    edges_ref, exit_ref, gain1_ref, shift1_ref, bq_ref, bv_ref, bo_ref, g2_ref, b2_ref, bd_ref, ub_ref,
    h_ref, cot_ref, wout_ref, wq_hbm, wk_hbm, wv_hbm, wup_hbm, wdown_hbm,
    dn_ref, layer_hbm, dmid_hbm, fq_hbm, fd_hbm, fu_hbm, n1t_hbm,
    gd_ref, gu_ref, fq_ref, d0, d1, d2, d3, d4, u0, u1, u2, u3, u4, q1, q2, q3,
    layer_ref, dmid_ref, q_ref, kv_ref, kt_ref, dz_ref, da_ref, do_ref, sib_out, sib_in, row_out,
    o_ref, lse_ref, att_ref, wback_ref,
    d_send, d_recv, d_free, d_out, u_send, u_recv, u_free, u_out, q_send, q_recv, q_free, q_out,
    do_send, do_recv, sib_send, sib_recv, dn_send, dn_recv, out_send, out_recv, load, wload, out_sem,
    a_send, a_recv, a_load,
):
    band, y, x, core = place()
    batch = lax.axis_index("batch")
    links = partners()
    sibling = links["core"][1]
    width = h_ref.shape[1]
    pl.run_scoped(
        functools.partial(
            attend, edges_ref, gain1_ref, shift1_ref, bq_ref, bv_ref, h_ref, wq_hbm, wk_hbm, wv_hbm,
            o_ref, lse_ref, att_ref, wback_ref, n1t_hbm, q_ref, kv_ref, kt_ref,
            lambda which: gd_ref.at[which // 2, which % 2],
            a_send, a_recv, out_send, out_recv, a_load, load.at[0],
        ),
        VM((width, BANDS * CAP), BF),
        VM((3, width, 256), BF),
        VM((3, 256, width), BF),
        VM((MINE, BANDS, 1, CAP), F32),
        VM((MINE, BANDS, 1, CAP), F32),
        VM((MINE, BANDS, HEAD, CAP), F32),
    )

    chains = [
        weight_chain(gd_ref, (d0, d1, d2, d3, d4), d_send, d_recv, d_free, k, D_AXES[k], fd_hbm, d_out)
        for k in range(BLOCKS + 2)
    ] + [
        weight_chain(gu_ref, (u0, u1, u2, u3, u4), u_send, u_recv, u_free, k, U_AXES[k], fu_hbm, u_out)
        for k in range(BLOCKS)
    ] + [
        head_chain(fq_ref, (q1, q2, q3), q_send, q_recv, q_free, k, Q_AXES[k], fq_hbm, q_out) for k in range(3)
    ]
    layer_out = pltpu.make_async_copy(layer_ref, layer_hbm, out_sem.at[0])
    dmid_out = pltpu.make_async_copy(dmid_ref, dmid_hbm, out_sem.at[1])

    def serve(point):
        for k in SCHEDULE.get(point, ()):
            chains[k].advance()

    lane = lax.broadcasted_iota(jnp.int32, (1, 2 * CAP), 1)
    limit = jnp.where(lane < CAP, counts_of(edges_ref, 0, band), counts_of(edges_ref, 1, band) + CAP)
    active_row = jnp.where((exit_ref[...] >= LAYER) & (lane < limit), 1.0, 0.0)
    active = jnp.broadcast_to(active_row, (8, 2 * CAP)).T[:, :1]

    def feed_forward(mid_ref, sum_ref, dn2_ref, n2_ref, n2t_ref, wu, wd, pre_ref, dact_ref, act_ref, dpre_ref, part_ref, row_ref):
        def weights(f):
            at = pl.ds(f * BLOCK, BLOCK)
            return (
                pltpu.make_async_copy(wup_hbm.at[:, at], wu.at[f % 2], wload.at[0, f % 2]),
                pltpu.make_async_copy(wdown_hbm.at[at], wd.at[f % 2], wload.at[1, f % 2]),
            )

        for copy in weights(0):
            copy.start()
        branch = dot(att_ref[...], wout_ref[...], TN) + as_row(bo_ref)
        middle = h_ref[...].astype(F32) + active * branch
        mid_ref[...] = middle
        center = middle - jnp.mean(middle, axis=-1, keepdims=True)
        spread = jnp.mean(center * center, axis=-1, keepdims=True)
        scale2 = lax.rsqrt(spread + 1e-05)
        n2 = (center * scale2 * as_row(g2_ref) + as_row(b2_ref)).astype(BF)
        n2_ref[...] = n2
        n2t_ref[...] = n2.T
        dz_ref[...] = (active * cot_ref[...].astype(F32)).astype(BF)
        up_row = as_row(ub_ref)
        row_ref[...] = jnp.zeros_like(row_ref)
        sum_ref[...] = jnp.zeros_like(sum_ref)
        dn2_ref[...] = jnp.zeros_like(dn2_ref)
        for f in range(BLOCKS):
            if f + 1 < BLOCKS:
                for copy in weights(f + 1):
                    copy.start()
            for copy in weights(f):
                copy.wait()
            slot = f % 2
            pre_ref[...] = dot(n2_ref[...], wu[slot], NN)
            dact_ref[...] = dot(dz_ref[...], wd[slot], NT)
            serve(f'p{f}')
            up_bias = up_row[:, f * BLOCK : (f + 1) * BLOCK]
            part_ref[...] = jnp.zeros_like(part_ref)

            def rows(r, carry):
                at = pl.ds(pl.multiple_of(r * 64, 64), 64)
                pre = pre_ref[at, :] + up_bias
                square = pre * pre
                t = jnp.tanh(0.7978845608028654 * pre * (1.0 + 0.044715 * square))
                half = 0.5 * (1.0 + t)
                slope = half + (0.5 * 0.7978845608028654) * pre * (1.0 - t * t) * (1.0 + 0.134145 * square)
                act_ref[at, :] = (pre * half).astype(BF)
                dpre = (dact_ref[at, :] * slope).astype(BF)
                dpre_ref[at, :] = dpre
                part_ref[...] += jnp.sum(dpre.astype(F32).reshape(8, 8, BLOCK), axis=0)
                return carry

            lax.fori_loop(0, 2 * CAP // 64, rows, 0)
            serve(f'g{f}')
            down = dot(act_ref[...], dz_ref[...], TN).astype(BF)
            gd_ref[f, 0] = down[: BLOCK // 2]
            gd_ref[f, 1] = down[BLOCK // 2 :]
            up = dot(n2t_ref[...], dpre_ref[...], NN).astype(BF)
            gu_ref[f, 0] = up[:, : BLOCK // 2]
            gu_ref[f, 1] = up[:, BLOCK // 2 :]
            row_ref[f : f + 1, :BLOCK] = jnp.sum(part_ref[...], axis=0, keepdims=True)
            serve(f'm{f}')
            sum_ref[...] += dot(act_ref[...], wd[slot], NN)
            dn2_ref[...] += dot(dpre_ref[...], wu[slot], NT)
            serve(f'a{f}')
        middle = mid_ref[...]
        center = middle - jnp.mean(middle, axis=-1, keepdims=True)
        spread = jnp.mean(center * center, axis=-1, keepdims=True)
        scale2 = lax.rsqrt(spread + 1e-05)
        xhat = center * scale2
        dn2 = dn2_ref[...]
        e2 = dn2 * as_row(g2_ref)
        dmid = cot_ref[...].astype(F32) + scale2 * (
            e2 - jnp.mean(e2, axis=-1, keepdims=True) - xhat * jnp.mean(e2 * xhat, axis=-1, keepdims=True)
        )
        dmid_ref[...] = dmid
        da = (active * dmid).astype(BF)
        n2_ref[...] = da
        da_ref[...] = dot(wout_ref[...], da, NT).astype(BF)
        for i in range(BANDS):
            copy = push(part_for(i), do_ref.at[band], do_send.at[i], do_recv.at[band], (i, batch))
            pl.when(band != i)(copy.start)
            local = pltpu.make_async_copy(part_for(i), do_ref.at[band], do_recv.at[band])
            pl.when(band == i)(local.start)
        dmid_out.start()
        row_ref[10:11, :] = jnp.sum(dn2 * xhat, axis=0, keepdims=True)
        serve('e')
        out = dot(att_ref[...], n2_ref[...], NN).astype(BF)
        gd_ref[BLOCKS, 0] = out[:256]
        gd_ref[BLOCKS, 1] = out[256:512]
        gd_ref[BLOCKS + 1, 0] = out[512:]
        serve('o')
        layer_ref[...] = (mid_ref[...] + active * (sum_ref[...] + as_row(bd_ref))).astype(BF)
        layer_out.start()
        count = jnp.sum(active_row)
        big = jnp.floor(count * (1.0 / 64.0))
        mid = jnp.floor((count - 64.0 * big) * 0.125)
        small = count - 64.0 * big - 8.0 * mid
        at = lax.broadcasted_iota(jnp.int32, (1, width), 1)
        digits = jnp.where(at == 0, big, jnp.where(at == 1, mid, jnp.where(at == 2, small, 0.0)))
        row_ref[8:9, :] = jnp.sum(dz_ref[...].astype(F32), axis=0, keepdims=True)
        row_ref[9:10, :] = jnp.sum(n2_ref[...].astype(F32), axis=0, keepdims=True)
        row_ref[11:12, :] = jnp.sum(dn2_ref[...], axis=0, keepdims=True)
        row_ref[12:13, :] = digits
        gd_ref[BLOCKS + 1, 1, :16, :] = row_ref[...].astype(BF)
        serve('s')

    def part_for(i):
        to_y, to_x, to_core = i // 4, (i // 2) % 2, i % 2
        return da_ref.at[pl.ds((2 * to_x + to_core) * SHARE, SHARE), pl.ds(to_y * CAP, CAP)]

    gd_ref[BLOCKS + 1, 1] = jnp.zeros(gd_ref.shape[2:], BF)
    rows2 = 2 * CAP
    pl.run_scoped(
        feed_forward,
        VM((rows2, width), F32), VM((rows2, width), F32), VM((rows2, width), F32),
        VM((rows2, width), BF), VM((width, rows2), BF),
        VM((2, width, BLOCK), BF), VM((2, BLOCK, width), BF),
        VM((rows2, BLOCK), F32), VM((rows2, BLOCK), F32), VM((rows2, BLOCK), BF), VM((rows2, BLOCK), BF),
        VM((8, BLOCK), F32), VM((16, width), F32),
    )
    half = pl.ds(pl.multiple_of(core * HALF, HALF), HALF)
    key_at = lax.broadcasted_iota(jnp.int32, (CAP, CAP), 0)
    query_at = lax.broadcasted_iota(jnp.int32, (CAP, CAP), 1)

    def sib_copy(i):
        return push(sib_out.at[i % 2], sib_in.at[i], sib_send.at[i], sib_recv.at[i], sibling)

    def dn_copy(i):
        return push(row_out.at[i % 2], dn_ref.at[y, x, half], dn_send.at[i], dn_recv.at[band], (i, batch))

    def dn_local(i):
        return pltpu.make_async_copy(row_out.at[i % 2], dn_ref.at[y, x, half], dn_recv.at[band])

    def backward(dk_ref, d_ref, mine_ref, n1t_ref, small_ref):
        turned_load = pltpu.make_async_copy(n1t_hbm, n1t_ref, load.at[3])
        turned_load.start()

        def finish(i):
            sib_copy(i).wait_recv()
            if i + 2 < BANDS:
                pl.when(band != i + 2)(dn_copy(i + 2).wait_send)

                @pl.when(band == i + 2)
                def _():
                    push(row_out.at[0], dn_ref.at[y, x, half], dn_send.at[0], dn_recv.at[band], sibling).wait_recv()

            row_out[i % 2] = (mine_ref[i % 2] + sib_in[i].astype(F32)).astype(BF)
            pl.when(band != i)(dn_copy(i).start)
            pl.when(band == i)(dn_local(i).start)

        def row_back(i, heads):
            cols = pl.ds(i * CAP, CAP)
            limit = counts_of(edges_ref, y, i)
            qts = [q_ref[h, i] for h in heads]
            douts = [do_ref[i, h * HEAD : (h + 1) * HEAD, :] for h in heads]
            pads = [jnp.concatenate([jnp.zeros_like(d), d], axis=0) for d in douts]
            deltas = [
                jnp.sum(d.astype(F32) * o_ref[i, h * HEAD : (h + 1) * HEAD, :].astype(F32), axis=0, keepdims=True)
                for h, d in zip(heads, douts)
            ]
            dqs = [jnp.zeros((HEAD, CAP), F32) for _ in heads]
            for j in range(i + 1):
                keep = key_at < counts_of(edges_ref, y, j)
                if i == j:
                    keep = keep & (key_at <= query_at)
                    alone = (key_at == query_at) & (query_at >= limit)
                for n, h in enumerate(heads):
                    kv = kv_ref[h, j]
                    s = dot(kv, qts[n], NN)
                    dp = dot(kv, pads[n], NN)
                    p = jnp.where(keep, jnp.exp(s - lse_ref[h, i]), 0.0)
                    if i == j:
                        p = jnp.where(alone, 1.0, p)
                    ds = (p * (dp - deltas[n])).astype(BF)
                    dqs[n] = dqs[n] + dot(kt_ref[h, j, :HEAD], ds, NN)
                    more = dot(ds, qts[n], NT) + dot(p.astype(BF), pads[n], NT)
                    if i == BANDS - 1:
                        dk_ref[h, j] = more
                    else:
                        dk_ref[h, j] += more
            for n, h in enumerate(heads):
                d_ref[h * HEAD : (h + 1) * HEAD, cols] = (dqs[n] * 0.125).astype(BF)
                pair = dk_ref[h, i].T.astype(BF)
                d_ref[SHARE + h * HEAD : SHARE + (h + 1) * HEAD, cols] = pair[:HEAD]
                d_ref[2 * SHARE + h * HEAD : 2 * SHARE + (h + 1) * HEAD, cols] = pair[HEAD:]

        def row_return(i):
            dn = dot(d_ref[:, i * CAP : (i + 1) * CAP], wback_ref[...], TN)
            mine_ref[2] = dn[:HALF]
            mine_ref[3] = dn[HALF:]
            if i + 2 < BANDS:
                sib_copy(i + 2).wait_send()
            sib_out[i % 2] = mine_ref[2 + (1 - core)].astype(BF)
            mine_ref[i % 2] = mine_ref[2 + core]
            sib_copy(i).start()
            if i < BANDS - 1:
                finish(i + 1)
            serve(f'd{i}')

        def heads_out(k):
            if k == 0:
                turned_load.wait()
                ones = jnp.ones((8, d_ref.shape[1]), BF)
                total = dot(ones, d_ref[...], NT)
                small_ref[:, : 3 * SHARE] = total
                small_ref[:, 3 * SHARE :] = jnp.zeros((8, width - 3 * SHARE), F32)
            rows = slice(k * 256, (k + 1) * 256)
            dw = dot(n1t_ref[rows, :], d_ref[...], NT)
            sums = small_ref[:1, : 3 * SHARE]
            column = small_ref[:, rows].T[:, :1]
            weight = wback_ref[:, rows].T.astype(F32)
            shift = jnp.sum(weight * sums, axis=1, keepdims=True)
            shift1 = jnp.broadcast_to(as_row(shift1_ref)[:, rows], (8, 256)).T[:, :1]
            gain = jnp.sum(weight * dw, axis=1, keepdims=True) - shift1 * shift
            fq_ref[x, core, k, :, : 3 * SHARE] = dw.astype(BF)
            at = lax.broadcasted_iota(jnp.int32, (256, QLANES - 3 * SHARE), 1)
            tail = jnp.where(at == 0, shift, jnp.where(at == 1, gain, jnp.where(at == 2, column, 0.0)))
            fq_ref[x, core, k, :, 3 * SHARE :] = tail.astype(BF)
            serve(f'q{k}')

        for event in EVENTS:
            kind, i = event[0], int(event[1])
            if kind == "b":
                push(do_ref.at[i], do_ref.at[i], do_send.at[i], do_recv.at[i], sibling).wait_recv()
                if i >= TOGETHER:
                    for h in range(MINE):
                        row_back(i, (h,))
                        serve(f'b{i}{h}')
                else:
                    row_back(i, tuple(range(MINE)))
                    serve(f'b{i}2')
            elif kind == "d":
                row_return(i)
            else:
                heads_out(i)
        finish(0)

    pl.run_scoped(
        backward,
        VM((MINE, BANDS, CAP, 128), F32),
        VM((3 * SHARE, BANDS * CAP), BF),
        VM((4, HALF, width), F32),
        VM((width, BANDS * CAP), BF),
        VM((8, width), F32),
    )
    serve('end')
    left = [[k] * (len(chain.steps) + 1 - chain.at) for k, chain in enumerate(chains)]
    while any(left):
        for k, rest in enumerate(left):
            if rest:
                chains[rest.pop()].advance()

    for i in range(BANDS):
        copy = push(part_for(i), do_ref.at[i], do_send.at[i], do_recv.at[i], sibling)
        pl.when(band != i)(copy.wait_send)
        if i < 2:
            sib_copy(i).wait_send()
            pl.when(band != i)(dn_copy(i).wait_send)
    for i in range(BANDS):
        from_y, from_x, from_core = i // 4, i // 2 % 2, i % 2
        arrived = push(row_out.at[0], dn_ref.at[from_y, from_x, pl.ds(from_core * HALF, HALF)],
                       dn_send.at[i], dn_recv.at[i], sibling)
        if i < 2:
            arrived.wait_recv()
        else:
            pl.when(band != i)(arrived.wait_recv)
    for chain in chains:
        chain.drain()
    layer_out.wait()
    dmid_out.wait()


def layer_call(edges, exits, vecs, h, cot, wout, wq, wk, wv, wup, wdown):
    width = h.shape[1]
    seq = BANDS * CAP
    vm = pl.BlockSpec(memory_space=VM)
    hbm = pl.BlockSpec(memory_space=pl.ANY)
    dma, credit = pltpu.SemaphoreType.DMA, pltpu.SemaphoreType.REGULAR
    eight = dma((BANDS,))

    def room(*shape):
        return VM(shape, BF)

    def spots(number, rows, lanes, levels):
        return [room(number, rows // 2**k, lanes) for k in levels]

    def sems(number, steps, levels):
        return [dma((number, steps)), dma((number, steps)), credit((number, levels)), dma((number,))]

    parts_d, parts_u = BLOCKS + 2, BLOCKS
    return pl.pallas_call(
        layer_kernel,
        name="layer",
        out_shape=[
            jax.ShapeDtypeStruct((2, 2, CAP, width), BF),
            jax.ShapeDtypeStruct(h.shape, BF),
            jax.ShapeDtypeStruct(h.shape, F32),
            jax.ShapeDtypeStruct((2, 2, 3, 256, QLANES), BF),
            jax.ShapeDtypeStruct((parts_d, 2, 256, width), BF),
            jax.ShapeDtypeStruct((parts_u, 2, width, 256), BF),
            jax.ShapeDtypeStruct((width, seq), BF),
        ],
        in_specs=[pl.BlockSpec(memory_space=pltpu.SMEM)] + [vm] * 13 + [hbm] * 5,
        out_specs=[vm] + [hbm] * 6,
        scratch_shapes=[room(parts_d, 2, 256, width), room(parts_u, 2, width, 256), room(2, 2, 3, 256, QLANES)]
        + spots(parts_d, 256, width, (0, 1, 2, 3, 3))
        + spots(parts_u, width, 256, (0, 1, 2, 3, 3))
        + spots(3, 256, QLANES, (1, 2, 2))
        + [
            room(*h.shape), VM(h.shape, F32),
            room(MINE, BANDS, 128, CAP), room(MINE, BANDS, CAP, 128), room(MINE, BANDS, 128, CAP),
            room(2 * CAP, width), room(width, 2 * CAP), room(BANDS, SHARE, CAP),
            room(2, HALF, width), room(BANDS, HALF, width), room(2, HALF, width),
            room(BANDS, SHARE, CAP), VM((MINE, BANDS, 1, CAP), F32), room(width, 2 * CAP), room(3 * SHARE, width),
        ]
        + sems(parts_d, 9, 5) + sems(parts_u, 9, 5) + sems(3, 7, 3)
        + [eight] * 8 + [dma((6,)), dma((2, 2)), dma((2,)), dma((13,)), dma((13,)), dma((3,))],
        compiler_params=pltpu.CompilerParams(
            collective_id=1, has_side_effects=True, vmem_limit_bytes=63 * 2**20
        ),
    )(edges, exits, *vecs, h, cot, wout, wq, wk, wv, wup, wdown)


SLOTS = 6


def finish_kernel(
    gain_ref, h_ref, dmid_ref, dn_ref, fd_hbm, fu_hbm, fq_hbm,
    grad_ref, g1_ref, b1_ref, qb_ref, vb_ref, ob_ref, g2_ref, b2_ref, ub_ref, db_ref,
    qw_hbm, kw_hbm, vw_hbm, ow_hbm, uw_hbm, dw_hbm,
    in_d, in_u, in_q, out_d, out_u, square, load_d, load_u, load_q, store_d, store_u, store_q,
):
    width = h_ref.shape[1]
    tail = (BLOCKS + 1, 1)
    halves_d = [tail] + [(f, c) for f in range(BLOCKS + 2) for c in range(2) if (f, c) != tail]
    halves_u = [(f, c) for f in range(BLOCKS) for c in range(2)]

    def load_of(kind, f, c):
        src, dst, sem = ((fd_hbm, in_d, load_d), (fu_hbm, in_u, load_u))[kind]
        return pltpu.make_async_copy(src.at[f, c], dst.at[f, c], sem.at[f, c])

    def q_load(g, k):
        return pltpu.make_async_copy(
            fq_hbm.at[g // 2, g % 2, k], in_q.at[g // 2, g % 2, k], load_q.at[g, k]
        )

    for k in range(max(len(halves_d), len(halves_u))):
        if k < len(halves_d):
            load_of(0, *halves_d[k]).start()
        if k < len(halves_u):
            load_of(1, *halves_u[k]).start()
    for k in range(3):
        for g in range(4):
            q_load(g, k).start()

    load_of(0, *tail).wait()
    rest = in_d[tail[0], tail[1], :16, :].astype(F32)
    count = rest[12:13, :3]
    total = 64.0 * count[:, 0:1] + 8.0 * count[:, 1:2] + count[:, 2:3]
    scale = 1.0 / total

    def store_of(kind, k):
        if kind == 0:
            f, c = halves_d[1:][k]
            row = f * BLOCK + c * 256
            target = dw_hbm.at[pl.ds(row, 256)] if f < BLOCKS else ow_hbm.at[pl.ds(row - BLOCKS * BLOCK, 256)]
            return pltpu.make_async_copy(out_d.at[k % SLOTS], target, store_d.at[k % SLOTS])
        f, c = halves_u[k]
        target = uw_hbm.at[:, pl.ds(f * BLOCK + c * 256, 256)]
        return pltpu.make_async_copy(out_u.at[k % SLOTS], target, store_u.at[k % SLOTS])

    def convert(kind, k):
        f, c = halves_u[k] if kind else halves_d[1:][k]
        source, out = ((in_d, out_d), (in_u, out_u))[kind]
        load_of(kind, f, c).wait()
        if k >= SLOTS:
            store_of(kind, k - SLOTS).wait()
        step = 64 if kind == 0 else 192

        def some(r, carry):
            at = pl.ds(pl.multiple_of(r * step, step), step)
            out[k % SLOTS, at, :] = source[f, c, at, :].astype(F32) * scale
            return carry

        lax.fori_loop(0, source.shape[2] // step, some, 0)
        store_of(kind, k).start()

    number_d, number_u = len(halves_d) - 1, len(halves_u)
    for k in range(max(number_d, number_u)):
        if k < number_d:
            convert(0, k)
        if k < number_u:
            convert(1, k)

    outs = (qw_hbm, kw_hbm, vw_hbm)

    def q_store(which, k):
        rows = pl.ds(k * 256, 256)
        return pltpu.make_async_copy(square.at[which, rows], outs[which].at[rows], store_q.at[which, k])

    for k in range(3):
        for g in range(4):
            q_load(g, k).wait()
        for which in range(3):
            square[which, k * 256 : (k + 1) * 256, :] = jnp.concatenate(
                [
                    in_q[g // 2, g % 2, k, :, which * SHARE : (which + 1) * SHARE].astype(F32) * scale
                    for g in range(4)
                ],
                axis=1,
            )
            q_store(which, k).start()

    hidden = h_ref[...].astype(F32)
    center = hidden - jnp.mean(hidden, axis=-1, keepdims=True)
    spread = jnp.mean(center * center, axis=-1, keepdims=True)
    scale1 = lax.rsqrt(spread + 1e-05)
    xhat = center * scale1
    dn1 = jnp.concatenate([dn_ref[s, 0].astype(F32) + dn_ref[s, 1].astype(F32) for s in range(2)], axis=0)
    gain = as_row(gain_ref)
    e1 = dn1 * gain
    grad_ref[...] = dmid_ref[...] + scale1 * (
        e1 - jnp.mean(e1, axis=-1, keepdims=True) - xhat * jnp.mean(e1 * xhat, axis=-1, keepdims=True)
    )

    gain1 = shift1 = jnp.zeros((1, width), F32)
    query_b, value_b = [], []
    for g in range(4):
        block = jnp.concatenate(
            [in_q[g // 2, g % 2, k, :, 3 * SHARE - HEAD :].T for k in range(3)], axis=1
        )[HEAD : HEAD + 16]
        shift1 = shift1 + block[0:1].astype(F32)
        gain1 = gain1 + block[1:2].astype(F32)
        query_b.append(block[2:3, :SHARE].astype(F32))
        value_b.append(block[2:3, 2 * SHARE : 3 * SHARE].astype(F32))
    query_b, value_b = jnp.concatenate(query_b, axis=1), jnp.concatenate(value_b, axis=1)
    for ref, value in (
        (g1_ref, gain1 / gain), (b1_ref, shift1), (qb_ref, query_b), (vb_ref, value_b),
        (ob_ref, rest[9:10]), (g2_ref, rest[10:11]), (b2_ref, rest[11:12]), (db_ref, rest[8:9]),
    ):
        ref[...] = (value * scale).reshape(width)
    ub_ref[...] = (jnp.concatenate([rest[f : f + 1, :BLOCK] for f in range(BLOCKS)], axis=1) * scale).reshape(
        BLOCKS * BLOCK
    )
    for k in range(3):
        for which in range(3):
            q_store(which, k).wait()
    for k in range(number_d - SLOTS, number_d):
        store_of(0, k).wait()
    for k in range(number_u - SLOTS, number_u):
        store_of(1, k).wait()


def finish_call(gain, h, dmid, dn, fd, fu, fq):
    width = h.shape[1]
    vm = pl.BlockSpec(memory_space=VM)
    hbm = pl.BlockSpec(memory_space=pl.ANY)
    dma = pltpu.SemaphoreType.DMA
    hidden = BLOCKS * BLOCK
    flat = jax.ShapeDtypeStruct((width, width), F32)
    line = jax.ShapeDtypeStruct((width,), F32)
    return pl.pallas_call(
        finish_kernel,
        name="finish",
        out_shape=[jax.ShapeDtypeStruct(h.shape, F32)]
        + [line] * 7
        + [jax.ShapeDtypeStruct((hidden,), F32), line]
        + [flat] * 4
        + [jax.ShapeDtypeStruct((width, hidden), F32), jax.ShapeDtypeStruct((hidden, width), F32)],
        in_specs=[vm] * 4 + [hbm] * 3,
        out_specs=[vm] * 10 + [hbm] * 6,
        scratch_shapes=[
            VM(fd.shape, BF), VM(fu.shape, BF), VM(fq.shape, BF),
            VM((SLOTS, 256, width), F32), VM((SLOTS, width, 256), F32), VM((3, width, width), F32),
            dma(fd.shape[:2]), dma(fu.shape[:2]), dma((4, 3)), dma((SLOTS,)), dma((SLOTS,)), dma((3, 3)),
        ],
        compiler_params=pltpu.CompilerParams(vmem_limit_bytes=56 * 2**20),
    )(gain, h, dmid, dn, fd, fu, fq)


def norm_rows(values):
    center = values - jnp.mean(values, axis=-1, keepdims=True)
    spread = jnp.mean(center * center, axis=-1, keepdims=True)
    return center * lax.rsqrt(spread + 1e-05)


def norm_affine(values, gain_vec, shift_vec):
    return norm_rows(values) * gain_vec + shift_vec


def left_product(left_mat, right_mat):
    return lax.dot_general(
        left_mat, right_mat, (((0,), (0,)), ((), ())), preferred_element_type=jnp.float32
    )


def right_product(left_mat, weight):
    return lax.dot_general(
        left_mat, weight, (((1,), (1,)), ((), ())), preferred_element_type=jnp.float32
    )


def slot_tags(first_row, count_rows, layout):
    begins_flat, finishes_flat, slot_rows, band_cap, band_count = layout
    slot_index = first_row + jnp.arange(count_rows, dtype=jnp.int32)
    owner = slot_index // slot_rows
    within = slot_index - owner * slot_rows
    member = within // band_cap
    offset = within - member * band_cap
    flat_code = member * band_count + owner
    all_codes = jnp.arange(begins_flat.shape[0], dtype=jnp.int32)
    hit_table = flat_code[:, None] == all_codes[None, :]
    begins = jnp.sum(jnp.where(hit_table, begins_flat[None, :], 0), axis=1)
    finish = jnp.sum(jnp.where(hit_table, finishes_flat[None, :], 0), axis=1)
    position = begins + offset
    return (member, position, position < finish, slot_index)


def allowed_pairs(query_tags, key_tags):
    query_member, query_position, query_valid, query_slot = query_tags
    key_member, key_position, key_valid, key_slot = key_tags
    same_slot = query_slot[:, None] == key_slot[None, :]
    causal = (query_member[:, None] == key_member[None, :]) & (
        key_position[None, :] <= query_position[:, None]
    )
    return same_slot | query_valid[:, None] & key_valid[None, :] & causal


def on_device(
    residual_in,
    exit_layer,
    band_edges,
    norm1_gain,
    norm1_bias,
    query_weight,
    query_bias,
    key_weight,
    value_weight,
    value_bias,
    out_weight,
    out_bias,
    norm2_gain,
    norm2_bias,
    up_weight,
    up_bias,
    down_weight,
    down_bias,
    cotangent,
):
    slot_rows = residual_in.shape[1]
    model_width = residual_in.shape[2]
    head_size = model_width // HEADS
    score_scale = head_size ** (-0.5)
    band_here = lax.axis_index("band")
    band_count = lax.axis_size("band")
    band_cap = slot_rows // band_edges.shape[1]
    finishes = jnp.concatenate([band_edges[0][:, 1:], band_edges[0][:, -1:] + band_cap], axis=1)
    layout = (band_edges[0].reshape(-1), finishes.reshape(-1), slot_rows, band_cap, band_count)
    own_tags = slot_tags(band_here * slot_rows, slot_rows, layout)
    active = ((exit_layer[0] >= LAYER) & own_tags[2]).astype(jnp.float32)[:, None]
    total_active = lax.psum(jnp.sum(active), ("band", "batch"))
    hidden_in = residual_in[0].astype(jnp.float32)
    normed_one, norm_one_back = jax.vjp(
        norm_affine, hidden_in, norm1_gain.astype(jnp.float32), norm1_bias.astype(jnp.float32)
    )
    normed_low = normed_one.astype(jnp.bfloat16)
    queries = (
        jnp.dot(normed_low, query_weight, preferred_element_type=jnp.float32)
        + query_bias.astype(jnp.float32)
    ).astype(jnp.bfloat16)
    keys_own = jnp.dot(normed_low, key_weight, preferred_element_type=jnp.float32).astype(
        jnp.bfloat16
    )
    values_own = (
        jnp.dot(normed_low, value_weight, preferred_element_type=jnp.float32)
        + value_bias.astype(jnp.float32)
    ).astype(jnp.bfloat16)
    query_heads = queries.reshape(slot_rows, HEADS, head_size)
    start_state = (
        jnp.full((HEADS, slot_rows), -1e30, jnp.float32),
        jnp.zeros((HEADS, slot_rows), jnp.float32),
        jnp.zeros((slot_rows, HEADS, head_size), jnp.float32),
    )
    key_piece = lax.all_gather(keys_own, "band", axis=0, tiled=True)
    value_piece = lax.all_gather(values_own, "band", axis=0, tiled=True)
    piece_rows = key_piece.shape[0]
    step_rows = min(piece_rows, slot_rows)

    def one_step(step_index, inner_state):
        offset_row = step_index * step_rows
        key_block = lax.dynamic_slice_in_dim(key_piece, offset_row, step_rows, 0).reshape(
            step_rows, HEADS, head_size
        )
        value_block = lax.dynamic_slice_in_dim(value_piece, offset_row, step_rows, 0).reshape(
            step_rows, HEADS, head_size
        )
        mask = allowed_pairs(own_tags, slot_tags(offset_row, step_rows, layout))

        def accumulate(running):
            top_old, total_old, sum_old = running
            scores = (
                jnp.einsum(
                    "qhd,khd->hqk", query_heads, key_block, preferred_element_type=jnp.float32
                )
                * score_scale
            )
            scores = jnp.where(mask[None], scores, -1e30)
            top_new = jnp.maximum(top_old, jnp.max(scores, axis=-1))
            rescale = jnp.exp(top_old - top_new)
            weights_new = jnp.where(mask[None], jnp.exp(scores - top_new[..., None]), 0.0)
            total_new = total_old * rescale + jnp.sum(weights_new, axis=-1)
            sum_new = sum_old * rescale.T[..., None] + jnp.einsum(
                "hqk,khd->qhd",
                weights_new.astype(jnp.bfloat16),
                value_block,
                preferred_element_type=jnp.float32,
            )
            return (top_new, total_new, sum_new)

        return lax.cond(jnp.any(mask), accumulate, lambda running: running, inner_state)

    top_score, weight_total, weighted_sum = lax.fori_loop(
        0, piece_rows // step_rows, one_step, start_state
    )
    attended = weighted_sum / weight_total.T[..., None]
    log_total = top_score + jnp.log(weight_total)
    mixed_low = attended.reshape(slot_rows, model_width).astype(jnp.bfloat16)
    branch = jnp.dot(mixed_low, out_weight, preferred_element_type=jnp.float32) + out_bias.astype(
        jnp.float32
    )
    middle = hidden_in + active * branch
    normed_two, norm_two_back = jax.vjp(
        norm_affine, middle, norm2_gain.astype(jnp.float32), norm2_bias.astype(jnp.float32)
    )
    normed_two_low = normed_two.astype(jnp.bfloat16)
    pre_act = jnp.dot(
        normed_two_low, up_weight, preferred_element_type=jnp.float32
    ) + up_bias.astype(jnp.float32)
    activated, gelu_back = jax.vjp(jax.nn.gelu, pre_act)
    activated_low = activated.astype(jnp.bfloat16)
    down_out = jnp.dot(
        activated_low, down_weight, preferred_element_type=jnp.float32
    ) + down_bias.astype(jnp.float32)
    layer_out = (middle + active * down_out).astype(jnp.bfloat16)[None]
    out_grad = cotangent[0].astype(jnp.float32)
    down_grad = (active * out_grad).astype(jnp.bfloat16)
    down_weight_sum = left_product(activated_low, down_grad)
    down_bias_sum = jnp.sum(down_grad.astype(jnp.float32), axis=0)
    (pre_grad,) = gelu_back(right_product(down_grad, down_weight))
    pre_low = pre_grad.astype(jnp.bfloat16)
    up_weight_sum = left_product(normed_two_low, pre_low)
    up_bias_sum = jnp.sum(pre_low.astype(jnp.float32), axis=0)
    middle_norm, gain_two_sum, shift_two_sum = norm_two_back(right_product(pre_low, up_weight))
    middle_grad = out_grad + middle_norm
    branch_grad = (active * middle_grad).astype(jnp.bfloat16)
    out_weight_sum = left_product(mixed_low, branch_grad)
    out_bias_sum = jnp.sum(branch_grad.astype(jnp.float32), axis=0)
    mixed_grad = right_product(branch_grad, out_weight).astype(jnp.bfloat16)
    grad_heads = mixed_grad.reshape(slot_rows, HEADS, head_size)
    delta_row = jnp.sum(grad_heads.astype(jnp.float32) * attended, axis=-1).T

    def pair_terms(query_blk, grad_blk, logsum_blk, delta_blk, key_block, value_block, mask):
        scores = (
            jnp.einsum("qhd,khd->hqk", query_blk, key_block, preferred_element_type=jnp.float32)
            * score_scale
        )
        probability = jnp.where(mask[None], jnp.exp(scores - logsum_blk[..., None]), 0.0)
        prob_grad = jnp.einsum(
            "qhd,khd->hqk", grad_blk, value_block, preferred_element_type=jnp.float32
        )
        score_grad = (probability * (prob_grad - delta_blk[..., None])).astype(jnp.bfloat16)
        return (probability.astype(jnp.bfloat16), score_grad)

    all_rows = slot_rows * band_count
    start_back = (
        jnp.zeros((slot_rows, HEADS, head_size), jnp.float32),
        jnp.zeros((all_rows, model_width), jnp.float32),
        jnp.zeros((all_rows, model_width), jnp.float32),
    )
    fold_key_piece = lax.all_gather(keys_own, "band", axis=0, tiled=True)
    fold_value_piece = lax.all_gather(values_own, "band", axis=0, tiled=True)
    piece_rows = fold_key_piece.shape[0]
    fold_step_rows = min(piece_rows, slot_rows)

    def one_step(step_index, inner_state):
        offset_row = step_index * fold_step_rows
        key_block = lax.dynamic_slice_in_dim(fold_key_piece, offset_row, fold_step_rows, 0).reshape(
            fold_step_rows, HEADS, head_size
        )
        value_block = lax.dynamic_slice_in_dim(
            fold_value_piece, offset_row, fold_step_rows, 0
        ).reshape(fold_step_rows, HEADS, head_size)
        mask = allowed_pairs(own_tags, slot_tags(offset_row, fold_step_rows, layout))

        def accumulate(running):
            query_acc, key_sums, value_sums = running
            prob_low, score_grad = pair_terms(
                query_heads, grad_heads, log_total, delta_row, key_block, value_block, mask
            )
            query_acc = (
                query_acc
                + jnp.einsum(
                    "hqk,khd->qhd", score_grad, key_block, preferred_element_type=jnp.float32
                )
                * score_scale
            )
            key_term = (
                jnp.einsum(
                    "hqk,qhd->khd", score_grad, query_heads, preferred_element_type=jnp.float32
                ).reshape(fold_step_rows, model_width)
                * score_scale
            )
            value_term = jnp.einsum(
                "hqk,qhd->khd", prob_low, grad_heads, preferred_element_type=jnp.float32
            ).reshape(fold_step_rows, model_width)
            key_sums = lax.dynamic_update_slice_in_dim(
                key_sums,
                lax.dynamic_slice_in_dim(key_sums, offset_row, fold_step_rows, 0) + key_term,
                offset_row,
                0,
            )
            value_sums = lax.dynamic_update_slice_in_dim(
                value_sums,
                lax.dynamic_slice_in_dim(value_sums, offset_row, fold_step_rows, 0) + value_term,
                offset_row,
                0,
            )
            return (query_acc, key_sums, value_sums)

        return lax.cond(jnp.any(mask), accumulate, lambda running: running, inner_state)

    back_state = lax.fori_loop(0, piece_rows // fold_step_rows, one_step, start_back)
    query_sum, key_sums_all, value_sums_all = back_state
    key_sum, value_sum = (
        lax.psum_scatter(
            key_sums_all.astype(jnp.bfloat16), "band", scatter_dimension=0, tiled=True
        ).astype(jnp.float32),
        lax.psum_scatter(
            value_sums_all.astype(jnp.bfloat16), "band", scatter_dimension=0, tiled=True
        ).astype(jnp.float32),
    )
    query_low = query_sum.reshape(slot_rows, model_width).astype(jnp.bfloat16)
    key_low = key_sum.astype(jnp.bfloat16)
    value_low = value_sum.astype(jnp.bfloat16)
    query_weight_sum = left_product(normed_low, query_low)
    query_bias_sum = jnp.sum(query_low.astype(jnp.float32), axis=0)
    key_weight_sum = left_product(normed_low, key_low)
    value_weight_sum = left_product(normed_low, value_low)
    value_bias_sum = jnp.sum(value_low.astype(jnp.float32), axis=0)
    normed_grad = (
        right_product(query_low, query_weight)
        + right_product(key_low, key_weight)
        + right_product(value_low, value_weight)
    )
    input_norm, gain_one_sum, shift_one_sum = norm_one_back(normed_grad)
    input_grad = (middle_grad + input_norm)[None]
    (
        total_g1,
        total_b1,
        total_qw,
        total_qb,
        total_kw,
        total_vw,
        total_vb,
        total_ow,
        total_ob,
        total_g2,
        total_b2,
        total_uw,
        total_ub,
        total_dw,
        total_db,
    ) = lax.psum(
        (
            gain_one_sum,
            shift_one_sum,
            query_weight_sum,
            query_bias_sum,
            key_weight_sum,
            value_weight_sum,
            value_bias_sum,
            out_weight_sum,
            out_bias_sum,
            gain_two_sum,
            shift_two_sum,
            up_weight_sum,
            up_bias_sum,
            down_weight_sum,
            down_bias_sum,
        ),
        ("band", "batch"),
    )
    return (
        layer_out,
        input_grad,
        total_g1 / total_active,
        total_b1 / total_active,
        total_qw / total_active,
        total_qb / total_active,
        total_kw / total_active,
        total_vw / total_active,
        total_vb / total_active,
        total_ow / total_active,
        total_ob / total_active,
        total_g2 / total_active,
        total_b2 / total_active,
        total_uw / total_active,
        total_ub / total_active,
        total_dw / total_active,
        total_db / total_active,
    )


def fast_device(
    residual_in, exit_layer, band_edges, norm1_gain, norm1_bias, query_weight, query_bias,
    key_weight, value_weight, value_bias, out_weight, out_bias, norm2_gain, norm2_bias,
    up_weight, up_bias, down_weight, down_bias, cotangent,
):
    h, cot = residual_in[0], cotangent[0]
    vecs = (
        norm1_gain, norm1_bias, query_bias, value_bias, out_bias, norm2_gain, norm2_bias, down_bias, up_bias
    )
    dn, layer, dmid, fq, fd, fu, _ = layer_call(
        band_edges, exit_layer, vecs, h, cot, out_weight, query_weight, key_weight, value_weight,
        up_weight, down_weight,
    )
    grad, g1, b1, qb, vb, ob, g2, b2, ub, db, qw, kw, vw, ow, uw, dw = finish_call(
        norm1_gain, h, dmid, dn, fd, fu, fq
    )
    return (layer[None], grad[None], g1, b1, qw, qb, kw, vw, vb, ow, ob, g2, b2, uw, ub, dw, db)


def solution(mesh):
    placed = (
        (P("batch", "band", None), P("batch", "band"), P("batch", None, None))
        + (P(),) * 15
        + (P("batch", "band", None),)
    )
    fast = mesh.shape["band"] == BANDS and mesh.shape["batch"] == 4
    return jax.shard_map(
        fast_device if fast else on_device,
        mesh=mesh,
        in_specs=placed,
        out_specs=(P("batch", "band", None),) * 2 + (P(),) * 15,
        check_vma=False,
    )
```

```python
import functools

import jax
import jax.numpy as jnp
from jax import lax
from jax.experimental import pallas as pl
from jax.experimental.pallas import tpu as pltpu
from jax.sharding import PartitionSpec as P

MESH = pl.DeviceIdType.MESH
VM = pltpu.VMEM
BF = jnp.bfloat16
F32 = jnp.float32
HEADS = 12
LAYER = 6
HEAD = 64
BANDS = 8
CAP = 256
HALF = 128
MINE = 3
SHARE = MINE * HEAD
NEG = -1e30


def place():
    band = lax.axis_index("band")
    return band, band // 4, (band // 2) % 2, band % 2


def device(y, x, core):
    return (y * 4 + x * 2 + core, lax.axis_index("batch"))


def push(src, dst, send, recv, target):
    return pltpu.make_async_remote_copy(
        src_ref=src, dst_ref=dst, send_sem=send, recv_sem=recv, device_id=target, device_id_type=MESH
    )


def dot(a, b, dims):
    return lax.dot_general(a, b, ((dims[0], dims[1]), ((), ())), preferred_element_type=F32)


NN = ((1,), (0,))
NT = ((1,), (1,))
TN = ((0,), (0,))


def as_row(ref):
    return ref[...].astype(F32).reshape(1, -1)


def counts_of(edges_ref, seq, band):
    after = edges_ref[0, seq, jnp.minimum(band + 1, BANDS - 1)]
    return jnp.where(band == BANDS - 1, CAP, after - edges_ref[0, seq, band])


def greet():
    band, _, _, _ = place()
    batch = lax.axis_index("batch")
    links = partners()
    barrier = pltpu.get_barrier_semaphore()
    for step in range(1, BANDS):
        pl.semaphore_signal(barrier, inc=1, device_id=((band + step) % BANDS, batch), device_id_type=MESH)
    for axis in ("a", "b"):
        pl.semaphore_signal(barrier, inc=1, device_id=links[axis][1], device_id_type=MESH)
    pl.semaphore_wait(barrier, BANDS + 1)


def attend(
    edges_ref, gain_ref, shift_ref, bq_ref, bv_ref, h_ref, wq_hbm, wk_hbm, wv_hbm,
    o_ref, lse_ref, att_ref, wback_ref, n1t_hbm, q_ref, kv_ref, kvt_ref, rows_at,
    send, recv, out_send, out_recv, load, store,
    n1t_ref, cols_ref, turned_ref, top_ref, total_ref, mix_ref,
):
    band, y, x, core = place()
    width = h_ref.shape[1]
    group = 2 * x + core
    wide = pl.ds(pl.multiple_of(x * 2 * SHARE + core * 128, 128), 256)
    loads = [
        pltpu.make_async_copy(ref.at[:, wide], cols_ref.at[k], load.at[k])
        for k, ref in enumerate((wq_hbm, wk_hbm, wv_hbm))
    ]
    for copy in loads:
        copy.start()
    greet()
    own = pl.ds(pl.multiple_of(y * CAP, CAP), CAP)
    half = pl.ds(pl.multiple_of(core * HALF, HALF), HALF)
    other_y, other_x, other_core = 1 - y, 1 - x, 1 - core
    sibling = device(y, x, other_core)
    copies = {}

    def go(name, src, dst, index, recv_index, target):
        copy = push(src, dst, send.at[index], recv.at[recv_index], target)
        copy.start()
        copies[name] = copy

    for k in range(2):
        from_rows = pl.ds(pl.multiple_of(other_y * CAP + k * HALF, HALF), HALF)
        go(("y", k), h_ref.at[from_rows], rows_at(band).at[pl.ds(k * HALF, HALF)], 1 + k, 1 + core,
           device(other_y, x, k))
    for k in range(2):
        from_rows = pl.ds(pl.multiple_of(y * CAP + k * HALF, HALF), HALF)
        go(("x", k), h_ref.at[from_rows], rows_at(band).at[pl.ds(k * HALF, HALF)], 3 + k, 3 + core,
           device(y, other_x, k))
    go("sib", h_ref.at[own], rows_at(band), 0, 0, sibling)

    gain, shift = as_row(gain_ref), as_row(shift_ref)
    for k, copy in enumerate(loads):
        copy.wait()
        turned_ref[k] = cols_ref[k].T
        for h in range(MINE):
            part = turned_ref[k, pl.ds(pl.multiple_of(core * HEAD + h * HEAD, HEAD), HEAD), :]
            at = k * SHARE + h * HEAD
            wback_ref[at : at + HEAD, :] = part
    row = lax.broadcasted_iota(jnp.int32, (3 * SHARE, width), 0)
    col = lax.broadcasted_iota(jnp.int32, (3 * SHARE, width), 1) - group * SHARE
    pick_q = jnp.where((row == col) & (row < SHARE), 1.0, 0.0).astype(BF)
    pick_v = jnp.where((row - 2 * SHARE == col) & (row >= 2 * SHARE), 1.0, 0.0).astype(BF)

    def spread_row(ref):
        return jnp.broadcast_to(as_row(ref), (8, width)).astype(BF)

    bias = (dot(pick_q, spread_row(bq_ref), NT) + dot(pick_v, spread_row(bv_ref), NT))[:, :1]

    def project(rows, which):
        wide_rows = rows.astype(F32)
        center = wide_rows - jnp.mean(wide_rows, axis=-1, keepdims=True)
        spread = jnp.mean(center * center, axis=-1, keepdims=True)
        n1 = (center * lax.rsqrt(spread + 1e-05) * gain + shift).astype(BF)
        at = pl.ds(pl.multiple_of(which * CAP, CAP), CAP)
        n1t_ref[:, at] = n1.T
        all_t = dot(wback_ref[...], n1, NT) + bias
        qt = (all_t[:SHARE] * 0.125).astype(BF)
        kvt = all_t[SHARE:].astype(BF)
        for h in range(MINE):
            one = jnp.concatenate(
                [kvt[h * HEAD : (h + 1) * HEAD], kvt[SHARE + h * HEAD : SHARE + (h + 1) * HEAD]], axis=0
            )
            kvt_ref[h, which] = one
            kv_ref[h, which] = one.T
            q_ref[h, which, :HEAD] = qt[h * HEAD : (h + 1) * HEAD]
            q_ref[h, which, HEAD:] = jnp.zeros((HEAD, CAP), BF)

    def project_two(first_y, first_x):
        def one(k, carry):
            which = first_y * 4 + first_x * 2 + k
            project(rows_at(which)[...], which)
            return carry

        lax.fori_loop(0, 2, one, 0)

    rows_at(band)[...] = h_ref[own, :]

    def wait_recv(index, which, size=HALF):
        ref = rows_at(which) if size == CAP else rows_at(which).at[half]
        push(ref, ref, send.at[0], recv.at[index], sibling).wait_recv()

    wait_recv(0, y * 4 + x * 2 + other_core, CAP)
    project_two(y, x)
    for k in range(2):
        from_band = other_y * 4 + x * 2 + k
        wait_recv(1 + k, from_band)
        piece = rows_at(from_band).at[half]
        go(("fx", k), piece, piece, 5 + k, 5 + k, device(y, other_x, core))
        go(("fs", k), piece, piece, 7 + k, 7 + k, sibling)
    for k in range(2):
        from_band = y * 4 + other_x * 2 + k
        wait_recv(3 + k, from_band)
        piece = rows_at(from_band).at[half]
        go(("fs", 2 + k), piece, piece, 9 + k, 9 + k, sibling)
    for k in range(2):
        copies[("fs", k)].wait_recv()
    project_two(other_y, x)
    for k in range(2):
        copies[("fs", 2 + k)].wait_recv()
    project_two(y, other_x)

    key_at = lax.broadcasted_iota(jnp.int32, (CAP, CAP), 0)
    query_at = lax.broadcasted_iota(jnp.int32, (CAP, CAP), 1)
    lane = lax.broadcasted_iota(jnp.int32, (1, CAP), 1)
    share = pl.ds(pl.multiple_of(group * SHARE, SHARE), SHARE)
    side = pl.ds(pl.multiple_of(y * CAP, CAP), CAP)

    def absorb(i, keys, fresh):
        scores, tops, totals, mixes = [], [], [], []
        keeps = []
        for number, j in enumerate(keys):
            keep = key_at < counts_of(edges_ref, y, j)
            if fresh and number == len(keys) - 1:
                keep = keep & (key_at <= query_at)
            keeps.append(keep)
        for h in range(MINE):
            qt = q_ref[h, i]
            scores.append([jnp.where(keep, dot(kv_ref[h, j], qt, NN), NEG) for j, keep in zip(keys, keeps)])
        for h in range(MINE):
            top = functools.reduce(jnp.maximum, [jnp.max(s, axis=0, keepdims=True) for s in scores[h]])
            if fresh:
                total = jnp.zeros((1, CAP), F32)
                mix = jnp.zeros((HEAD, CAP), F32)
            else:
                before = top_ref[h, i]
                top = jnp.maximum(top, before)
                rescale = jnp.exp(before - top)
                total = total_ref[h, i] * rescale
                mix = mix_ref[h, i] * rescale
            for s, j in zip(scores[h], keys):
                p = jnp.exp(s - top)
                total = total + jnp.sum(p, axis=0, keepdims=True)
                mix = mix + dot(kvt_ref[h, j, HEAD:], p.astype(BF), NN)
            tops.append(top)
            totals.append(total)
            mixes.append(mix)
        for h in range(MINE):
            top_ref[h, i] = tops[h]
            total_ref[h, i] = totals[h]
            mix_ref[h, i] = mixes[h]

    def settle(pair):
        for r in range(2):
            i = 2 * pair + r
            valid = lane < counts_of(edges_ref, y, i)
            for h in range(MINE):
                total = total_ref[h, i]
                mix = jnp.where(valid, mix_ref[h, i] / total, kvt_ref[h, i, HEAD:].astype(F32))
                o_ref[i, h * HEAD : (h + 1) * HEAD, :] = mix.astype(BF)
                lse_ref[h, i] = jnp.where(valid, top_ref[h, i] + jnp.log(total), -NEG)
            copy = push(o_ref.at[i], att_ref.at[share, side], out_send.at[i], out_recv.at[band],
                        (i, lax.axis_index("batch")))
            pl.when(band != i)(copy.start)
            local = pltpu.make_async_copy(o_ref.at[i], att_ref.at[share, side], out_recv.at[band])
            pl.when(band == i)(local.start)

    late = 3 - (2 * y + x)
    early = [jnp.where(late <= k, k + 1, k) for k in range(3)]
    for a in range(3):
        before = [2 * early[b] + r for b in range(a) for r in range(2)]
        absorb(2 * early[a], before + [2 * early[a]], True)
        absorb(2 * early[a] + 1, before + [2 * early[a], 2 * early[a] + 1], True)
    for k in range(2):
        from_band = other_y * 4 + other_x * 2 + k
        copies[("fx", k)].wait_recv()
        piece = rows_at(from_band).at[half]
        go(("fs", 4 + k), piece, piece, 11 + k, 11 + k, sibling)
    for a in range(3):
        pl.when(early[a] < late)(functools.partial(settle, early[a]))
    for k in range(2):
        copies[("fs", 4 + k)].wait_recv()
    project_two(other_y, other_x)
    keep_turned = pltpu.make_async_copy(n1t_ref, n1t_hbm, store)
    keep_turned.start()
    for a in range(3):
        query, key = jnp.maximum(early[a], late), jnp.minimum(early[a], late)
        if a == 0:
            absorb(2 * late, [2 * late], True)
            absorb(2 * late + 1, [2 * late, 2 * late + 1], True)
        for r in range(2):
            absorb(2 * query + r, [2 * key, 2 * key + 1], False)
        pl.when(early[a] > late)(functools.partial(settle, early[a]))
    settle(late)
    for i in range(BANDS):
        from_y, from_x, from_core = i // 4, (i // 2) % 2, i % 2
        ref = att_ref.at[pl.ds((2 * from_x + from_core) * SHARE, SHARE), pl.ds(from_y * CAP, CAP)]
        copy = push(o_ref.at[i], ref, out_send.at[i], out_recv.at[i], sibling)
        copy.wait_recv()
        pl.when(band != i)(copy.wait_send)
    for copy in copies.values():
        copy.wait_send()
    keep_turned.wait()


BLOCK = 512
BLOCKS = 6
QLANES = 640
D_AXES = ('xyab', 'xyab', 'aybx', 'xaby', 'yxab', 'yxba', 'xyab', 'yxab')
U_AXES = ('yxba', 'xbay', 'yabx', 'axby', 'axyb', 'xayb')
Q_AXES = ('aby-bxa', 'yab-axy', 'ayb-yax')
TOGETHER = 0
EVENTS = ('b7', 'd7', 'b6', 'd6', 'b5', 'd5', 'b4', 'd4', 'b3', 'd3', 'b2', 'd2', 'b1', 'd1', 'b0', 'd0', 'q0', 'q1', 'q2')
SCHEDULE = {'m0': (0, 8), 'm1': (1, 9, 0), 'a1': (8,), 'm2': (2, 10, 1, 9), 'm3': (3, 11, 2, 10), 'm4': (4, 12, 3, 11, 0), 'a4': (8,), 'g5': (4,), 'm5': (5, 13, 12), 'a5': (1,), 'e': (5, 13, 2, 9, 10, 0), 'o': (6,), 's': (7, 11, 3, 4, 6, 8, 7, 12, 1, 10, 9, 0, 3), 'b71': (1, 8), 'b72': (5, 13, 9, 10, 0), 'd7': (11,), 'b60': (2, 3, 4), 'b62': (7, 1, 8, 9), 'd6': (6, 13), 'b50': (0, 12), 'b51': (11, 3), 'b52': (5, 2, 4, 10, 1), 'b40': (8, 9), 'b42': (6, 7, 13), 'b30': (3,), 'b31': (2, 0), 'b32': (5, 12, 11), 'b20': (4,), 'b21': (6, 1, 8), 'b22': (7, 10), 'd1': (3,), 'd0': (9,), 'q0': (14, 5, 13, 0), 'q1': (15, 2, 4), 'q2': (16, 8, 12, 0), 'end': (1, 10, 11, 8, 1, 6, 14, 13, 7, 5, 3, 16, 15, 6, 3, 2, 12, 14, 13, 7, 9, 10, 15, 9, 4, 16, 10, 11, 6, 2, 5, 14, 2, 12, 15, 4, 13, 4, 11, 16, 13, 7, 11, 5, 5, 14, 6, 12, 16, 6, 15, 12, 7, 14, 7, 16, 15, 14, 14, 16, 15, 16, 15)}


def partners():
    band, y, x, core = place()
    z = lax.axis_index("batch")
    return {
        "core": (core, device(y, x, 1 - core)),
        "x": (x, device(y, 1 - x, core)),
        "y": (y, device(1 - y, x, core)),
        "a": (z % 2, (band, z + 1 - 2 * (z % 2))),
        "b": (z // 2, (band, (z + 2) % 4)),
    }


class Chain:
    def __init__(self, send, recv, free, store):
        self.send, self.recv, self.free, self.finish = send, recv, free, store
        self.links = partners()
        self.steps = []
        self.at = 0

    def halve(self, piece, rows, axes, landing):
        start, spans = 0, {}
        first = len(self.steps)
        for level, axis in enumerate(axes[:-1]):
            rows //= 2
            bit = self.links[axis][0]
            keep, give = (start + bit * rows, rows), (start + (1 - bit) * rows, rows)
            self.steps.append(
                (axis, piece(give), landing[level], landing[level], piece(keep), first + level, None)
            )
            start = keep[0]
            spans[axis] = (keep, give, first + level)
        mine = piece((start, rows))
        self.steps.append((axes[-1], mine, landing[-1], landing[-1], mine, None, None))
        return spans

    def copy(self, number, arrival=False):
        axis, src, dst, got = self.steps[number][:4]
        if arrival:
            src = dst = got
        return push(src, dst, self.send.at[number], self.recv.at[number], self.links[axis][1])

    def add(self, target, source):
        rows, lanes = source.shape
        size = 32 if lanes < 512 and rows % 32 == 0 else 16

        def some(r, carry):
            at = pl.ds(pl.multiple_of(r * size, size), size)
            target[at, :] = (target[at, :].astype(F32) + source[at, :].astype(F32)).astype(BF)
            return carry

        lax.fori_loop(0, rows // size, some, 0)

    def advance(self):
        number, self.at = self.at, self.at + 1
        if number > 0:
            axis, _, _, got, add, frees, _ = self.steps[number - 1]
            self.copy(number - 1, True).wait_recv()
            if add is not None:
                self.copy(number - 1).wait_send()
                if frees is not None:
                    pl.semaphore_signal(
                        self.free.at[frees], inc=1, device_id=self.links[axis][1], device_id_type=MESH
                    )
                self.add(add, got)
        if number < len(self.steps):
            freed = self.steps[number][6]
            if freed is not None:
                pl.semaphore_wait(self.free.at[freed], 1)
            self.copy(number).start()
        else:
            self.finish.start()

    def drain(self):
        for number, step in enumerate(self.steps):
            if step[4] is None:
                self.copy(number).wait_send()
        self.finish.wait()


def weight_chain(total, landing, send, recv, free, index, axes, out, out_sem):
    core = lax.axis_index("band") % 2
    chain = Chain(
        send.at[index], recv.at[index], free.at[index],
        pltpu.make_async_copy(total.at[index], out.at[index], out_sem.at[index]),
    )
    mine, other, first = total.at[index, core], total.at[index, 1 - core], landing[0].at[index]
    chain.steps.append(("core", other, first, first, mine, 0, None))

    def piece(span):
        return total.at[index, core, pl.ds(pl.multiple_of(span[0], 16), span[1])]

    spans = chain.halve(piece, total.shape[2], axes, [spot.at[index] for spot in landing[1:]])
    for axis in axes[-2::-1]:
        keep, give, level = spans[axis]
        chain.steps.append((axis, piece(keep), piece(keep), piece(give), None, None, level))
    chain.steps.append(("core", mine, mine, other, None, None, 0))
    return chain


def head_chain(total, landing, send, recv, free, index, axes, out, out_sem):
    _, _, x, core = place()
    chain = Chain(
        send.at[index], recv.at[index], free.at[index],
        pltpu.make_async_copy(total.at[:, :, index], out.at[:, :, index], out_sem.at[index]),
    )

    def piece(span, which="own"):
        rows = pl.ds(pl.multiple_of(span[0], 16), span[1])
        if which == "both":
            return total.at[:, core, index, rows]
        return total.at[x if which == "own" else 1 - x, core, index, rows]

    axes, tail = axes.split("-")
    spans = chain.halve(piece, total.shape[3], axes, [spot.at[index] for spot in landing])
    held, which = spans[axes[-2]][0], "own"
    for axis in tail:
        if axis == "x":
            mine = piece(held)
            chain.steps.append(("x", mine, mine, piece(held, "other"), None, None, None))
            which = "both"
            continue
        keep, give, level = spans[axis]
        chain.steps.append((axis, piece(keep, which), piece(keep, which), piece(give, which), None, None, level))
        outer = axes.index(axis) - 1
        held = spans[axes[outer]][0] if outer >= 0 else (0, total.shape[3])
    both = total.at[:, core, index]
    chain.steps.append(("core", both, both, total.at[:, 1 - core, index], None, None, None))
    return chain


def layer_kernel(
    edges_ref, exit_ref, gain1_ref, shift1_ref, bq_ref, bv_ref, bo_ref, g2_ref, b2_ref, bd_ref, ub_ref,
    h_ref, cot_hbm, wout_hbm, wq_hbm, wk_hbm, wv_hbm, wup_hbm, wdown_hbm,
    dn_hbm, layer_hbm, dmid_hbm, fq_hbm, fd_hbm, fu_hbm, n1t_hbm,
    gd_ref, gu_ref, fq_ref, d0, d1, d2, d3, d4, u0, u1, u2, u3, u4, q1, q2, q3,
    layer_ref, dmid_ref, q_ref, kv_ref, kt_ref, dz_ref, da_ref, do_ref, sib_out, sib_in, row_out,
    o_ref, lse_ref, att_ref, wback_ref, cot_ref, wout_ref, dn_ref,
    d_send, d_recv, d_free, d_out, u_send, u_recv, u_free, u_out, q_send, q_recv, q_free, q_out,
    do_send, do_recv, sib_send, sib_recv, dn_send, dn_recv, out_send, out_recv, load, wload, out_sem,
    a_send, a_recv, a_load,
):
    band, y, x, core = place()
    batch = lax.axis_index("batch")
    links = partners()
    sibling = links["core"][1]
    width = h_ref.shape[1]
    early = [
        pltpu.make_async_copy(cot_hbm, cot_ref, load.at[1]),
        pltpu.make_async_copy(wout_hbm, wout_ref, load.at[2]),
    ]
    for copy in early:
        copy.start()
    pl.run_scoped(
        functools.partial(
            attend, edges_ref, gain1_ref, shift1_ref, bq_ref, bv_ref, h_ref, wq_hbm, wk_hbm, wv_hbm,
            o_ref, lse_ref, att_ref, wback_ref, n1t_hbm, q_ref, kv_ref, kt_ref,
            lambda which: gd_ref.at[which // 2, which % 2],
            a_send, a_recv, out_send, out_recv, a_load, load.at[0],
        ),
        VM((width, BANDS * CAP), BF),
        VM((3, width, 256), BF),
        VM((3, 256, width), BF),
        VM((MINE, BANDS, 1, CAP), F32),
        VM((MINE, BANDS, 1, CAP), F32),
        VM((MINE, BANDS, HEAD, CAP), F32),
    )

    chains = [
        weight_chain(gd_ref, (d0, d1, d2, d3, d4), d_send, d_recv, d_free, k, D_AXES[k], fd_hbm, d_out)
        for k in range(BLOCKS + 2)
    ] + [
        weight_chain(gu_ref, (u0, u1, u2, u3, u4), u_send, u_recv, u_free, k, U_AXES[k], fu_hbm, u_out)
        for k in range(BLOCKS)
    ] + [
        head_chain(fq_ref, (q1, q2, q3), q_send, q_recv, q_free, k, Q_AXES[k], fq_hbm, q_out) for k in range(3)
    ]
    layer_out = pltpu.make_async_copy(layer_ref, layer_hbm, out_sem.at[0])
    dmid_out = pltpu.make_async_copy(dmid_ref, dmid_hbm, out_sem.at[1])

    def serve(point):
        for k in SCHEDULE.get(point, ()):
            chains[k].advance()

    lane = lax.broadcasted_iota(jnp.int32, (1, 2 * CAP), 1)
    limit = jnp.where(lane < CAP, counts_of(edges_ref, 0, band), counts_of(edges_ref, 1, band) + CAP)
    active_row = jnp.where((exit_ref[...] >= LAYER) & (lane < limit), 1.0, 0.0)
    active = jnp.broadcast_to(active_row, (8, 2 * CAP)).T[:, :1]

    def feed_forward(mid_ref, sum_ref, dn2_ref, n2_ref, n2t_ref, wu, wd, pre_ref, dact_ref, act_ref, dpre_ref, part_ref, row_ref):
        def weights(f):
            at = pl.ds(f * BLOCK, BLOCK)
            return (
                pltpu.make_async_copy(wup_hbm.at[:, at], wu.at[f % 2], wload.at[0, f % 2]),
                pltpu.make_async_copy(wdown_hbm.at[at], wd.at[f % 2], wload.at[1, f % 2]),
            )

        for copy in weights(0):
            copy.start()
        for copy in early:
            copy.wait()
        branch = dot(att_ref[...], wout_ref[...], TN) + as_row(bo_ref)
        middle = h_ref[...].astype(F32) + active * branch
        mid_ref[...] = middle
        center = middle - jnp.mean(middle, axis=-1, keepdims=True)
        spread = jnp.mean(center * center, axis=-1, keepdims=True)
        scale2 = lax.rsqrt(spread + 1e-05)
        n2 = (center * scale2 * as_row(g2_ref) + as_row(b2_ref)).astype(BF)
        n2_ref[...] = n2
        n2t_ref[...] = n2.T
        dz_ref[...] = (active * cot_ref[...].astype(F32)).astype(BF)
        up_row = as_row(ub_ref)
        row_ref[...] = jnp.zeros_like(row_ref)
        sum_ref[...] = jnp.zeros_like(sum_ref)
        dn2_ref[...] = jnp.zeros_like(dn2_ref)
        for f in range(BLOCKS):
            if f + 1 < BLOCKS:
                for copy in weights(f + 1):
                    copy.start()
            for copy in weights(f):
                copy.wait()
            slot = f % 2
            pre_ref[...] = dot(n2_ref[...], wu[slot], NN)
            dact_ref[...] = dot(dz_ref[...], wd[slot], NT)
            serve(f'p{f}')
            up_bias = up_row[:, f * BLOCK : (f + 1) * BLOCK]
            part_ref[...] = jnp.zeros_like(part_ref)

            def rows(r, carry):
                at = pl.ds(pl.multiple_of(r * 64, 64), 64)
                pre = pre_ref[at, :] + up_bias
                square = pre * pre
                t = jnp.tanh(0.7978845608028654 * pre * (1.0 + 0.044715 * square))
                half = 0.5 * (1.0 + t)
                slope = half + (0.5 * 0.7978845608028654) * pre * (1.0 - t * t) * (1.0 + 0.134145 * square)
                act_ref[at, :] = (pre * half).astype(BF)
                dpre = (dact_ref[at, :] * slope).astype(BF)
                dpre_ref[at, :] = dpre
                part_ref[...] += jnp.sum(dpre.astype(F32).reshape(8, 8, BLOCK), axis=0)
                return carry

            lax.fori_loop(0, 2 * CAP // 64, rows, 0)
            serve(f'g{f}')
            down = dot(act_ref[...], dz_ref[...], TN).astype(BF)
            gd_ref[f, 0] = down[: BLOCK // 2]
            gd_ref[f, 1] = down[BLOCK // 2 :]
            up = dot(n2t_ref[...], dpre_ref[...], NN).astype(BF)
            gu_ref[f, 0] = up[:, : BLOCK // 2]
            gu_ref[f, 1] = up[:, BLOCK // 2 :]
            row_ref[f : f + 1, :BLOCK] = jnp.sum(part_ref[...], axis=0, keepdims=True)
            serve(f'm{f}')
            sum_ref[...] += dot(act_ref[...], wd[slot], NN)
            dn2_ref[...] += dot(dpre_ref[...], wu[slot], NT)
            serve(f'a{f}')
        middle = mid_ref[...]
        center = middle - jnp.mean(middle, axis=-1, keepdims=True)
        spread = jnp.mean(center * center, axis=-1, keepdims=True)
        scale2 = lax.rsqrt(spread + 1e-05)
        xhat = center * scale2
        dn2 = dn2_ref[...]
        e2 = dn2 * as_row(g2_ref)
        dmid = cot_ref[...].astype(F32) + scale2 * (
            e2 - jnp.mean(e2, axis=-1, keepdims=True) - xhat * jnp.mean(e2 * xhat, axis=-1, keepdims=True)
        )
        dmid_ref[...] = dmid
        da = (active * dmid).astype(BF)
        n2_ref[...] = da
        da_ref[...] = dot(wout_ref[...], da, NT).astype(BF)
        for i in range(BANDS):
            copy = push(part_for(i), do_ref.at[band], do_send.at[i], do_recv.at[band], (i, batch))
            pl.when(band != i)(copy.start)
            local = pltpu.make_async_copy(part_for(i), do_ref.at[band], do_recv.at[band])
            pl.when(band == i)(local.start)
        dmid_out.start()
        row_ref[10:11, :] = jnp.sum(dn2 * xhat, axis=0, keepdims=True)
        serve('e')
        out = dot(att_ref[...], n2_ref[...], NN).astype(BF)
        gd_ref[BLOCKS, 0] = out[:256]
        gd_ref[BLOCKS, 1] = out[256:512]
        gd_ref[BLOCKS + 1, 0] = out[512:]
        serve('o')
        layer_ref[...] = (mid_ref[...] + active * (sum_ref[...] + as_row(bd_ref))).astype(BF)
        layer_out.start()
        count = jnp.sum(active_row)
        big = jnp.floor(count * (1.0 / 64.0))
        mid = jnp.floor((count - 64.0 * big) * 0.125)
        small = count - 64.0 * big - 8.0 * mid
        at = lax.broadcasted_iota(jnp.int32, (1, width), 1)
        digits = jnp.where(at == 0, big, jnp.where(at == 1, mid, jnp.where(at == 2, small, 0.0)))
        row_ref[8:9, :] = jnp.sum(dz_ref[...].astype(F32), axis=0, keepdims=True)
        row_ref[9:10, :] = jnp.sum(n2_ref[...].astype(F32), axis=0, keepdims=True)
        row_ref[11:12, :] = jnp.sum(dn2_ref[...], axis=0, keepdims=True)
        row_ref[12:13, :] = digits
        gd_ref[BLOCKS + 1, 1, :16, :] = row_ref[...].astype(BF)
        serve('s')

    def part_for(i):
        to_y, to_x, to_core = i // 4, (i // 2) % 2, i % 2
        return da_ref.at[pl.ds((2 * to_x + to_core) * SHARE, SHARE), pl.ds(to_y * CAP, CAP)]

    gd_ref[BLOCKS + 1, 1] = jnp.zeros(gd_ref.shape[2:], BF)
    rows2 = 2 * CAP
    pl.run_scoped(
        feed_forward,
        VM((rows2, width), F32), VM((rows2, width), F32), VM((rows2, width), F32),
        VM((rows2, width), BF), VM((width, rows2), BF),
        VM((2, width, BLOCK), BF), VM((2, BLOCK, width), BF),
        VM((rows2, BLOCK), F32), VM((rows2, BLOCK), F32), VM((rows2, BLOCK), BF), VM((rows2, BLOCK), BF),
        VM((8, BLOCK), F32), VM((16, width), F32),
    )
    half = pl.ds(pl.multiple_of(core * HALF, HALF), HALF)
    key_at = lax.broadcasted_iota(jnp.int32, (CAP, CAP), 0)
    query_at = lax.broadcasted_iota(jnp.int32, (CAP, CAP), 1)

    def sib_copy(i):
        return push(sib_out.at[i % 2], sib_in.at[i], sib_send.at[i], sib_recv.at[i], sibling)

    def dn_copy(i):
        return push(row_out.at[i % 2], dn_ref.at[y, x, half], dn_send.at[i], dn_recv.at[band], (i, batch))

    def dn_local(i):
        return pltpu.make_async_copy(row_out.at[i % 2], dn_ref.at[y, x, half], dn_recv.at[band])

    def backward(dk_ref, d_ref, mine_ref, n1t_ref, small_ref):
        turned_load = pltpu.make_async_copy(n1t_hbm, n1t_ref, load.at[3])
        turned_load.start()

        def finish(i):
            sib_copy(i).wait_recv()
            if i + 2 < BANDS:
                pl.when(band != i + 2)(dn_copy(i + 2).wait_send)

                @pl.when(band == i + 2)
                def _():
                    push(row_out.at[0], dn_ref.at[y, x, half], dn_send.at[0], dn_recv.at[band], sibling).wait_recv()

            row_out[i % 2] = (mine_ref[i % 2] + sib_in[i].astype(F32)).astype(BF)
            pl.when(band != i)(dn_copy(i).start)
            pl.when(band == i)(dn_local(i).start)

        def row_back(i, heads):
            cols = pl.ds(i * CAP, CAP)
            limit = counts_of(edges_ref, y, i)
            qts = [q_ref[h, i] for h in heads]
            douts = [do_ref[i, h * HEAD : (h + 1) * HEAD, :] for h in heads]
            pads = [jnp.concatenate([jnp.zeros_like(d), d], axis=0) for d in douts]
            deltas = [
                jnp.sum(d.astype(F32) * o_ref[i, h * HEAD : (h + 1) * HEAD, :].astype(F32), axis=0, keepdims=True)
                for h, d in zip(heads, douts)
            ]
            dqs = [jnp.zeros((HEAD, CAP), F32) for _ in heads]
            for j in range(i + 1):
                keep = key_at < counts_of(edges_ref, y, j)
                if i == j:
                    keep = keep & (key_at <= query_at)
                    alone = (key_at == query_at) & (query_at >= limit)
                for n, h in enumerate(heads):
                    kv = kv_ref[h, j]
                    s = dot(kv, qts[n], NN)
                    dp = dot(kv, pads[n], NN)
                    p = jnp.where(keep, jnp.exp(s - lse_ref[h, i]), 0.0)
                    if i == j:
                        p = jnp.where(alone, 1.0, p)
                    ds = (p * (dp - deltas[n])).astype(BF)
                    dqs[n] = dqs[n] + dot(kt_ref[h, j, :HEAD], ds, NN)
                    more = dot(ds, qts[n], NT) + dot(p.astype(BF), pads[n], NT)
                    if i == BANDS - 1:
                        dk_ref[h, j] = more
                    else:
                        dk_ref[h, j] += more
            for n, h in enumerate(heads):
                d_ref[h * HEAD : (h + 1) * HEAD, cols] = (dqs[n] * 0.125).astype(BF)
                pair = dk_ref[h, i].T.astype(BF)
                d_ref[SHARE + h * HEAD : SHARE + (h + 1) * HEAD, cols] = pair[:HEAD]
                d_ref[2 * SHARE + h * HEAD : 2 * SHARE + (h + 1) * HEAD, cols] = pair[HEAD:]

        def row_return(i):
            dn = dot(d_ref[:, i * CAP : (i + 1) * CAP], wback_ref[...], TN)
            mine_ref[2] = dn[:HALF]
            mine_ref[3] = dn[HALF:]
            if i + 2 < BANDS:
                sib_copy(i + 2).wait_send()
            sib_out[i % 2] = mine_ref[2 + (1 - core)].astype(BF)
            mine_ref[i % 2] = mine_ref[2 + core]
            sib_copy(i).start()
            if i < BANDS - 1:
                finish(i + 1)
            serve(f'd{i}')

        def heads_out(k):
            if k == 0:
                turned_load.wait()
                ones = jnp.ones((8, d_ref.shape[1]), BF)
                total = dot(ones, d_ref[...], NT)
                small_ref[:, : 3 * SHARE] = total
                small_ref[:, 3 * SHARE :] = jnp.zeros((8, width - 3 * SHARE), F32)
            rows = slice(k * 256, (k + 1) * 256)
            dw = dot(n1t_ref[rows, :], d_ref[...], NT)
            sums = small_ref[:1, : 3 * SHARE]
            column = small_ref[:, rows].T[:, :1]
            weight = wback_ref[:, rows].T.astype(F32)
            shift = jnp.sum(weight * sums, axis=1, keepdims=True)
            shift1 = jnp.broadcast_to(as_row(shift1_ref)[:, rows], (8, 256)).T[:, :1]
            gain = jnp.sum(weight * dw, axis=1, keepdims=True) - shift1 * shift
            fq_ref[x, core, k, :, : 3 * SHARE] = dw.astype(BF)
            at = lax.broadcasted_iota(jnp.int32, (256, QLANES - 3 * SHARE), 1)
            tail = jnp.where(at == 0, shift, jnp.where(at == 1, gain, jnp.where(at == 2, column, 0.0)))
            fq_ref[x, core, k, :, 3 * SHARE :] = tail.astype(BF)
            serve(f'q{k}')

        for event in EVENTS:
            kind, i = event[0], int(event[1])
            if kind == "b":
                push(do_ref.at[i], do_ref.at[i], do_send.at[i], do_recv.at[i], sibling).wait_recv()
                if i >= TOGETHER:
                    for h in range(MINE):
                        row_back(i, (h,))
                        serve(f'b{i}{h}')
                else:
                    row_back(i, tuple(range(MINE)))
                    serve(f'b{i}2')
            elif kind == "d":
                row_return(i)
            else:
                heads_out(i)
        finish(0)

    pl.run_scoped(
        backward,
        VM((MINE, BANDS, CAP, 128), F32),
        VM((3 * SHARE, BANDS * CAP), BF),
        VM((4, HALF, width), F32),
        VM((width, BANDS * CAP), BF),
        VM((8, width), F32),
    )
    last = SCHEDULE.get('end', ())
    for k in last[:-10]:
        chains[k].advance()
    for i in range(BANDS):
        from_y, from_x, from_core = i // 4, i // 2 % 2, i % 2
        arrived = push(row_out.at[0], dn_ref.at[from_y, from_x, pl.ds(from_core * HALF, HALF)],
                       dn_send.at[i], dn_recv.at[i], sibling)
        if i < 2:
            arrived.wait_recv()
        else:
            pl.when(band != i)(arrived.wait_recv)
    dn_out = pltpu.make_async_copy(dn_ref, dn_hbm, out_sem.at[2])
    dn_out.start()
    for k in last[-10:]:
        chains[k].advance()
    left = [[k] * (len(chain.steps) + 1 - chain.at) for k, chain in enumerate(chains)]
    while any(left):
        for k, rest in enumerate(left):
            if rest:
                chains[rest.pop()].advance()

    for i in range(BANDS):
        copy = push(part_for(i), do_ref.at[i], do_send.at[i], do_recv.at[i], sibling)
        pl.when(band != i)(copy.wait_send)
        if i < 2:
            sib_copy(i).wait_send()
            pl.when(band != i)(dn_copy(i).wait_send)
    for chain in chains:
        chain.drain()
    layer_out.wait()
    dmid_out.wait()
    dn_out.wait()


def layer_call(edges, exits, vecs, h, cot, wout, wq, wk, wv, wup, wdown):
    width = h.shape[1]
    seq = BANDS * CAP
    vm = pl.BlockSpec(memory_space=VM)
    hbm = pl.BlockSpec(memory_space=pl.ANY)
    dma, credit = pltpu.SemaphoreType.DMA, pltpu.SemaphoreType.REGULAR
    eight = dma((BANDS,))

    def room(*shape):
        return VM(shape, BF)

    def spots(number, rows, lanes, levels):
        return [room(number, rows // 2**k, lanes) for k in levels]

    def sems(number, steps, levels):
        return [dma((number, steps)), dma((number, steps)), credit((number, levels)), dma((number,))]

    parts_d, parts_u = BLOCKS + 2, BLOCKS
    return pl.pallas_call(
        layer_kernel,
        name="layer",
        out_shape=[
            jax.ShapeDtypeStruct((2, 2, CAP, width), BF),
            jax.ShapeDtypeStruct(h.shape, BF),
            jax.ShapeDtypeStruct(h.shape, F32),
            jax.ShapeDtypeStruct((2, 2, 3, 256, QLANES), BF),
            jax.ShapeDtypeStruct((parts_d, 2, 256, width), BF),
            jax.ShapeDtypeStruct((parts_u, 2, width, 256), BF),
            jax.ShapeDtypeStruct((width, seq), BF),
        ],
        in_specs=[pl.BlockSpec(memory_space=pltpu.SMEM)] + [vm] * 11 + [hbm] * 7,
        out_specs=[hbm] * 7,
        scratch_shapes=[room(parts_d, 2, 256, width), room(parts_u, 2, width, 256), room(2, 2, 3, 256, QLANES)]
        + spots(parts_d, 256, width, (0, 1, 2, 3, 3))
        + spots(parts_u, width, 256, (0, 1, 2, 3, 3))
        + spots(3, 256, QLANES, (1, 2, 2))
        + [
            room(*h.shape), VM(h.shape, F32),
            room(MINE, BANDS, 128, CAP), room(MINE, BANDS, CAP, 128), room(MINE, BANDS, 128, CAP),
            room(2 * CAP, width), room(width, 2 * CAP), room(BANDS, SHARE, CAP),
            room(2, HALF, width), room(BANDS, HALF, width), room(2, HALF, width),
            room(BANDS, SHARE, CAP), VM((MINE, BANDS, 1, CAP), F32), room(width, 2 * CAP), room(3 * SHARE, width),
            room(*h.shape), room(width, width), room(2, 2, CAP, width),
        ]
        + sems(parts_d, 9, 5) + sems(parts_u, 9, 5) + sems(3, 7, 3)
        + [eight] * 8 + [dma((6,)), dma((2, 2)), dma((3,)), dma((13,)), dma((13,)), dma((3,))],
        compiler_params=pltpu.CompilerParams(
            collective_id=1, has_side_effects=True, vmem_limit_bytes=63 * 2**20
        ),
    )(edges, exits, *vecs, h, cot, wout, wq, wk, wv, wup, wdown)


SLOTS = 6


def finish_kernel(
    gain_ref, h_ref, dmid_ref, dn_ref, layer_ref, fd_hbm, fu_hbm, fq_hbm,
    out_ref, grad_ref, g1_ref, b1_ref, qb_ref, vb_ref, ob_ref, g2_ref, b2_ref, ub_ref, db_ref,
    qw_hbm, kw_hbm, vw_hbm, ow_hbm, uw_hbm, dw_hbm,
    in_d, in_u, in_q, out_d, out_u, square, load_d, load_u, load_q, store_d, store_u, store_q,
):
    width = h_ref.shape[1]
    out_ref[...] = layer_ref[...]
    tail = (BLOCKS + 1, 1)
    halves_d = [tail] + [(f, c) for f in range(BLOCKS + 2) for c in range(2) if (f, c) != tail]
    halves_u = [(f, c) for f in range(BLOCKS) for c in range(2)]

    def load_of(kind, f, c):
        src, dst, sem = ((fd_hbm, in_d, load_d), (fu_hbm, in_u, load_u))[kind]
        return pltpu.make_async_copy(src.at[f, c], dst.at[f, c], sem.at[f, c])

    def q_load(g, k):
        return pltpu.make_async_copy(
            fq_hbm.at[g // 2, g % 2, k], in_q.at[g // 2, g % 2, k], load_q.at[g, k]
        )

    for k in range(max(len(halves_d), len(halves_u))):
        if k < len(halves_d):
            load_of(0, *halves_d[k]).start()
        if k < len(halves_u):
            load_of(1, *halves_u[k]).start()
    for k in range(3):
        for g in range(4):
            q_load(g, k).start()

    load_of(0, *tail).wait()
    rest = in_d[tail[0], tail[1], :16, :].astype(F32)
    count = rest[12:13, :3]
    total = 64.0 * count[:, 0:1] + 8.0 * count[:, 1:2] + count[:, 2:3]
    scale = 1.0 / total

    def store_of(kind, k):
        if kind == 0:
            f, c = halves_d[1:][k]
            row = f * BLOCK + c * 256
            target = dw_hbm.at[pl.ds(row, 256)] if f < BLOCKS else ow_hbm.at[pl.ds(row - BLOCKS * BLOCK, 256)]
            return pltpu.make_async_copy(out_d.at[k % SLOTS], target, store_d.at[k % SLOTS])
        f, c = halves_u[k]
        target = uw_hbm.at[:, pl.ds(f * BLOCK + c * 256, 256)]
        return pltpu.make_async_copy(out_u.at[k % SLOTS], target, store_u.at[k % SLOTS])

    def convert(kind, k):
        f, c = halves_u[k] if kind else halves_d[1:][k]
        source, out = ((in_d, out_d), (in_u, out_u))[kind]
        load_of(kind, f, c).wait()
        if k >= SLOTS:
            store_of(kind, k - SLOTS).wait()
        step = 64 if kind == 0 else 192

        def some(r, carry):
            at = pl.ds(pl.multiple_of(r * step, step), step)
            out[k % SLOTS, at, :] = source[f, c, at, :].astype(F32) * scale
            return carry

        lax.fori_loop(0, source.shape[2] // step, some, 0)
        store_of(kind, k).start()

    number_d, number_u = len(halves_d) - 1, len(halves_u)
    for k in range(max(number_d, number_u)):
        if k < number_d:
            convert(0, k)
        if k < number_u:
            convert(1, k)

    outs = (qw_hbm, kw_hbm, vw_hbm)

    def q_store(which, k):
        rows = pl.ds(k * 256, 256)
        return pltpu.make_async_copy(square.at[which, rows], outs[which].at[rows], store_q.at[which, k])

    for k in range(3):
        for g in range(4):
            q_load(g, k).wait()
        for which in range(3):
            square[which, k * 256 : (k + 1) * 256, :] = jnp.concatenate(
                [
                    in_q[g // 2, g % 2, k, :, which * SHARE : (which + 1) * SHARE].astype(F32) * scale
                    for g in range(4)
                ],
                axis=1,
            )
            q_store(which, k).start()

    hidden = h_ref[...].astype(F32)
    center = hidden - jnp.mean(hidden, axis=-1, keepdims=True)
    spread = jnp.mean(center * center, axis=-1, keepdims=True)
    scale1 = lax.rsqrt(spread + 1e-05)
    xhat = center * scale1
    dn1 = jnp.concatenate([dn_ref[s, 0].astype(F32) + dn_ref[s, 1].astype(F32) for s in range(2)], axis=0)
    gain = as_row(gain_ref)
    e1 = dn1 * gain
    grad_ref[...] = dmid_ref[...] + scale1 * (
        e1 - jnp.mean(e1, axis=-1, keepdims=True) - xhat * jnp.mean(e1 * xhat, axis=-1, keepdims=True)
    )

    gain1 = shift1 = jnp.zeros((1, width), F32)
    query_b, value_b = [], []
    for g in range(4):
        block = jnp.concatenate(
            [in_q[g // 2, g % 2, k, :, 3 * SHARE - HEAD :].T for k in range(3)], axis=1
        )[HEAD : HEAD + 16]
        shift1 = shift1 + block[0:1].astype(F32)
        gain1 = gain1 + block[1:2].astype(F32)
        query_b.append(block[2:3, :SHARE].astype(F32))
        value_b.append(block[2:3, 2 * SHARE : 3 * SHARE].astype(F32))
    query_b, value_b = jnp.concatenate(query_b, axis=1), jnp.concatenate(value_b, axis=1)
    for ref, value in (
        (g1_ref, gain1 / gain), (b1_ref, shift1), (qb_ref, query_b), (vb_ref, value_b),
        (ob_ref, rest[9:10]), (g2_ref, rest[10:11]), (b2_ref, rest[11:12]), (db_ref, rest[8:9]),
    ):
        ref[...] = (value * scale).reshape(width)
    ub_ref[...] = (jnp.concatenate([rest[f : f + 1, :BLOCK] for f in range(BLOCKS)], axis=1) * scale).reshape(
        BLOCKS * BLOCK
    )
    for k in range(3):
        for which in range(3):
            q_store(which, k).wait()
    for k in range(number_d - SLOTS, number_d):
        store_of(0, k).wait()
    for k in range(number_u - SLOTS, number_u):
        store_of(1, k).wait()


def finish_call(gain, h, dmid, dn, layer, fd, fu, fq):
    width = h.shape[1]
    vm = pl.BlockSpec(memory_space=VM)
    hbm = pl.BlockSpec(memory_space=pl.ANY)
    dma = pltpu.SemaphoreType.DMA
    hidden = BLOCKS * BLOCK
    flat = jax.ShapeDtypeStruct((width, width), F32)
    line = jax.ShapeDtypeStruct((width,), F32)
    return pl.pallas_call(
        finish_kernel,
        name="finish",
        out_shape=[jax.ShapeDtypeStruct(h.shape, BF), jax.ShapeDtypeStruct(h.shape, F32)]
        + [line] * 7
        + [jax.ShapeDtypeStruct((hidden,), F32), line]
        + [flat] * 4
        + [jax.ShapeDtypeStruct((width, hidden), F32), jax.ShapeDtypeStruct((hidden, width), F32)],
        in_specs=[vm] * 5 + [hbm] * 3,
        out_specs=[vm] * 11 + [hbm] * 6,
        scratch_shapes=[
            VM(fd.shape, BF), VM(fu.shape, BF), VM(fq.shape, BF),
            VM((SLOTS, 256, width), F32), VM((SLOTS, width, 256), F32), VM((3, width, width), F32),
            dma(fd.shape[:2]), dma(fu.shape[:2]), dma((4, 3)), dma((SLOTS,)), dma((SLOTS,)), dma((3, 3)),
        ],
        compiler_params=pltpu.CompilerParams(vmem_limit_bytes=56 * 2**20),
    )(gain, h, dmid, dn, layer, fd, fu, fq)


def norm_rows(values):
    center = values - jnp.mean(values, axis=-1, keepdims=True)
    spread = jnp.mean(center * center, axis=-1, keepdims=True)
    return center * lax.rsqrt(spread + 1e-05)


def norm_affine(values, gain_vec, shift_vec):
    return norm_rows(values) * gain_vec + shift_vec


def left_product(left_mat, right_mat):
    return lax.dot_general(
        left_mat, right_mat, (((0,), (0,)), ((), ())), preferred_element_type=jnp.float32
    )


def right_product(left_mat, weight):
    return lax.dot_general(
        left_mat, weight, (((1,), (1,)), ((), ())), preferred_element_type=jnp.float32
    )


def slot_tags(first_row, count_rows, layout):
    begins_flat, finishes_flat, slot_rows, band_cap, band_count = layout
    slot_index = first_row + jnp.arange(count_rows, dtype=jnp.int32)
    owner = slot_index // slot_rows
    within = slot_index - owner * slot_rows
    member = within // band_cap
    offset = within - member * band_cap
    flat_code = member * band_count + owner
    all_codes = jnp.arange(begins_flat.shape[0], dtype=jnp.int32)
    hit_table = flat_code[:, None] == all_codes[None, :]
    begins = jnp.sum(jnp.where(hit_table, begins_flat[None, :], 0), axis=1)
    finish = jnp.sum(jnp.where(hit_table, finishes_flat[None, :], 0), axis=1)
    position = begins + offset
    return (member, position, position < finish, slot_index)


def allowed_pairs(query_tags, key_tags):
    query_member, query_position, query_valid, query_slot = query_tags
    key_member, key_position, key_valid, key_slot = key_tags
    same_slot = query_slot[:, None] == key_slot[None, :]
    causal = (query_member[:, None] == key_member[None, :]) & (
        key_position[None, :] <= query_position[:, None]
    )
    return same_slot | query_valid[:, None] & key_valid[None, :] & causal


def on_device(
    residual_in,
    exit_layer,
    band_edges,
    norm1_gain,
    norm1_bias,
    query_weight,
    query_bias,
    key_weight,
    value_weight,
    value_bias,
    out_weight,
    out_bias,
    norm2_gain,
    norm2_bias,
    up_weight,
    up_bias,
    down_weight,
    down_bias,
    cotangent,
):
    slot_rows = residual_in.shape[1]
    model_width = residual_in.shape[2]
    head_size = model_width // HEADS
    score_scale = head_size ** (-0.5)
    band_here = lax.axis_index("band")
    band_count = lax.axis_size("band")
    band_cap = slot_rows // band_edges.shape[1]
    finishes = jnp.concatenate([band_edges[0][:, 1:], band_edges[0][:, -1:] + band_cap], axis=1)
    layout = (band_edges[0].reshape(-1), finishes.reshape(-1), slot_rows, band_cap, band_count)
    own_tags = slot_tags(band_here * slot_rows, slot_rows, layout)
    active = ((exit_layer[0] >= LAYER) & own_tags[2]).astype(jnp.float32)[:, None]
    total_active = lax.psum(jnp.sum(active), ("band", "batch"))
    hidden_in = residual_in[0].astype(jnp.float32)
    normed_one, norm_one_back = jax.vjp(
        norm_affine, hidden_in, norm1_gain.astype(jnp.float32), norm1_bias.astype(jnp.float32)
    )
    normed_low = normed_one.astype(jnp.bfloat16)
    queries = (
        jnp.dot(normed_low, query_weight, preferred_element_type=jnp.float32)
        + query_bias.astype(jnp.float32)
    ).astype(jnp.bfloat16)
    keys_own = jnp.dot(normed_low, key_weight, preferred_element_type=jnp.float32).astype(
        jnp.bfloat16
    )
    values_own = (
        jnp.dot(normed_low, value_weight, preferred_element_type=jnp.float32)
        + value_bias.astype(jnp.float32)
    ).astype(jnp.bfloat16)
    query_heads = queries.reshape(slot_rows, HEADS, head_size)
    start_state = (
        jnp.full((HEADS, slot_rows), -1e30, jnp.float32),
        jnp.zeros((HEADS, slot_rows), jnp.float32),
        jnp.zeros((slot_rows, HEADS, head_size), jnp.float32),
    )
    key_piece = lax.all_gather(keys_own, "band", axis=0, tiled=True)
    value_piece = lax.all_gather(values_own, "band", axis=0, tiled=True)
    piece_rows = key_piece.shape[0]
    step_rows = min(piece_rows, slot_rows)

    def one_step(step_index, inner_state):
        offset_row = step_index * step_rows
        key_block = lax.dynamic_slice_in_dim(key_piece, offset_row, step_rows, 0).reshape(
            step_rows, HEADS, head_size
        )
        value_block = lax.dynamic_slice_in_dim(value_piece, offset_row, step_rows, 0).reshape(
            step_rows, HEADS, head_size
        )
        mask = allowed_pairs(own_tags, slot_tags(offset_row, step_rows, layout))

        def accumulate(running):
            top_old, total_old, sum_old = running
            scores = (
                jnp.einsum(
                    "qhd,khd->hqk", query_heads, key_block, preferred_element_type=jnp.float32
                )
                * score_scale
            )
            scores = jnp.where(mask[None], scores, -1e30)
            top_new = jnp.maximum(top_old, jnp.max(scores, axis=-1))
            rescale = jnp.exp(top_old - top_new)
            weights_new = jnp.where(mask[None], jnp.exp(scores - top_new[..., None]), 0.0)
            total_new = total_old * rescale + jnp.sum(weights_new, axis=-1)
            sum_new = sum_old * rescale.T[..., None] + jnp.einsum(
                "hqk,khd->qhd",
                weights_new.astype(jnp.bfloat16),
                value_block,
                preferred_element_type=jnp.float32,
            )
            return (top_new, total_new, sum_new)

        return lax.cond(jnp.any(mask), accumulate, lambda running: running, inner_state)

    top_score, weight_total, weighted_sum = lax.fori_loop(
        0, piece_rows // step_rows, one_step, start_state
    )
    attended = weighted_sum / weight_total.T[..., None]
    log_total = top_score + jnp.log(weight_total)
    mixed_low = attended.reshape(slot_rows, model_width).astype(jnp.bfloat16)
    branch = jnp.dot(mixed_low, out_weight, preferred_element_type=jnp.float32) + out_bias.astype(
        jnp.float32
    )
    middle = hidden_in + active * branch
    normed_two, norm_two_back = jax.vjp(
        norm_affine, middle, norm2_gain.astype(jnp.float32), norm2_bias.astype(jnp.float32)
    )
    normed_two_low = normed_two.astype(jnp.bfloat16)
    pre_act = jnp.dot(
        normed_two_low, up_weight, preferred_element_type=jnp.float32
    ) + up_bias.astype(jnp.float32)
    activated, gelu_back = jax.vjp(jax.nn.gelu, pre_act)
    activated_low = activated.astype(jnp.bfloat16)
    down_out = jnp.dot(
        activated_low, down_weight, preferred_element_type=jnp.float32
    ) + down_bias.astype(jnp.float32)
    layer_out = (middle + active * down_out).astype(jnp.bfloat16)[None]
    out_grad = cotangent[0].astype(jnp.float32)
    down_grad = (active * out_grad).astype(jnp.bfloat16)
    down_weight_sum = left_product(activated_low, down_grad)
    down_bias_sum = jnp.sum(down_grad.astype(jnp.float32), axis=0)
    (pre_grad,) = gelu_back(right_product(down_grad, down_weight))
    pre_low = pre_grad.astype(jnp.bfloat16)
    up_weight_sum = left_product(normed_two_low, pre_low)
    up_bias_sum = jnp.sum(pre_low.astype(jnp.float32), axis=0)
    middle_norm, gain_two_sum, shift_two_sum = norm_two_back(right_product(pre_low, up_weight))
    middle_grad = out_grad + middle_norm
    branch_grad = (active * middle_grad).astype(jnp.bfloat16)
    out_weight_sum = left_product(mixed_low, branch_grad)
    out_bias_sum = jnp.sum(branch_grad.astype(jnp.float32), axis=0)
    mixed_grad = right_product(branch_grad, out_weight).astype(jnp.bfloat16)
    grad_heads = mixed_grad.reshape(slot_rows, HEADS, head_size)
    delta_row = jnp.sum(grad_heads.astype(jnp.float32) * attended, axis=-1).T

    def pair_terms(query_blk, grad_blk, logsum_blk, delta_blk, key_block, value_block, mask):
        scores = (
            jnp.einsum("qhd,khd->hqk", query_blk, key_block, preferred_element_type=jnp.float32)
            * score_scale
        )
        probability = jnp.where(mask[None], jnp.exp(scores - logsum_blk[..., None]), 0.0)
        prob_grad = jnp.einsum(
            "qhd,khd->hqk", grad_blk, value_block, preferred_element_type=jnp.float32
        )
        score_grad = (probability * (prob_grad - delta_blk[..., None])).astype(jnp.bfloat16)
        return (probability.astype(jnp.bfloat16), score_grad)

    all_rows = slot_rows * band_count
    start_back = (
        jnp.zeros((slot_rows, HEADS, head_size), jnp.float32),
        jnp.zeros((all_rows, model_width), jnp.float32),
        jnp.zeros((all_rows, model_width), jnp.float32),
    )
    fold_key_piece = lax.all_gather(keys_own, "band", axis=0, tiled=True)
    fold_value_piece = lax.all_gather(values_own, "band", axis=0, tiled=True)
    piece_rows = fold_key_piece.shape[0]
    fold_step_rows = min(piece_rows, slot_rows)

    def one_step(step_index, inner_state):
        offset_row = step_index * fold_step_rows
        key_block = lax.dynamic_slice_in_dim(fold_key_piece, offset_row, fold_step_rows, 0).reshape(
            fold_step_rows, HEADS, head_size
        )
        value_block = lax.dynamic_slice_in_dim(
            fold_value_piece, offset_row, fold_step_rows, 0
        ).reshape(fold_step_rows, HEADS, head_size)
        mask = allowed_pairs(own_tags, slot_tags(offset_row, fold_step_rows, layout))

        def accumulate(running):
            query_acc, key_sums, value_sums = running
            prob_low, score_grad = pair_terms(
                query_heads, grad_heads, log_total, delta_row, key_block, value_block, mask
            )
            query_acc = (
                query_acc
                + jnp.einsum(
                    "hqk,khd->qhd", score_grad, key_block, preferred_element_type=jnp.float32
                )
                * score_scale
            )
            key_term = (
                jnp.einsum(
                    "hqk,qhd->khd", score_grad, query_heads, preferred_element_type=jnp.float32
                ).reshape(fold_step_rows, model_width)
                * score_scale
            )
            value_term = jnp.einsum(
                "hqk,qhd->khd", prob_low, grad_heads, preferred_element_type=jnp.float32
            ).reshape(fold_step_rows, model_width)
            key_sums = lax.dynamic_update_slice_in_dim(
                key_sums,
                lax.dynamic_slice_in_dim(key_sums, offset_row, fold_step_rows, 0) + key_term,
                offset_row,
                0,
            )
            value_sums = lax.dynamic_update_slice_in_dim(
                value_sums,
                lax.dynamic_slice_in_dim(value_sums, offset_row, fold_step_rows, 0) + value_term,
                offset_row,
                0,
            )
            return (query_acc, key_sums, value_sums)

        return lax.cond(jnp.any(mask), accumulate, lambda running: running, inner_state)

    back_state = lax.fori_loop(0, piece_rows // fold_step_rows, one_step, start_back)
    query_sum, key_sums_all, value_sums_all = back_state
    key_sum, value_sum = (
        lax.psum_scatter(
            key_sums_all.astype(jnp.bfloat16), "band", scatter_dimension=0, tiled=True
        ).astype(jnp.float32),
        lax.psum_scatter(
            value_sums_all.astype(jnp.bfloat16), "band", scatter_dimension=0, tiled=True
        ).astype(jnp.float32),
    )
    query_low = query_sum.reshape(slot_rows, model_width).astype(jnp.bfloat16)
    key_low = key_sum.astype(jnp.bfloat16)
    value_low = value_sum.astype(jnp.bfloat16)
    query_weight_sum = left_product(normed_low, query_low)
    query_bias_sum = jnp.sum(query_low.astype(jnp.float32), axis=0)
    key_weight_sum = left_product(normed_low, key_low)
    value_weight_sum = left_product(normed_low, value_low)
    value_bias_sum = jnp.sum(value_low.astype(jnp.float32), axis=0)
    normed_grad = (
        right_product(query_low, query_weight)
        + right_product(key_low, key_weight)
        + right_product(value_low, value_weight)
    )
    input_norm, gain_one_sum, shift_one_sum = norm_one_back(normed_grad)
    input_grad = (middle_grad + input_norm)[None]
    (
        total_g1,
        total_b1,
        total_qw,
        total_qb,
        total_kw,
        total_vw,
        total_vb,
        total_ow,
        total_ob,
        total_g2,
        total_b2,
        total_uw,
        total_ub,
        total_dw,
        total_db,
    ) = lax.psum(
        (
            gain_one_sum,
            shift_one_sum,
            query_weight_sum,
            query_bias_sum,
            key_weight_sum,
            value_weight_sum,
            value_bias_sum,
            out_weight_sum,
            out_bias_sum,
            gain_two_sum,
            shift_two_sum,
            up_weight_sum,
            up_bias_sum,
            down_weight_sum,
            down_bias_sum,
        ),
        ("band", "batch"),
    )
    return (
        layer_out,
        input_grad,
        total_g1 / total_active,
        total_b1 / total_active,
        total_qw / total_active,
        total_qb / total_active,
        total_kw / total_active,
        total_vw / total_active,
        total_vb / total_active,
        total_ow / total_active,
        total_ob / total_active,
        total_g2 / total_active,
        total_b2 / total_active,
        total_uw / total_active,
        total_ub / total_active,
        total_dw / total_active,
        total_db / total_active,
    )


def fast_device(
    residual_in, exit_layer, band_edges, norm1_gain, norm1_bias, query_weight, query_bias,
    key_weight, value_weight, value_bias, out_weight, out_bias, norm2_gain, norm2_bias,
    up_weight, up_bias, down_weight, down_bias, cotangent,
):
    h, cot = residual_in[0], cotangent[0]
    vecs = (
        norm1_gain, norm1_bias, query_bias, value_bias, out_bias, norm2_gain, norm2_bias, down_bias, up_bias
    )
    dn, layer, dmid, fq, fd, fu, _ = layer_call(
        band_edges, exit_layer, vecs, h, cot, out_weight, query_weight, key_weight, value_weight,
        up_weight, down_weight,
    )
    layer, grad, g1, b1, qb, vb, ob, g2, b2, ub, db, qw, kw, vw, ow, uw, dw = finish_call(
        norm1_gain, h, dmid, dn, layer, fd, fu, fq
    )
    return (layer[None], grad[None], g1, b1, qw, qb, kw, vw, vb, ow, ob, g2, b2, uw, ub, dw, db)


def solution(mesh):
    placed = (
        (P("batch", "band", None), P("batch", "band"), P("batch", None, None))
        + (P(),) * 15
        + (P("batch", "band", None),)
    )
    fast = mesh.shape["band"] == BANDS and mesh.shape["batch"] == 4
    return jax.shard_map(
        fast_device if fast else on_device,
        mesh=mesh,
        in_specs=placed,
        out_specs=(P("batch", "band", None),) * 2 + (P(),) * 15,
        check_vma=False,
    )
```
